32 devices in a mesh: wide: 8 (over z, x), narrow: 4 (over y, core).
Axes of the slice: x: 2, y: 2, z: 4, core: 2. Of those that a mesh axis runs over, the one named last changes fastest.
Arguments:
- tokens: bfloat16 [4096, 960], P('wide'), may hold values from -6 to 6
- attn_in: bfloat16 [5, 960, 320], replicated, may hold values from -0.1875 to 0.1875
- attn_out: bfloat16 [5, 192, 960], replicated, may hold values from -0.5 to 0.5
- gate_weight: bfloat16 [960, 2560], P(None, 'narrow'), may hold values from -0.1875 to 0.1875
- up_weight: bfloat16 [960, 2560], P(None, 'narrow'), may hold values from -0.1875 to 0.1875
- down_weight: bfloat16 [2560, 960], P('narrow'), may hold values from -0.125 to 0.125
- attn_gain: float32 [960], replicated, may hold values from 0.5 to 1.5
- ffn_gain: float32 [960], replicated, may hold values from 0.5 to 1.5
- cotangent: bfloat16 [4096, 960], P('wide'), may hold values from -6 to 6
- seq_ids: int32 [4096], P('wide'), may hold values from 0 to 4, as said below
- positions: int32 [4096], P('wide'), may hold values from 0 to 2046, as said below
- valid_mask: int32 [4096], P('wide'), may hold values from 0 to 1, as said below
- group_owner: int32 [5], replicated, may hold values from 0 to 3, as said below
Outputs:
- layer_out: bfloat16 [4096, 960], P('wide')
- grad_tokens: bfloat16 [4096, 960], P('wide')
- grad_attn_in: float32 [8, 960, 320], P('narrow')
- grad_attn_out: float32 [8, 192, 960], P('narrow')
- grad_gate: float32 [960, 2560], P(None, 'narrow')
- grad_up: float32 [960, 2560], P(None, 'narrow')
- grad_down: float32 [2560, 960], P('narrow')
- grad_attn_gain: float32 [960], replicated
- grad_ffn_gain: float32 [960], replicated
The draws below stay inside these ranges and needn't reach their ends.
Inputs may be any that keep to these rules, and one draw needn't show every extreme that they name: `seq_ids`: on each wide member's 512 tokens the id never falls; tokens with equal id on one member form one sequence; id 4 marks padding at the end of a member's tokens, at most 64 of them; in every draw some member holds a single sequence of 512 tokens. Within a sequence the positions rise by one from token to token, from that sequence's own offset. `valid_mask`: padding tokens are 0; about one in ten of the other tokens is 0. `group_owner`: each of the 4 narrow members holds one or two groups; exactly one holds two.
All inputs are finite; a program needn't handle non-finite values.
Results may differ from the reference program's by a relative error of at most 0.019.
Values sent between devices are 32-bit elements; how exact they have to be, the bound alone decides.
No kernel may reach another device: no remote copies, remote signals or barrier semaphores. Data moves between devices by JAX's collectives and lax.ppermute only.
A program may use at most 128 MiB of HBM per device.

```python
import math
import jax
import jax.numpy as jnp
from jax import lax

D = 960
FF = 2560
GROUPS = 5
HEAD = 64
Q_PER = 3
QKV = 320
SLOTS = 2
LAYERS = 2
TOK_DEV = 512
TOKENS = 4096
N_NARROW = 4


def layout(key):
    members = TOKENS // TOK_DEV
    base_key = jax.random.fold_in(key, 11)
    key_pattern, key_full, key_pad = jax.random.split(base_key, 3)
    row_ids = jnp.arange(members, dtype=jnp.int32)
    pattern = jax.random.randint(key_pattern, (members,), 0, 4)
    full_row = jax.random.randint(key_full, (), 0, members)
    pattern = jnp.where(row_ids == full_row, 0, pattern)
    padding = jax.random.randint(key_pad, (members,), 1, TOK_DEV // 8 + 1)
    padding = jnp.where(row_ids == full_row, 0, padding)
    quarter = TOK_DEV // 4
    cut_table = jnp.array([[4, 4, 4], [2, 4, 4], [2, 3, 4], [1, 2, 3]], dtype=jnp.int32) * quarter
    cut_points = cut_table[pattern]
    place_ids = jnp.arange(TOK_DEV, dtype=jnp.int32)
    segment = jnp.sum((place_ids[None, :, None] >= cut_points[:, None, :]).astype(jnp.int32), axis=2)
    pad_start = (TOK_DEV - padding).astype(jnp.int32)
    padded = place_ids[None, :] >= pad_start[:, None]
    segment = jnp.where(padded, 4, segment).astype(jnp.int32)
    starts = jnp.concatenate([jnp.zeros((members, 1), jnp.int32), cut_points, pad_start[:, None]], axis=1)
    return (segment, padded, starts, full_row, row_ids, place_ids)


def draw_seq_ids(key, part):
    segment, padded, starts, full_row, row_ids, place_ids = layout(key)
    return segment.reshape(-1).astype(jnp.int32)


def draw_valid_mask(key, part):
    segment, padded, starts, full_row, row_ids, place_ids = layout(key)
    dropped = jax.random.randint(jax.random.fold_in(key, 23), segment.shape, 0, 10) == 0
    return jnp.where(padded | dropped, 0, 1).reshape(-1).astype(jnp.int32)


def draw_positions(key, part):
    segment, padded, starts, full_row, row_ids, place_ids = layout(key)
    members = segment.shape[0]
    offsets = jax.random.randint(jax.random.fold_in(key, 31), (members, 5), 0, 1536)
    first_col = jnp.arange(5)[None, :] == 0
    offsets = jnp.where((row_ids == full_row)[:, None] & first_col, 1535, offsets)
    other_row = (full_row + 1) % members
    offsets = jnp.where((row_ids == other_row)[:, None] & first_col, 0, offsets)
    seg_offset = jnp.take_along_axis(offsets, segment, axis=1)
    seg_start = jnp.take_along_axis(starts, segment, axis=1)
    return (seg_offset + place_ids[None, :] - seg_start).reshape(-1).astype(jnp.int32)


def draw_group_owner(key, part):
    base_key = jax.random.fold_in(key, 41)
    key_extra, key_shuffle = jax.random.split(base_key, 2)
    extra_owner = jax.random.randint(key_extra, (GROUPS - N_NARROW,), 0, N_NARROW)
    owners = jnp.concatenate([jnp.arange(N_NARROW, dtype=jnp.int32), extra_owner.astype(jnp.int32)])
    shuffle = jax.random.permutation(key_shuffle, GROUPS)
    return owners[shuffle].astype(jnp.int32)


def steps_of(stream_key, extent, cuts, least, high):
    level, own = 1.0, jax.random.fold_in(stream_key, 6)
    for position, parts in cuts:
        draws = jnp.exp(jax.random.uniform(jax.random.fold_in(own, position), (parts,), jnp.float32, least / len(cuts), high / len(cuts)))
        level = level * jnp.repeat(draws, extent[position] // parts).reshape([-1 if axis == position else 1 for axis in range(len(extent))])
    return level


def noise(key, dims, deviation, reach, shards=(), held_as=jnp.bfloat16):
    level = steps_of(key, dims, shards, -0.22, 0.18) if shards else 1.0
    drawn = jax.random.normal(key, dims, jnp.float32) * deviation * level
    return jnp.minimum(jnp.maximum(drawn, -reach), reach).astype(held_as)


def setup_inputs(seed: int = 0) -> dict:
    keys = jax.random.split(jax.random.key(seed), 14)
    tokens = noise(keys[0], (TOKENS, D), 1.0, 6.0, ((0, 8),))
    attn_in = noise(keys[1], (GROUPS, D, QKV), D ** -0.5, 0.1875)
    attn_out = noise(keys[2], (GROUPS, Q_PER * HEAD, D), (D // 8) ** -0.5, 0.5)
    gate_weight = noise(keys[3], (D, FF), D ** -0.5, 0.1875, ((1, 4),))
    up_weight = noise(keys[4], (D, FF), D ** -0.5, 0.1875, ((1, 4),))
    down_weight = noise(keys[5], (FF, D), FF ** -0.5, 0.125, ((0, 4),))
    attn_gain = jnp.clip(1.0 + 0.1 * jax.random.normal(keys[6], (D,), jnp.float32), 0.5, 1.5)
    ffn_gain = jnp.clip(1.0 + 0.1 * jax.random.normal(keys[7], (D,), jnp.float32), 0.5, 1.5)
    cotangent = noise(keys[8], (TOKENS, D), 1.0, 6.0, ((0, 8),))
    seq_ids = draw_seq_ids(jax.random.fold_in(keys[13], 71), 0)
    positions = draw_positions(jax.random.fold_in(keys[13], 71), 0)
    valid_mask = draw_valid_mask(jax.random.fold_in(keys[13], 71), 0)
    group_owner = draw_group_owner(jax.random.fold_in(keys[13], 71), 0)
    return dict(tokens=tokens, attn_in=attn_in, attn_out=attn_out, gate_weight=gate_weight, up_weight=up_weight, down_weight=down_weight, attn_gain=attn_gain, ffn_gain=ffn_gain, cotangent=cotangent, seq_ids=seq_ids, positions=positions, valid_mask=valid_mask, group_owner=group_owner)


EPS = 1e-05
THETA = 10000.0
HIGH = lax.Precision.HIGHEST

@jax.custom_vjp
def low(v):
    return lax.optimization_barrier(v.astype(jnp.bfloat16)).astype(jnp.float32)

@jax.custom_vjp
def low_back(v):
    return v

def low_keep(v):
    return (low(v), None)

def low_pass(kept, grad):
    return (grad,)

def back_keep(v):
    return (v, None)

def back_low(kept, grad):
    return (low(grad),)
low.defvjp(low_keep, low_pass)
low_back.defvjp(back_keep, back_low)

def rope_tables(positions, half_width):
    powers = -jnp.arange(half_width, dtype=jnp.float32) / half_width
    frequency = THETA ** powers
    angles = positions.astype(jnp.float32)[:, None] * frequency[None, :]
    return (jnp.cos(angles), jnp.sin(angles))

def rotate(vector, cosine, sine):
    half_width = vector.shape[-1] // 2
    first_half = vector[..., :half_width]
    second_half = vector[..., half_width:]
    return jnp.concatenate([first_half * cosine - second_half * sine, second_half * cosine + first_half * sine], axis=-1)

def rms_norm(stream, gain):
    return stream * lax.rsqrt(lax.optimization_barrier(jnp.mean(stream * stream, axis=-1, keepdims=True)) + EPS) * gain

def reference(tokens, attn_in, attn_out, gate_weight, up_weight, down_weight, attn_gain, ffn_gain, cotangent, seq_ids, positions, valid_mask, group_owner):
    members = TOKENS // TOK_DEV
    per_block = min(members, max(1, 4096 // TOK_DEV))
    span_rows = per_block * TOK_DEV
    block_count = members // per_block
    cosine, sine = rope_tables(positions, HEAD // 2)
    score_scale = 1.0 / math.sqrt(HEAD)
    query_width = Q_PER * HEAD

    def attend(member_parts):
        query_rot, key_rot, value_low, seq_block, valid_block = member_parts
        scores = low_back(jnp.einsum('qgjh,kgh->gjqk', query_rot, key_rot, precision=HIGH) * score_scale)
        place_ids = jnp.arange(TOK_DEV, dtype=jnp.int32)
        allowed = (seq_block[:, None] == seq_block[None, :]) & (place_ids[None, :] <= place_ids[:, None]) & (valid_block[None, :] == 1) | (place_ids[None, :] == place_ids[:, None])
        masked = jnp.where(allowed, scores, -jnp.inf)
        row_peak = lax.optimization_barrier(jnp.max(masked, axis=-1, keepdims=True))
        exponent = jnp.exp(masked - row_peak)
        attn_prob = low(exponent / lax.optimization_barrier(jnp.sum(exponent, axis=-1, keepdims=True)))
        return jnp.einsum('gjqk,kgh->qgjh', attn_prob, value_low, precision=HIGH)

    def two_layers(stream, seq_block, valid_block, cos_block, sin_block, weights):
        w_in, w_out, w_gate, w_up, w_down, gain_one, gain_two = weights
        row_count = stream.shape[0]
        for layer_index in range(LAYERS):
            normed_one = low(rms_norm(stream, gain_one))
            projected = low_back(jnp.einsum('td,gdc->tgc', normed_one, w_in, precision=HIGH))
            query_raw = projected[..., :query_width].reshape(row_count, GROUPS, Q_PER, HEAD)
            query_rot = low(rotate(query_raw, cos_block[:, None, None, :], sin_block[:, None, None, :]))
            key_rot = low(rotate(projected[..., query_width:query_width + HEAD], cos_block[:, None, :], sin_block[:, None, :]))
            value_low = low(projected[..., query_width + HEAD:])
            member_parts = (query_rot.reshape(per_block, TOK_DEV, GROUPS, Q_PER, HEAD), key_rot.reshape(per_block, TOK_DEV, GROUPS, HEAD), value_low.reshape(per_block, TOK_DEV, GROUPS, HEAD), seq_block.reshape(per_block, TOK_DEV), valid_block.reshape(per_block, TOK_DEV))
            mixed_heads = lax.map(jax.checkpoint(attend), member_parts)
            mixed_heads = low(low_back(mixed_heads.reshape(row_count, GROUPS, query_width)))
            attn_branch = low_back(jnp.einsum('tgc,gcd->td', mixed_heads, w_out, precision=HIGH))
            hidden_stream = stream + attn_branch
            normed_two = low(rms_norm(hidden_stream, gain_two))
            gate_pre = low_back(jnp.dot(normed_two, w_gate, precision=HIGH))
            upper = low_back(jnp.dot(normed_two, w_up, precision=HIGH))
            inner_act = low(jax.nn.silu(gate_pre) * upper)
            stream = hidden_stream + low_back(jnp.dot(inner_act, w_down, precision=HIGH))
        return stream

    def forward(stream_all, weights):

        def step_block(carry, block_index):
            row_start = (block_index * span_rows).astype(jnp.int32)
            piece_rows = lax.dynamic_slice_in_dim(stream_all, row_start, span_rows, 0)
            seq_block = lax.dynamic_slice_in_dim(seq_ids, row_start, span_rows, 0)
            valid_block = lax.dynamic_slice_in_dim(valid_mask, row_start, span_rows, 0)
            cos_block = lax.dynamic_slice_in_dim(cosine, row_start, span_rows, 0)
            sin_block = lax.dynamic_slice_in_dim(sine, row_start, span_rows, 0)
            result = jax.checkpoint(two_layers)(piece_rows, seq_block, valid_block, cos_block, sin_block, weights)
            return (carry, result)
        carry_end, outputs = lax.scan(step_block, jnp.zeros((), jnp.int32), jnp.arange(block_count, dtype=jnp.int32))
        return outputs.reshape(TOKENS, D)
    weights32 = (attn_in.astype(jnp.float32), attn_out.astype(jnp.float32), gate_weight.astype(jnp.float32), up_weight.astype(jnp.float32), down_weight.astype(jnp.float32), attn_gain.astype(jnp.float32), ffn_gain.astype(jnp.float32))
    primal, pullback = jax.vjp(forward, tokens.astype(jnp.float32), weights32)
    grad_x, grad_all = pullback(cotangent.astype(jnp.float32))
    g_in, g_out, g_gate, g_up, g_down, g_gain_one, g_gain_two = grad_all
    group_order = jnp.arange(GROUPS, dtype=jnp.int32)
    sharing = (group_owner[:, None] == group_owner[None, :]) & (group_order[None, :] < group_order[:, None])
    group_rank = lax.optimization_barrier(jnp.sum(sharing.astype(jnp.int32), axis=1))
    slot_ids = jnp.arange(SLOTS * N_NARROW, dtype=jnp.int32)
    slot_pick = (group_owner[None, :] == slot_ids[:, None] // SLOTS) & (group_rank[None, :] == slot_ids[:, None] % SLOTS)
    slot_live = jnp.any(slot_pick, axis=1)
    chosen = lax.optimization_barrier(jnp.sum(jnp.where(slot_pick, group_order[None, :], 0), axis=1)).astype(jnp.int32)
    slot_in = jnp.where(slot_live[:, None, None], jnp.take(g_in, chosen, axis=0), jnp.zeros((), g_in.dtype))
    slot_out = jnp.where(slot_live[:, None, None], jnp.take(g_out, chosen, axis=0), jnp.zeros((), g_out.dtype))
    return (primal.astype(jnp.bfloat16), grad_x.astype(jnp.bfloat16), slot_in, slot_out, g_gate, g_up, g_down, g_gain_one, g_gain_two)
```

```python
import functools
import math

import jax
import jax.numpy as jnp
from jax import lax
from jax.experimental import pallas as pl
from jax.experimental.pallas import tpu as pltpu
from jax.sharding import PartitionSpec as P

HEAD = 64
Q_PER = 3
SLOTS = 2
EPS = 1e-05
THETA = 10000.0
RB = 128
F32 = jnp.float32
BF16 = jnp.bfloat16
NEG = -1e30
VMEM_LIMIT = 56 * 1024 * 1024


def dot(a, b):
    return jnp.dot(a, b, preferred_element_type=F32)


def dot_nt(a, b):
    return lax.dot_general(a, b, (((1,), (1,)), ((), ())), preferred_element_type=F32)


def dot_tn(a, b):
    return lax.dot_general(a, b, (((0,), (0,)), ((), ())), preferred_element_type=F32)


def lane_iota(rows):
    return lax.broadcasted_iota(jnp.int32, (rows, 128), 1)


def low_half(rows):
    return lane_iota(rows) < HEAD


def rope128(v, cs, sn):
    lane = lane_iota(v.shape[0])
    partner = jnp.where((lane & 63) < 32, pltpu.roll(v, 96, 1), pltpu.roll(v, 32, 1))
    return v * cs + partner * sn


def allowed_bias(seqc_ref, seqr_ref, valr_ref, r0, nk):
    t = r0 + lax.broadcasted_iota(jnp.int32, (RB, nk), 0)
    u = lax.broadcasted_iota(jnp.int32, (RB, nk), 1)
    same = seqc_ref[r0 : r0 + RB, :] == seqr_ref[:, :nk]
    ok = (same & (u <= t) & (valr_ref[:, :nk] == 1)) | (u == t)
    return jnp.where(ok, 0.0, NEG).astype(F32)


def masked_heads(x, y):
    low = low_half(1).astype(F32)
    low_b, high_b = low.astype(BF16), (1.0 - low).astype(BF16)
    return jnp.concatenate([x * low_b, x * high_b, y * low_b], axis=0)


def fwd_kernel(
    second, t, groups, *refs
):
    it = iter(refs)
    x_ref = next(it)
    add_ref = next(it) if second else None
    win, wout, g1, g2, cs_ref, sn_ref, seqc, seqr, valr, wg, wu, wd = (next(it) for _ in range(12))
    cot = next(it) if second else None
    n1_ref, qk_ref, kt_ref, vt_ref, o_ref, lse_ref, h_ref, n2_ref = (next(it) for _ in range(8))
    if second:
        x_out, hid_ref, dgate_ref, dup_ref, part_ref, dn2_ref = (next(it) for _ in range(6))
    else:
        gate_ref, up_ref, hid_ref, part_ref = (next(it) for _ in range(4))
    acc = next(it)
    d = n1_ref.shape[1]

    if second:
        x = x_ref[...] + add_ref[...]
        x_out[...] = x
    else:
        x = x_ref[...].astype(F32)
    r1 = lax.rsqrt(jnp.mean(x * x, axis=1, keepdims=True) + EPS)
    n1_ref[...] = (x * r1 * g1[...]).astype(BF16)
    acc[...] = x
    lse_ref[...] = jnp.zeros_like(lse_ref)

    def group(g, carry):
        n1 = n1_ref[...]
        qk = dot(n1, win[g, :, :256])
        v = dot(n1, win[g, :, 256:320])
        cs, sn = cs_ref[...], sn_ref[...]
        xr = rope128(qk[:, :128], cs, sn)
        yr = rope128(qk[:, 128:], cs, sn)
        qk_ref[g, :, :128] = xr.astype(BF16)
        qk_ref[g, :, 128:] = yr.astype(BF16)
        kt_ref[g] = jnp.where(low_half(t), pltpu.roll(yr, 64, 1), yr).astype(BF16)
        vt_ref[g] = jnp.concatenate([v, v], axis=1).astype(BF16)
        for rb in range(t // RB):
            r0, nk = rb * RB, (rb + 1) * RB
            rows = slice(r0, r0 + RB)
            q = masked_heads(qk_ref[g, rows, :128], qk_ref[g, rows, 128:])
            s = dot_nt(q, kt_ref[g, :nk, :])
            bias = allowed_bias(seqc, seqr, valr, r0, nk)
            s = (s.reshape(3, RB, nk) * 0.125 + bias[None]).reshape(3 * RB, nk)
            m = jnp.max(s, axis=1, keepdims=True)
            e = jnp.exp(s - m)
            l = jnp.sum(e, axis=1, keepdims=True)
            o = dot(e.astype(BF16), vt_ref[g, :nk, :]) / l
            low = low_half(RB)
            o_ref[g, rows, :128] = jnp.where(low, o[:RB], o[RB : 2 * RB]).astype(BF16)
            o_ref[g, rows, 128:] = jnp.where(low, o[2 * RB :], 0.0).astype(BF16)
            ls = m + jnp.log(l)
            lane = lane_iota(RB)
            cur = lse_ref[rows, :]
            for j in range(3):
                cur = jnp.where(lane == g * 3 + j, ls[j * RB : (j + 1) * RB], cur)
            lse_ref[rows, :] = cur
        acc[...] += dot(o_ref[g, :, :192], wout[g])
        return carry

    lax.fori_loop(0, groups, group, 0)
    h = acc[...]
    h_ref[...] = h
    r2 = lax.rsqrt(jnp.mean(h * h, axis=1, keepdims=True) + EPS)
    n2_ref[...] = (h * r2 * g2[...]).astype(BF16)
    for rb in range(t // 256):
        rows = slice(rb * 256, rb * 256 + 256)
        n2 = n2_ref[rows, :]
        gate = dot(n2, wg[...])
        up = dot(n2, wu[...])
        sig = jax.nn.sigmoid(gate)
        act = gate * sig
        hid = (act * up).astype(BF16)
        hid_ref[rows, :] = hid
        part_ref[rows, :] = dot(hid, wd[...])
        if second:
            dhid = dot_nt(cot[rows, :], wd[...])
            dgate = (dhid * up * sig * (1.0 + gate * (1.0 - sig))).astype(BF16)
            dup = (dhid * act).astype(BF16)
            dgate_ref[rows, :] = dgate
            dup_ref[rows, :] = dup
            dn2_ref[rows, :] = dot_nt(dgate, wg[...]) + dot_nt(dup, wu[...])
        else:
            gate_ref[rows, :] = gate
            up_ref[rows, :] = up


def norm_back(dn, stream, gain):
    r = lax.rsqrt(jnp.mean(stream * stream, axis=1, keepdims=True) + EPS)
    m = stream * r
    dgain = jnp.sum(dn * m, axis=0, keepdims=True)
    dm = dn * gain
    return r * (dm - m * jnp.mean(dm * m, axis=1, keepdims=True)), dgain


def bwd_kernel(last, t, groups, *refs):
    it = iter(refs)
    (dz_ref, dn2_ref, h_ref, x_ref, qk_ref, kt_ref, vt_ref, o_ref, lse_ref,
     win, wout, g1, g2, cs_ref, sn_ref, seqc, seqr, valr) = (next(it) for _ in range(18))
    da_ref, dproj_ref, dx_ref, dg1_ref, dg2_ref = (next(it) for _ in range(5))
    acc, dkv = next(it), next(it)

    dh, dg2 = norm_back(dn2_ref[...], h_ref[...], g2[...])
    dh = dz_ref[...].astype(F32) + dh
    dg2_ref[...] = dg2
    da_ref[...] = dh.astype(BF16)
    acc[...] = jnp.zeros_like(acc)

    def group(g, carry):
        da = da_ref[...]
        cs, sn = cs_ref[...], -sn_ref[...]
        dkv[...] = jnp.zeros_like(dkv)
        low = low_half(RB)
        lane = lane_iota(RB)
        for rb in range(t // RB):
            r0, nk = rb * RB, (rb + 1) * RB
            rows = slice(r0, r0 + RB)
            do = dot_nt(da[rows], wout[g])
            dox = do[:, :128].astype(BF16)
            doy = jnp.concatenate([do[:, 128:192], jnp.zeros((RB, 64), F32)], axis=1).astype(BF16)
            px = dox.astype(F32) * o_ref[g, rows, :128].astype(F32)
            py = doy.astype(F32) * o_ref[g, rows, 128:].astype(F32)
            delta = jnp.concatenate(
                [
                    jnp.sum(jnp.where(low, px, 0.0), axis=1, keepdims=True),
                    jnp.sum(jnp.where(low, 0.0, px), axis=1, keepdims=True),
                    jnp.sum(py, axis=1, keepdims=True),
                ],
                axis=0,
            )
            ls = lse_ref[rows, :]
            lse = jnp.concatenate(
                [jnp.sum(jnp.where(lane == g * 3 + j, ls, 0.0), axis=1, keepdims=True) for j in range(3)],
                axis=0,
            )
            q = masked_heads(qk_ref[g, rows, :128], qk_ref[g, rows, 128:])
            dos = masked_heads(dox, doy)
            s = dot_nt(q, kt_ref[g, :nk, :])
            dp = dot_nt(dos, vt_ref[g, :nk, :])
            bias = allowed_bias(seqc, seqr, valr, r0, nk)
            s = (s.reshape(3, RB, nk) * 0.125 + bias[None]).reshape(3 * RB, nk)
            p = jnp.exp(s - lse)
            ds = (p * (dp - delta)).astype(BF16)
            dq = dot(ds, kt_ref[g, :nk, :])
            dkv[0, :nk, :] += dot_tn(ds, q)
            dkv[1, :nk, :] += dot_tn(p.astype(BF16), dos)
            dqx = jnp.where(low, dq[:RB], dq[RB : 2 * RB]) * 0.125
            dproj_ref[g, rows, :128] = rope128(dqx, cs[rows], sn[rows]).astype(BF16)
            dkv[2, rows, :] = dq[2 * RB :] * 0.125
        dk = dkv[0]
        dk = (dk + pltpu.roll(dk, 64, 1)) * 0.125
        dy = jnp.where(low_half(t), dkv[2], dk)
        dproj_ref[g, :, 128:256] = rope128(dy, cs, sn).astype(BF16)
        dv = dkv[1]
        dv = dv + pltpu.roll(dv, 64, 1)
        dproj_ref[g, :, 256:320] = dv[:, :64].astype(BF16)
        acc[...] += dot_nt(dproj_ref[g], win[g])
        return carry

    lax.fori_loop(0, groups, group, 0)
    dx, dg1 = norm_back(acc[...], x_ref[...].astype(F32), g1[...])
    dg1_ref[...] = dg1
    dx = dx + (dz_ref[...].astype(F32) + norm_back(dn2_ref[...], h_ref[...], g2[...])[0])
    dx_ref[...] = dx.astype(dx_ref.dtype)


def ffn_back_kernel(t, dz_ref, gate_ref, up_ref, wg, wu, wd, dgate_ref, dup_ref, dn2_ref, df_ref):
    for rb in range(t // 256):
        rows = slice(rb * 256, rb * 256 + 256)
        df = dz_ref[rows, :].astype(BF16)
        df_ref[rows, :] = df
        dhid = dot_nt(df, wd[...])
        gate, up = gate_ref[rows, :], up_ref[rows, :]
        sig = jax.nn.sigmoid(gate)
        dgate = (dhid * up * sig * (1.0 + gate * (1.0 - sig))).astype(BF16)
        dup = (dhid * gate * sig).astype(BF16)
        dgate_ref[rows, :] = dgate
        dup_ref[rows, :] = dup
        dn2_ref[rows, :] = dot_nt(dgate, wg[...]) + dot_nt(dup, wu[...])


def ffn_grad_kernel(add, *refs):
    n2, dgate, dup, hid, df = refs[:5]
    outs = refs[-3:]
    old = refs[5:8] if add else (None,) * 3
    for out, base, a, b in zip(outs, old, (n2, n2, hid), (dgate, dup, df)):
        rows = out.shape[0]
        for r in range(0, rows, 320):
            v = dot_tn(a[:, r : r + 320], b[...])
            out[r : r + 320, :] = v + base[r : r + 320, :] if add else v


def attn_grad_kernel(idx, n1a, n1b, dpa, dpb, oa, ob, daa, dab, gin, gout):
    for s in range(SLOTS):
        g = idx[s]
        live = idx[SLOTS + s].astype(F32)
        gin[s] = (dot_tn(n1a[...], dpa[g]) + dot_tn(n1b[...], dpb[g])) * live
        gout[s] = (dot_tn(oa[g, :, :192], daa[...]) + dot_tn(ob[g, :, :192], dab[...])) * live


def call(kernel, outs, ins, scratch=(), smem=0, flops=0):
    specs = [pl.BlockSpec(memory_space=pltpu.SMEM)] * smem
    specs += [pl.BlockSpec(memory_space=pltpu.VMEM)] * (len(ins) - smem)
    moved = sum(math.prod(a.shape) * a.dtype.itemsize for a in list(ins) + list(outs))
    return pl.pallas_call(
        kernel,
        out_shape=tuple(outs),
        in_specs=specs,
        out_specs=tuple(pl.BlockSpec(memory_space=pltpu.VMEM) for _ in outs),
        scratch_shapes=list(scratch),
        compiler_params=pltpu.CompilerParams(vmem_limit_bytes=VMEM_LIMIT),
        cost_estimate=pl.CostEstimate(flops=flops, bytes_accessed=moved, transcendentals=0),
    )(*ins)


def S(shape, dtype):
    return jax.ShapeDtypeStruct(shape, dtype)


class Links:
    def __init__(self, mesh):
        self.wide, self.narrow = mesh.shape["wide"], mesh.shape["narrow"]
        self.known = (self.wide, self.narrow) == (8, 4)

    def permute(self, v, step):
        pairs = []
        for w in range(self.wide):
            for n in range(self.narrow):
                to = step(w // 2, w % 2, n // 2, n % 2)
                if to is not None:
                    z, x, y, c = to
                    pairs.append((w * self.narrow + n, (z * 2 + x) * self.narrow + y * 2 + c))
        return lax.ppermute(v, ("wide", "narrow"), pairs)

    def core(self, v):
        return self.permute(v, lambda z, x, y, c: (z, x, y, 1 - c))

    def y(self, v):
        return self.permute(v, lambda z, x, y, c: (z, x, 1 - y, c))

    def x(self, v):
        return self.permute(v, lambda z, x, y, c: (z, 1 - x, y, c))

    def inward(self, v):
        return self.permute(v, lambda z, x, y, c: ({0: 1, 3: 2}[z], x, y, c) if z in (0, 3) else None)

    def outward(self, v):
        return self.permute(v, lambda z, x, y, c: ({1: 0, 2: 3}[z], x, y, c) if z in (1, 2) else None)

    def middle(self, v):
        return self.permute(v, lambda z, x, y, c: (3 - z, x, y, c) if z in (1, 2) else None)

    def sum_narrow(self, v):
        if not self.known:
            return lax.psum(v, "narrow")
        c = lax.axis_index("narrow") % 2
        h = v.shape[0] // 2
        keep = lax.dynamic_slice_in_dim(v, c * h, h, 0)
        send = lax.dynamic_slice_in_dim(v, (1 - c) * h, h, 0)
        r = keep + self.core(send)
        r = r + self.y(r)
        o = self.core(r)
        return jnp.where(c == 0, jnp.concatenate([r, o], 0), jnp.concatenate([o, r], 0))

    def sum_wide(self, v):
        if not self.known:
            return lax.psum(v, "wide")
        w = lax.axis_index("wide")
        x, z = w % 2, w // 2
        h = v.shape[0] // 2
        keep = lax.dynamic_slice_in_dim(v, x * h, h, 0)
        send = lax.dynamic_slice_in_dim(v, (1 - x) * h, h, 0)
        r = keep + self.x(send)
        r = r + self.inward(r)
        r = r + self.middle(r)
        r = jnp.where((z == 1) | (z == 2), r, self.outward(r))
        o = self.x(r)
        return jnp.where(x == 0, jnp.concatenate([r, o], 0), jnp.concatenate([o, r], 0))


def per_device(links, tokens, attn_in, attn_out, gate_weight, up_weight, down_weight, attn_gain, ffn_gain,
               cotangent, seq_ids, positions, valid_mask, group_owner):
    t, d = tokens.shape
    groups = attn_in.shape[0]
    f = gate_weight.shape[1]
    member = lax.axis_index("narrow")
    order = jnp.arange(groups, dtype=jnp.int32)
    sharing = (group_owner[:, None] == group_owner[None, :]) & (order[None, :] < order[:, None])
    rank = jnp.sum(sharing.astype(jnp.int32), axis=1)
    pick = (group_owner[None, :] == member) & (rank[None, :] == jnp.arange(SLOTS, dtype=jnp.int32)[:, None])
    live = jnp.any(pick, axis=1)
    chosen = jnp.sum(jnp.where(pick, order[None, :], 0), axis=1)
    idx = jnp.concatenate([chosen, live.astype(jnp.int32)]).astype(jnp.int32)

    lane = jnp.arange(128, dtype=jnp.int32)
    half = HEAD // 2
    freq = THETA ** (-(lane % half).astype(F32) / half)
    angles = positions.astype(F32)[:, None] * freq[None, :]
    cs = jnp.cos(angles)
    sn = jnp.sin(angles) * jnp.where(lane % HEAD < half, -1.0, 1.0).astype(F32)[None, :]
    seqc, seqr, valr = seq_ids.reshape(t, 1), seq_ids.reshape(1, t), valid_mask.reshape(1, t)
    g1, g2 = attn_gain.reshape(1, d), ffn_gain.reshape(1, d)

    saved = [S((t, d), BF16), S((groups, t, 256), BF16), S((groups, t, 128), BF16), S((groups, t, 128), BF16),
             S((groups, t, 256), BF16), S((t, 128), F32), S((t, d), F32), S((t, d), BF16)]
    scratch = [pltpu.VMEM((t, d), F32)]
    weights = [attn_in, attn_out, g1, g2, cs, sn, seqc, seqr, valr]
    ffn_w = [gate_weight, up_weight, down_weight]
    *kept1, gate1, up1, hid1, part1 = call(
        functools.partial(fwd_kernel, False, t, groups),
        saved + [S((t, f), F32), S((t, f), F32), S((t, f), BF16), S((t, d), F32)],
        [tokens] + weights + ffn_w, scratch, flops=6 * 10**9,
    )
    sum1 = links.sum_narrow(part1)
    *kept2, x1, hid2, dgate2, dup2, part2, dn2p2 = call(
        functools.partial(fwd_kernel, True, t, groups),
        saved + [S((t, d), F32), S((t, f), BF16), S((t, f), BF16), S((t, f), BF16), S((t, d), F32), S((t, d), F32)],
        [kept1[6], sum1] + weights + ffn_w + [cotangent], scratch, flops=8 * 10**9,
    )
    n1a, qk1, kt1, vt1, o1, lse1, h1, n2a = kept1
    n1b, qk2, kt2, vt2, o2, lse2, h2, n2b = kept2
    dn2_2 = links.sum_narrow(dn2p2)
    grads = call(
        functools.partial(ffn_grad_kernel, False),
        [S((d, f), F32), S((d, f), F32), S((f, d), F32)],
        [n2b, dgate2, dup2, hid2, cotangent], flops=2 * 10**9,
    )
    bscratch = [pltpu.VMEM((t, d), F32), pltpu.VMEM((3, t, 128), F32)]
    bouts = [S((t, d), BF16), S((groups, t, 320), BF16)]
    gains = [S((1, d), F32), S((1, d), F32)]
    da2, dproj2, dz1, dg1b, dg2b = call(
        functools.partial(bwd_kernel, False, t, groups), bouts + [S((t, d), F32)] + gains,
        [cotangent, dn2_2, h2, x1, qk2, kt2, vt2, o2, lse2] + weights, bscratch, flops=8 * 10**9,
    )
    dgate1, dup1, dn2p1, df1 = call(
        functools.partial(ffn_back_kernel, t), [S((t, f), BF16), S((t, f), BF16), S((t, d), F32), S((t, d), BF16)],
        [dz1, gate1, up1] + ffn_w, flops=2 * 10**9,
    )
    dn2_1 = links.sum_narrow(dn2p1)
    grads = call(
        functools.partial(ffn_grad_kernel, True),
        [S((d, f), F32), S((d, f), F32), S((f, d), F32)],
        [n2a, dgate1, dup1, hid1, df1, *grads], flops=2 * 10**9,
    )
    da1, dproj1, dx, dg1a, dg2a = call(
        functools.partial(bwd_kernel, True, t, groups), bouts + [S((t, d), BF16)] + gains,
        [dz1, dn2_1, h1, tokens, qk1, kt1, vt1, o1, lse1] + weights, bscratch, flops=8 * 10**9,
    )
    gin, gout = call(
        attn_grad_kernel, [S((SLOTS, d, 320), F32), S((SLOTS, 192, d), F32)],
        [idx, n1a, n1b, dproj1, dproj2, o1, o2, da1, da2], smem=1, flops=2 * 10**9,
    )
    small = jnp.concatenate([dg1a + dg1b, dg2a + dg2b], axis=0)
    small = lax.psum(small, "wide")
    ggate, gup, gdown = (links.sum_wide(v) for v in grads)
    gin = links.sum_wide(gin.reshape(SLOTS * d, 320)).reshape(SLOTS, d, 320)
    gout = links.sum_wide(gout.reshape(SLOTS * 192, d)).reshape(SLOTS, 192, d)
    layer_out = (h2 + lax.psum(part2, "narrow")).astype(BF16)
    return layer_out, dx, gin, gout, ggate, gup, gdown, small[0], small[1]


def solution(mesh):
    in_specs = (P("wide", None), P(), P(), P(None, "narrow"), P(None, "narrow"), P("narrow", None), P(), P(),
                P("wide", None), P("wide"), P("wide"), P("wide"), P())
    out_specs = (P("wide", None), P("wide", None), P("narrow", None, None), P("narrow", None, None),
                 P(None, "narrow"), P(None, "narrow"), P("narrow", None), P(), P())
    return jax.shard_map(functools.partial(per_device, Links(mesh)), mesh=mesh, in_specs=in_specs,
                         out_specs=out_specs, check_vma=False)
```

```python
import functools
import math

import jax
import jax.numpy as jnp
from jax import lax
from jax.experimental import pallas as pl
from jax.experimental.pallas import tpu as pltpu
from jax.sharding import PartitionSpec as P

HEAD = 64
Q_PER = 3
SLOTS = 2
EPS = 1e-05
THETA = 10000.0
RB = 128
VMEM = 56
F32 = jnp.float32
BF16 = jnp.bfloat16
NEG = -1e30


def dot(a, b):
    return jnp.dot(a, b, preferred_element_type=F32)


def dot_nt(a, b):
    return lax.dot_general(a, b, (((1,), (1,)), ((), ())), preferred_element_type=F32)


def dot_tn(a, b):
    return lax.dot_general(a, b, (((0,), (0,)), ((), ())), preferred_element_type=F32)


def lane_iota(rows):
    return lax.broadcasted_iota(jnp.int32, (rows, 128), 1)


def low_half(rows):
    return lane_iota(rows) < HEAD


def rope128(v, cs, sn):
    lane = lane_iota(v.shape[0])
    partner = jnp.where((lane & 63) < 32, pltpu.roll(v, 96, 1), pltpu.roll(v, 32, 1))
    return v * cs + partner * sn


def allowed_bias(seqr_ref, valr_ref, r0, nk):
    t = r0 + lax.broadcasted_iota(jnp.int32, (RB, nk), 0)
    u = lax.broadcasted_iota(jnp.int32, (RB, nk), 1)
    mine = jnp.broadcast_to(seqr_ref[:, r0 : r0 + RB].astype(F32), (128, RB)).T[:, :1]
    same = mine == seqr_ref[:, :nk].astype(F32)
    ok = (same & (u <= t) & (valr_ref[:, :nk] == 1)) | (u == t)
    return jnp.where(ok, 0.0, NEG).astype(F32)


def masked_heads(x, y):
    low = low_half(1).astype(F32)
    low_b, high_b = low.astype(BF16), (1.0 - low).astype(BF16)
    return jnp.concatenate([x * low_b, x * high_b, y * low_b], axis=0)


def pack_half(xi, a, b):
    low = low_half(a.shape[0])
    at, bt = a[:, 512:], b[:, 512:]
    if xi == 0:
        return a[:, :256], b[:, :256], jnp.where(low, at, pltpu.roll(bt, 64, 1))
    return a[:, 256:512], b[:, 256:512], jnp.where(low, pltpu.roll(at, 64, 1), bt)


def store_pair(idx, ref, rows, a, b):
    for xi in range(2):
        @pl.when(idx[0] == xi)
        def _():
            p, q, r = pack_half(xi, a, b)
            ref[rows, :256] = p.astype(ref.dtype)
            ref[rows, 256:512] = q.astype(ref.dtype)
            ref[rows, 512:] = r.astype(ref.dtype)


def store_one(idx, ref, rows, a):
    low = low_half(a.shape[0])
    at = a[:, 512:]
    for xi in range(2):
        @pl.when(idx[0] == xi)
        def _():
            ref[rows, :256] = a[:, xi * 256 : xi * 256 + 256].astype(ref.dtype)
            ref[rows, 256:] = jnp.where(low, at if xi == 0 else pltpu.roll(at, 64, 1), 0.0).astype(ref.dtype)


def ffn_back(dhid, gate, up, sig):
    return dhid * up * sig * (1.0 + gate * (1.0 - sig)), dhid * (gate * sig)


def put_wide(ref, v):
    d = v.shape[1]
    ref[:, :d] = v
    if ref.shape[1] > d:
        ref[:, d:] = jnp.zeros((ref.shape[0], ref.shape[1] - d), ref.dtype)


def half_rows(ref, which, n):
    return ref[pl.ds(pl.multiple_of(which * n, 8), n), :]


def split_send(idx, whole, keep, send):
    n = keep.shape[0]
    put_wide(keep, half_rows(whole, idx[1], n))
    put_wide(send, half_rows(whole, 1 - idx[1], n))


def take_sum(idx, pieces, out):
    d = out.shape[1]
    if len(pieces) == 1:
        out[...] = pieces[0][:, :d]
        return
    n = pieces[0].shape[0]
    out[pl.ds(pl.multiple_of(idx[1] * n, n), n), :] = pieces[0][:, :d]
    out[pl.ds(pl.multiple_of((1 - idx[1]) * n, n), n), :] = pieces[1][:, :d]


class Late:
    def __init__(self, source, buffer, sems, at, grouped):
        self.source, self.buffer, self.sems, self.at, self.grouped = source, buffer, sems, at, grouped
        self.waited = False

    def copy(self, g=None):
        if g is None:
            return pltpu.make_async_copy(self.source, self.buffer, self.sems.at[self.at])
        return pltpu.make_async_copy(self.source.at[g], self.buffer.at[g], self.sems.at[self.at + g])

    def start(self):
        if self.grouped:
            for g in range(self.buffer.shape[0]):
                self.copy(g).start()
        else:
            self.copy().start()

    def wait(self):
        if not self.waited:
            self.copy().wait()
            self.waited = True
        return self.buffer


def ready(*refs):
    got = [r.wait() if isinstance(r, Late) else r for r in refs]
    return got if len(got) > 1 else got[0]


def ready_group(g, *refs):
    for r in refs:
        r.copy(g).wait()


def buffers(*refs):
    return [r.buffer for r in refs]


def fwd_kernel(second, split, part, groups, *refs):
    it = iter(refs)
    idx = next(it)
    x_ref = next(it)
    add_refs = [next(it) for _ in range(2 if split else 1)] if second else None
    win, wout, g1, g2, cs_ref, sn_ref, seqr, valr, wg, wu, wdt = (next(it) for _ in range(11))
    kt_old, vt_old, n2_old = (next(it) for _ in range(3)) if part else (None, None, None)
    cot = next(it) if second else None
    n1_ref, qk_ref, kt_ref, vt_ref, o_ref, lse_ref, h_ref, n2_ref, hidh_ref = (next(it) for _ in range(9))
    n2s_ref = next(it) if part else None
    x_out = next(it)
    if second:
        duh_ref, part_ref = next(it), next(it)
    else:
        gate_ref, up_ref = next(it), next(it)
    outs = [next(it) for _ in range(2 if split else 1)]
    acc, whole, ktf, vtf = (next(it) for _ in range(4))
    t = n1_ref.shape[0]
    base = part * t

    if second:
        take_sum(idx, add_refs, acc)
        x = x_ref[...] + acc[...]
        x_out[...] = x
    else:
        x = x_ref[:, base : base + t].astype(F32).T
        x_out[...] = x.astype(BF16)
    r1 = lax.rsqrt(jnp.mean(x * x, axis=1, keepdims=True) + EPS)
    n1_ref[...] = (x * r1 * g1[...]).astype(BF16)
    acc[...] = x
    flush(n1_ref)
    flush(x_out)
    lse_ref[...] = jnp.zeros_like(lse_ref)
    cs_ref, sn_ref = ready(cs_ref, sn_ref)
    win_l, wout_l = win, wout
    win, wout = buffers(win, wout)

    def group(g, carry):
        ready_group(g, win_l, wout_l)
        n1 = n1_ref[...]
        qk = dot_nt(n1, win[g, :256, :])
        v = dot_nt(n1, win[g, 256:320, :])
        cs, sn = cs_ref[base : base + t, :], sn_ref[base : base + t, :]
        xr = rope128(qk[:, :128], cs, sn)
        yr = rope128(qk[:, 128:], cs, sn)
        qk_ref[g, :, :128] = xr.astype(BF16)
        qk_ref[g, :, 128:] = yr.astype(BF16)
        kt = jnp.where(low_half(t), pltpu.roll(yr, 64, 1), yr).astype(BF16)
        vt = jnp.concatenate([v, v], axis=1).astype(BF16)
        kt_ref[g] = kt
        vt_ref[g] = vt
        if part:
            ktf[:base, :] = kt_old[g]
            vtf[:base, :] = vt_old[g]
        ktf[base : base + t, :] = kt
        vtf[base : base + t, :] = vt
        for rb in range(t // RB):
            r0 = rb * RB
            nk = base + r0 + RB
            rows = slice(r0, r0 + RB)
            q = masked_heads(qk_ref[g, rows, :128], qk_ref[g, rows, 128:])
            s = dot_nt(q, ktf[:nk, :])
            bias = allowed_bias(seqr, valr, base + r0, nk)
            s = (s.reshape(3, RB, nk) * 0.125 + bias[None]).reshape(3 * RB, nk)
            m = jnp.max(s, axis=1, keepdims=True)
            e = jnp.exp(s - m)
            l = jnp.sum(e, axis=1, keepdims=True)
            o = dot(e.astype(BF16), vtf[:nk, :]) / l
            low = low_half(RB)
            o_ref[g, rows, :128] = jnp.where(low, o[:RB], o[RB : 2 * RB]).astype(BF16)
            o_ref[g, rows, 128:] = jnp.where(low, o[2 * RB :], 0.0).astype(BF16)
            ls = m + jnp.log(l)
            lane = lane_iota(RB)
            cur = lse_ref[rows, :]
            for j in range(3):
                cur = jnp.where(lane == g * 3 + j, ls[j * RB : (j + 1) * RB], cur)
            lse_ref[rows, :] = cur
        acc[...] += dot(o_ref[g, :, :192], wout[g])
        return carry

    lax.fori_loop(0, groups, group, 0)
    for ref in (qk_ref, kt_ref, vt_ref, o_ref, lse_ref):
        flush(ref)
    h = acc[...]
    h_ref[...] = h
    flush(h_ref)
    r2 = lax.rsqrt(jnp.mean(h * h, axis=1, keepdims=True) + EPS)
    n2 = (h * r2 * g2[...]).astype(BF16)
    n2_ref[...] = n2
    flush(n2_ref)
    if part:
        n2_old = ready(n2_old)
        if split:
            for c in range(2):
                @pl.when(idx[1] == c)
                def _():
                    put_wide(n2s_ref, (n2_old if c == 0 else n2_ref)[...].astype(F32))
        else:
            put_wide(n2s_ref.at[:t, :], n2_old[...].astype(F32))
            put_wide(n2s_ref.at[t:, :], n2_ref[...].astype(F32))
    if part:
        flush(n2s_ref)
    wg, wu, wdt = ready(wg, wu, wdt)
    every = slice(0, t)
    gate = dot(n2, wg[...])
    up = dot(n2, wu[...])
    sig = jax.nn.sigmoid(gate)
    hid = gate * sig * up
    store_one(idx, hidh_ref, every, hid)
    flush(hidh_ref)
    if second:
        cot = ready(cot)
        part_ref[...] = dot_nt(hid.astype(BF16), wdt[...])
        flush(part_ref)
        dgate, dup = ffn_back(dot(cot[base : base + t, :], wdt[...]), gate, up, sig)
        store_pair(idx, duh_ref, every, dgate, dup)
        flush(duh_ref)
        whole[...] = dot_nt(dgate.astype(BF16), wg[...]) + dot_nt(dup.astype(BF16), wu[...])
    else:
        gate_ref[...] = gate
        up_ref[...] = up
        flush(gate_ref)
        flush(up_ref)
        whole[...] = dot_nt(hid.astype(BF16), wdt[...])
    if split:
        split_send(idx, whole, *outs)
    else:
        put_wide(outs[0], whole[...])


def norm_back(dn, stream, gain):
    r = lax.rsqrt(jnp.mean(stream * stream, axis=1, keepdims=True) + EPS)
    m = stream * r
    dgain = jnp.sum(dn * m, axis=0, keepdims=True)
    dm = dn * gain
    return r * (dm - m * jnp.mean(dm * m, axis=1, keepdims=True)), dgain


def bwd_enter(idx, dn2_refs, dz_ref, h_ref, g2, dh_ref, da_ref, dg2_ref):
    take_sum(idx, dn2_refs, dh_ref)
    dh, dg2 = norm_back(dh_ref[...], h_ref[...], g2[...])
    dh = dz_ref[...].astype(F32) + dh
    dh_ref[...] = dh
    da_ref[...] = dh.astype(BF16)
    dg2_ref[...] = dg2


def bwd_block(g, r0, base, da, qk_ref, o_ref, lse_ref, ktf, vtf, wout, seqr, valr, dkv):
    low, lane = low_half(RB), lane_iota(RB)
    nk = base + r0 + RB
    rows = slice(r0, r0 + RB)
    do = dot_nt(da[rows], wout[g])
    dox = do[:, :128].astype(BF16)
    doy = jnp.concatenate([do[:, 128:192], jnp.zeros((RB, 64), F32)], axis=1).astype(BF16)
    px = dox.astype(F32) * o_ref[g, rows, :128].astype(F32)
    py = doy.astype(F32) * o_ref[g, rows, 128:].astype(F32)
    delta = jnp.concatenate(
        [
            jnp.sum(jnp.where(low, px, 0.0), axis=1, keepdims=True),
            jnp.sum(jnp.where(low, 0.0, px), axis=1, keepdims=True),
            jnp.sum(py, axis=1, keepdims=True),
        ],
        axis=0,
    )
    ls = lse_ref[rows, :]
    lse = jnp.concatenate(
        [jnp.sum(jnp.where(lane == g * 3 + j, ls, 0.0), axis=1, keepdims=True) for j in range(3)], axis=0
    )
    q = masked_heads(qk_ref[g, rows, :128], qk_ref[g, rows, 128:])
    dos = masked_heads(dox, doy)
    kt = ktf(nk)
    s = dot_nt(q, kt)
    dp = dot_nt(dos, vtf(nk))
    bias = allowed_bias(seqr, valr, base + r0, nk)
    s = (s.reshape(3, RB, nk) * 0.125 + bias[None]).reshape(3 * RB, nk)
    p = jnp.exp(s - lse)
    ds = (p * (dp - delta)).astype(BF16)
    dq = dot(ds, kt) * 0.125
    dkv[0, :nk, :] += dot_tn(ds, q)
    dkv[1, :nk, :] += dot_tn(p.astype(BF16), dos)
    return jnp.where(low, dq[:RB], dq[RB : 2 * RB]), dq[2 * RB :]


def bwd_a_kernel(split, groups, *refs):
    it = iter(refs)
    idx = next(it)
    dn2_refs = [next(it) for _ in range(2 if split else 1)]
    dz_ref, h_ref, qk_ref, kt_ref, vt_ref, o_ref, lse_ref, wout, g2, cs_ref, sn_ref, seqr, valr = (
        next(it) for _ in range(13))
    dh_ref, da_ref, dqx_ref, dqy_ref, dkv_ref, dg2_ref = (next(it) for _ in range(6))
    t = dh_ref.shape[0]
    bwd_enter(idx, dn2_refs, dz_ref, h_ref, g2, dh_ref, da_ref, dg2_ref)
    flush(dh_ref)
    flush(da_ref)
    dkv_ref[...] = jnp.zeros_like(dkv_ref)
    lse_ref, cs_ref, sn_ref = ready(lse_ref, cs_ref, sn_ref)
    waits = (qk_ref, kt_ref, vt_ref, o_ref, wout)
    qk_ref, kt_ref, vt_ref, o_ref, wout = buffers(*waits)

    def group(g, carry):
        ready_group(g, *waits)
        da = da_ref[...]
        for r0 in range(0, t, RB):
            rows = slice(r0, r0 + RB)
            dqx, dqy = bwd_block(g, r0, 0, da, qk_ref, o_ref, lse_ref, lambda n: kt_ref[g, :n, :],
                                 lambda n: vt_ref[g, :n, :], wout, seqr, valr, dkv_ref.at[g])
            dqx_ref[g, rows, :] = rope128(dqx, cs_ref[rows, :], -sn_ref[rows, :]).astype(BF16)
            dqy_ref[g, rows, :] = dqy
        return carry

    lax.fori_loop(0, groups, group, 0)


def bwd_b_kernel(last, split, groups, *refs):
    it = iter(refs)
    idx = next(it)
    dn2_refs = [next(it) for _ in range(2 if split else 1)]
    (dz_ref, h_ref, qk_ref, kt_ref, vt_ref, o_ref, lse_ref, xa_ref, xb_ref, kt_old, vt_old, dha_ref, dqxa_ref, dqya_ref,
     dkva_ref, win, wout, g1, g2, cs_ref, sn_ref, seqr, valr) = (next(it) for _ in range(23))
    da_ref, dpa_ref, dpb_ref, dxa_ref, dxb_ref, dg1_ref, dg2_ref = (next(it) for _ in range(7))
    dfs_ref = None if last else next(it)
    dh_ref, acca, accb, dkv, ktf, vtf, dqy_ref = (next(it) for _ in range(7))
    t = dh_ref.shape[0]
    bwd_enter(idx, dn2_refs, dz_ref, h_ref, g2, dh_ref, da_ref, dg2_ref)
    acca[...] = jnp.zeros_like(acca)
    flush(da_ref)
    accb[...] = jnp.zeros_like(accb)
    lse_ref, cs_ref, sn_ref = ready(lse_ref, cs_ref, sn_ref)
    waits = (qk_ref, kt_ref, vt_ref, o_ref, kt_old, vt_old, dqxa_ref, dqya_ref, dkva_ref, win, wout)
    qk_ref, kt_ref, vt_ref, o_ref, kt_old, vt_old, dqxa_ref, dqya_ref, dkva_ref, win, wout = buffers(*waits)

    def group(g, carry):
        ready_group(g, *waits)
        da = da_ref[...]
        ktf[:t, :] = kt_old[g]
        ktf[t:, :] = kt_ref[g]
        vtf[:t, :] = vt_old[g]
        vtf[t:, :] = vt_ref[g]
        dkv[:, :t, :] = dkva_ref[g]
        dkv[:, t:, :] = jnp.zeros((2, t, 128), F32)
        for r0 in range(0, t, RB):
            rows = slice(r0, r0 + RB)
            dqx, dqy = bwd_block(g, r0, t, da, qk_ref, o_ref, lse_ref, lambda n: ktf[:n, :], lambda n: vtf[:n, :],
                                 wout, seqr, valr, dkv)
            full = slice(t + r0, t + r0 + RB)
            dpb_ref[g, rows, :128] = rope128(dqx, cs_ref[full, :], -sn_ref[full, :]).astype(BF16)
            dqy_ref[rows, :] = dqy
        dpa_ref[g, :, :128] = dqxa_ref[g]
        low = low_half(t)
        for k, (ref, dqy) in enumerate(((dpa_ref, dqya_ref[g]), (dpb_ref, dqy_ref[...]))):
            rows = slice(k * t, k * t + t)
            dk, dv = dkv[0, rows, :], dkv[1, rows, :]
            dk = (dk + pltpu.roll(dk, 64, 1)) * 0.125
            dv = dv + pltpu.roll(dv, 64, 1)
            dy = jnp.where(low, dqy, dk)
            ref[g, :, 128:256] = rope128(dy, cs_ref[rows, :], -sn_ref[rows, :]).astype(BF16)
            ref[g, :, 256:320] = dv[:, :64].astype(BF16)
        acca[...] += dot(dpa_ref[g], win[g])
        accb[...] += dot(dpb_ref[g], win[g])
        return carry

    lax.fori_loop(0, groups, group, 0)
    flush(dpa_ref)
    flush(dpb_ref)
    xa_ref, xb_ref, dha_ref = ready(xa_ref, xb_ref, dha_ref)
    dxa, dg1a = norm_back(acca[...], xa_ref[...].astype(F32), g1[...])
    dxb, dg1b = norm_back(accb[...], xb_ref[...].astype(F32), g1[...])
    dg1_ref[...] = dg1a + dg1b
    dxa_ref[...] = (dxa + dha_ref[...]).astype(dxa_ref.dtype)
    dxb_ref[...] = (dxb + dh_ref[...]).astype(dxb_ref.dtype)
    flush(dxa_ref)
    flush(dxb_ref)
    if not last:
        if split:
            for c in range(2):
                @pl.when(idx[1] == c)
                def _():
                    put_wide(dfs_ref, (dxa_ref if c == 0 else dxb_ref)[...].astype(BF16).astype(F32))
        else:
            put_wide(dfs_ref.at[:t, :], dxa_ref[...].astype(BF16).astype(F32))
            put_wide(dfs_ref.at[t:, :], dxb_ref[...].astype(BF16).astype(F32))


def ffn_back_kernel(split, *refs):
    idx, dza, dzb, gatea, gateb, upa, upb, wg, wu, wdt, duha, duhb, dfa, dfb, *rest = refs
    outs, whole = rest[:-1], rest[-1]
    per = len(outs) // 2
    for k, (dz_ref, gate_ref, up_ref, duh_ref, df_ref) in enumerate(
            ((dza, gatea, upa, duha, dfa), (dzb, gateb, upb, duhb, dfb))):
        df = ready(dz_ref)[...].astype(BF16)
        df_ref[...] = df
        flush(df_ref)
        wdt, gate_ref, up_ref = ready(wdt, gate_ref, up_ref)
        gate, up = gate_ref[...], up_ref[...]
        dgate, dup = ffn_back(dot(df, wdt[...]), gate, up, jax.nn.sigmoid(gate))
        store_pair(idx, duh_ref, slice(0, df.shape[0]), dgate, dup)
        flush(duh_ref)
        wg, wu = ready(wg, wu)
        whole[...] = dot_nt(dgate.astype(BF16), wg[...]) + dot_nt(dup.astype(BF16), wu[...])
        if split:
            split_send(idx, whole, *outs[per * k : per * k + per])
        else:
            put_wide(outs[k], whole[...])
        for ref in outs[per * k : per * k + per]:
            flush(ref)


def own_grads(n2, duh, hidh, df, base, put):
    for r in range(0, n2[0].shape[1], 320):
        put(0, r, sum((dot_tn(a[:, r : r + 320], b[...]) for a, b in zip(n2, duh)), base(0, r)))
        put(1, r, sum((dot_tn(a[:, r : r + 320], b[...]) for a, b in zip(df, hidh)), base(1, r)))


def peer_acts(n2, df, wgu, wdh, du, hd, rows):
    gu = dot(n2, wgu[...])
    dh = dot(df, wdh[...])
    ga, ua, tile = gu[:, :256], gu[:, 256:512], gu[:, 512:]
    turned = pltpu.roll(tile, 64, 1)
    sa, sb = jax.nn.sigmoid(ga), jax.nn.sigmoid(tile)
    low = low_half(n2.shape[0])
    hd[rows, :256] = (ga * sa * ua).astype(BF16)
    hd[rows, 256:] = jnp.where(low, tile * sb * turned, 0.0).astype(BF16)
    dga, dua = ffn_back(dh[:, :256], ga, ua, sa)
    dgb, dub = ffn_back(dh[:, 256:], tile, turned, sb)
    du[rows, :256] = dga.astype(BF16)
    du[rows, 256:512] = dua.astype(BF16)
    du[rows, 512:] = jnp.where(low, dgb, pltpu.roll(dub, 64, 1)).astype(BF16)


def peer_grads(n2p, dfp, wgu, wdh, scratch, base, put):
    n2, df, du, hd = scratch
    d = n2.shape[1]
    n = n2p[0].shape[0]
    for i in range(len(n2p)):
        rows = slice(i * n, i * n + n)
        n2[rows, :] = n2p[i][:, :d].astype(BF16)
        df[rows, :] = dfp[i][:, :d].astype(BF16)
        for r in range(i * n, i * n + n, 256):
            part = slice(r, r + 256)
            peer_acts(n2[part, :], df[part, :], wgu, wdh, du, hd, part)
    own_grads([n2], [du], [hd], [df], base, put)


def own_grads_kernel(*refs):
    n2, duh, hidh, cot, outs = refs[:2], refs[2:4], refs[4:6], refs[6], refs[7:]
    t = n2[0].shape[0]

    def put(k, r, v):
        outs[k][r : r + 320, :] = v
        flush(outs[k], slice(r, r + 320))

    own_grads(n2, duh, hidh, [cot.at[:t, :], cot.at[t:, :]], lambda k, r: 0.0, put)


def both_grads_kernel(count, *refs):
    n2p, dfp = refs[:count], refs[count : 2 * count]
    wgu, wdh, *rest = refs[2 * count :]
    n2, duh, hidh, df = (rest[2 * k : 2 * k + 2] for k in range(4))
    old, outs, scratch = rest[8:10], rest[10:12], rest[12:]

    def put(k, r, v):
        outs[k][r : r + 320, :] = v

    def put_last(k, r, v):
        outs[k][r : r + 320, :] = v
        flush(outs[k], slice(r, r + 320))

    old = ready(*old)
    own_grads(n2, duh, hidh, df, lambda k, r: old[k][r : r + 320, :], put)
    n2p, dfp = [ready(r) for r in n2p], [ready(r) for r in dfp]
    wgu, wdh = ready(wgu, wdh)
    peer_grads(n2p, dfp, wgu, wdh, scratch, lambda k, r: outs[k][r : r + 320, :], put_last)


def last_grads_kernel(count, n_chunks, *refs):
    n2p, dfp = refs[:count], refs[count : 2 * count]
    wgu, wdh, *rest = refs[2 * count :]
    old, chunks, scratch = rest[:2], rest[2 : 2 + n_chunks], rest[2 + n_chunks : 6 + n_chunks]
    gu, dn = rest[6 + n_chunks :]

    def put(k, r, v):
        (gu, dn)[k][r : r + 320, :] = v

    peer_grads(n2p, dfp, wgu, wdh, scratch, lambda k, r: ready(old[k])[r : r + 320, :], put)
    at = 0
    half = dn.shape[0] // 2
    for out in chunks:
        n = out.shape[0]
        if at < gu.shape[0]:
            out[...] = gu[at : at + n, :]
        else:
            r = at - gu.shape[0]
            a, b = dn[r : r + n, :], dn[half + r : half + r + n, :]
            out[:, :256] = a[:, :256]
            out[:, 256:512] = b[:, :256]
            out[:, 512:] = jnp.where(low_half(n), a[:, 256:], pltpu.roll(b[:, 256:], 64, 1))
        flush(out)
        at += n


def unpack_kernel(count, stacked, *refs):
    idx = refs[0]
    own, other, outs = refs[1 : 1 + count], refs[1 + count : 1 + 2 * count], refs[1 + 2 * count :]
    at = 0
    for o, p in zip(own, other):
        o, p = ready(o, p)
        n = o.shape[0]
        for xi in range(2):
            @pl.when(idx[0] == xi)
            def _():
                a, b = (o, p) if xi == 0 else (p, o)
                low = low_half(n)
                at4, bt4 = a[:, 512:], b[:, 512:]
                firsts = jnp.where(low, at4, pltpu.roll(bt4, 64, 1))
                seconds = jnp.where(low, pltpu.roll(at4, 64, 1), bt4)
                for k, tile in ((0, firsts), (1, seconds)):
                    ref = outs[0] if stacked else outs[k]
                    r = at + (k * (ref.shape[0] // 2) if stacked else 0)
                    ref[r : r + n, :256] = a[:, 256 * k : 256 * k + 256]
                    ref[r : r + n, 256:512] = b[:, 256 * k : 256 * k + 256]
                    ref[r : r + n, 512:] = tile
        for k in range(2):
            ref = outs[0] if stacked else outs[k]
            r = at + (k * (ref.shape[0] // 2) if stacked else 0)
            flush(ref, slice(r, r + n))
        at += n


def attn_grad_kernel(idx, *refs):
    n1, dp, o, da = (refs[4 * k : 4 * k + 4] for k in range(4))
    gains, keep2, keep0, keep1, send, whole, extra = refs[16:]

    def grads(g, out, at):
        out[at : at + 320, :] = sum(dot_tn(p[g], n[...]) for p, n in zip(dp, n1))
        out[at + 320 : at + 512, :] = sum(dot_tn(v[g, :, :192], a[...]) for v, a in zip(o, da))

    grads(idx[2], whole, 0)
    half = whole.shape[0] // 2
    lead = send.shape[0] - half
    for k, ref in enumerate((keep0, keep1)):
        put_wide(ref, whole[pl.ds(pl.multiple_of(idx[0] * half + k * (half // 2), 8), half // 2), :])
    put_wide(send.at[lead:, :], half_rows(whole, 1 - idx[0], half))
    grads(idx[3], whole, 0)
    rows_in, rows_out = 320 // idx_parts(extra), 192 // idx_parts(extra)
    extra[:rows_in, :] = whole[pl.ds(pl.multiple_of(idx[4] * rows_in, 8), rows_in), :]
    extra[rows_in : rows_in + rows_out, :] = whole[pl.ds(pl.multiple_of(320 + idx[4] * rows_out, 8), rows_out), :]
    n = rows_in + rows_out
    extra[n:, :] = jnp.zeros((extra.shape[0] - n, extra.shape[1]), F32)
    extra[n : n + 2, :] = gains[...]
    half = extra.shape[0] // 2
    put_wide(keep2, half_rows(extra, idx[0], half))
    put_wide(send.at[:lead, :], half_rows(extra, 1 - idx[0], half))


def attn_finish_kernel(parts, idx, a0, a1, b0, b1, slot1, gin, gout):
    d = gin.shape[2]
    for xi in range(2):
        @pl.when(idx[0] == xi)
        def _():
            p0, p1, q0, q1 = (a0, a1, b0, b1) if xi == 0 else (b0, b1, a0, a1)
            gin[0, :128, :] = p0[:, :d]
            gin[0, 128:256, :] = p1[:, :d]
            gin[0, 256:, :] = q0[:64, :d]
            gout[0, :64, :] = q0[64:, :d]
            gout[0, 64:, :] = q1[:, :d]
    mine = idx[5].astype(F32)
    rows_in, rows_out = 320 // parts, 192 // parts
    for k in range(parts):
        r = k * (rows_in + rows_out)
        gin[1, k * rows_in : (k + 1) * rows_in, :] = slot1[r : r + rows_in, :d] * mine
        gout[1, k * rows_out : (k + 1) * rows_out, :] = slot1[r + rows_in : r + rows_in + rows_out, :d] * mine


def idx_parts(extra):
    return 512 // (extra.shape[0] - 16)


BIG = 32 * 1024
OUT = {}


def flush(ref, rows=None):
    out, sem, whole = OUT[id(ref)]
    part = ref if rows is None else ref.at[rows, :]
    to = out if rows is None else out.at[rows, :]
    pltpu.make_async_copy(part, to, sem).start()
    OUT[id(ref)] = (out, sem, True)


def size(a):
    return math.prod(a.shape) * jnp.dtype(a.dtype).itemsize


def call(kernel, outs, ins, scratch=(), smem=0, flops=0, late=(), grouped=()):
    n_in, n_out = len(ins), len(outs)
    big_in = [i for i in range(smem, n_in) if size(ins[i]) >= BIG]
    big_out = [i for i in range(n_out) if size(outs[i]) >= BIG]
    in_specs = [
        pl.BlockSpec(memory_space=pltpu.SMEM if i < smem else pl.ANY if i in big_in else pltpu.VMEM) for i in range(n_in)
    ]
    out_specs = [pl.BlockSpec(memory_space=pl.ANY if i in big_out else pltpu.VMEM) for i in range(n_out)]
    buffers = [pltpu.VMEM(ins[i].shape, ins[i].dtype) for i in big_in]
    buffers += [pltpu.VMEM(outs[i].shape, outs[i].dtype) for i in big_out]
    at, n_sems = {}, 0
    for i in big_in:
        at[i] = n_sems
        n_sems += ins[i].shape[0] if i in grouped else 1
    out_at = n_sems
    sems = pltpu.SemaphoreType.DMA((n_sems + len(big_out),))

    def body(*refs):
        ins_, outs_, rest = list(refs[:n_in]), list(refs[n_in : n_in + n_out]), list(refs[n_in + n_out :])
        own, (bufs, sem) = rest[: len(scratch)], (rest[len(scratch) : -1], rest[-1])
        kept = []
        order = [i for i in big_in if i not in late and i not in grouped]
        order += [i for i in big_in if i in grouped] + [i for i in late if i in big_in]
        for i in order:
            k = big_in.index(i)
            item = Late(ins_[i], bufs[k], sem, at[i], i in grouped)
            item.start()
            kept.append((i, item))
        for i, item in kept:
            early = i not in late and i not in grouped
            ins_[i] = item.wait() if early else item
        OUT.clear()
        for k, i in enumerate(big_out):
            buf = bufs[len(big_in) + k]
            OUT[id(buf)] = (outs_[i], sem.at[out_at + k], False)
            outs_[i] = buf
        kernel(*ins_, *outs_, *own)
        for i in big_out:
            if not OUT[id(outs_[i])][2]:
                flush(outs_[i])
        for i, item in kept:
            assert item.grouped or item.waited
        for i in big_out:
            out, s, _ = OUT[id(outs_[i])]
            pltpu.make_async_copy(outs_[i], out, s).wait()
        OUT.clear()

    moved = sum(size(a) for a in list(ins) + list(outs))
    return pl.pallas_call(
        body,
        out_shape=tuple(outs),
        in_specs=in_specs,
        out_specs=tuple(out_specs),
        scratch_shapes=list(scratch) + buffers + [sems],
        compiler_params=pltpu.CompilerParams(vmem_limit_bytes=VMEM * 1024 * 1024),
        cost_estimate=pl.CostEstimate(flops=flops, bytes_accessed=moved, transcendentals=0),
    )(*ins)


def S(shape, dtype):
    return jax.ShapeDtypeStruct(shape, dtype)


class Links:
    def __init__(self, mesh):
        self.wide, self.narrow = mesh.shape["wide"], mesh.shape["narrow"]
        self.known = (self.wide, self.narrow) == (8, 4)

    def permute(self, v, step):
        pairs = []
        for w in range(self.wide):
            for n in range(self.narrow):
                to = step(w // 2, w % 2, n // 2, n % 2)
                if to is not None:
                    z, x, y, c = to
                    pairs.append((w * self.narrow + n, (z * 2 + x) * self.narrow + y * 2 + c))
        return lax.ppermute(v, ("wide", "narrow"), pairs)

    def core(self, v):
        return self.permute(v, lambda z, x, y, c: (z, x, y, 1 - c))

    def y(self, v):
        return self.permute(v, lambda z, x, y, c: (z, x, 1 - y, c))

    def x(self, v):
        return self.permute(v, lambda z, x, y, c: (z, 1 - x, y, c))

    def inward(self, v):
        return self.permute(v, lambda z, x, y, c: ({0: 1, 3: 2}[z], x, y, c) if z in (0, 3) else None)

    def outward(self, v):
        return self.permute(v, lambda z, x, y, c: ({1: 0, 2: 3}[z], x, y, c) if z in (1, 2) else None)

    def middle(self, v):
        return self.permute(v, lambda z, x, y, c: (3 - z, x, y, c) if z in (1, 2) else None)

    def sum_cores(self, pieces):
        return pieces[0] + self.core(pieces[1]) if self.known else pieces[0]

    def y_start(self, r):
        return self.y(r) if self.known else r

    def sum_chips(self, r, got):
        if not self.known:
            return [lax.psum(r, "narrow")]
        r = r + got
        return [r, self.core(r)]

    def both_cores(self, got):
        return [got, self.core(got)] if self.known else [got]

    def sum_lines(self, chunks, jobs, hooks):
        last = chunks[0]
        if not self.known:
            for job in jobs:
                last = job(last)
            *keeps, send = last
            n = len(chunks) + len(keeps)
            got = self.x(send)
            pairs, at = [], 0
            for keep in keeps:
                pairs.append((keep, at))
                at += keep.shape[0]
            vals, theirs, results = list(chunks) + [None] * len(pairs), [None] * n, {}
            groups = [list(range(k, self.wide, 2)) for k in range(2)]
            for i, (keep, at) in enumerate(pairs):
                vals[len(chunks) + i] = keep + got[at : at + keep.shape[0]]
            vals = [lax.psum(r, "wide", axis_index_groups=groups) for r in vals]
            theirs = [self.x(r) for r in vals]
            for c, hook in hooks.items():
                results[c] = hook(vals, theirs)
            return vals, theirs, results
        z = lax.axis_index("wide") // 2
        inner = (z == 1) | (z == 2)
        n_keep = 3
        n = len(chunks) + n_keep
        order = [*range(4), len(chunks), *range(4, len(chunks)), *range(len(chunks) + 1, n)]
        moved = [self.inward(r) for r in chunks] + [None] * n_keep
        vals, theirs, results = list(chunks) + [None] * n_keep, [None] * n, {}
        last = jobs[0](last)[0]
        for s in range(n + 3):
            for stage in range(4):
                c = s - stage
                if not 0 <= c < n:
                    continue
                c = order[c]
                if stage == 3:
                    theirs[c] = last = after(theirs[c], last)
                    if c in hooks:
                        results[c] = hooks[c](vals, theirs)
                        last = results[c][0]
                    continue
                new = after(moved[c], last)
                vals[c] = jnp.where(inner, vals[c], new) if stage == 2 else vals[c] + new
                last = vals[c]
                if stage == 0:
                    moved[c] = self.middle(vals[c])
                elif stage == 1:
                    moved[c] = self.outward(vals[c])
                else:
                    theirs[c] = self.x(vals[c])
            if s == 0:
                last = jobs[1](last)[0]
            if s == 1:
                *keeps, send = jobs[2](last)
                last = keeps[0]
                got = self.x(send)
            if s == 3:
                got = after(got, last)
                at = 0
                for i, keep in enumerate(keeps):
                    c = len(chunks) + i
                    vals[c] = last = keep + got[at : at + keep.shape[0]]
                    at += keep.shape[0]
                    moved[c] = self.inward(last)
        return vals, theirs, results

    def gather_narrow(self, v):
        if not self.known:
            return lax.all_gather(v, "narrow", axis=0, tiled=True)
        n = lax.axis_index("narrow")
        o = self.core(v)
        two = jnp.where(n % 2 == 0, jnp.concatenate([v, o], 0), jnp.concatenate([o, v], 0))
        o = self.y(two)
        return jnp.where(n // 2 == 0, jnp.concatenate([two, o], 0), jnp.concatenate([o, two], 0))


def tie(*groups):
    return lax.optimization_barrier(groups)


def after(v, *deps):
    return lax.optimization_barrier((v, *deps))[0]


CHUNKS = (240, 240, 240, 240, 240, 240)


def per_device(links, tokens, attn_in, attn_out, gate_weight, up_weight, down_weight, attn_gain, ffn_gain,
               cotangent, seq_ids, positions, valid_mask, group_owner):
    t, d = tokens.shape
    groups = attn_in.shape[0]
    f = gate_weight.shape[1]
    split = links.known
    member = lax.axis_index("narrow")
    xi = lax.axis_index("wide") % 2
    core = member % 2
    idx = jnp.stack([xi, core]).astype(jnp.int32)
    lane = jnp.arange(128, dtype=jnp.int32)
    half = HEAD // 2
    freq = THETA ** (-(lane % half).astype(F32) / half)
    angles = positions.astype(F32)[:, None] * freq[None, :]
    cs = jnp.cos(angles)
    sn = jnp.sin(angles) * jnp.where(lane % HEAD < half, -1.0, 1.0).astype(F32)[None, :]
    seqr, valr = seq_ids.reshape(1, t), valid_mask.reshape(1, t)
    g1, g2 = attn_gain.reshape(1, d), ffn_gain.reshape(1, d)
    win_t = jnp.swapaxes(attn_in, 1, 2)
    wd_t = down_weight.T

    def x_half(w):
        return lax.dynamic_slice_in_dim(w, xi * 256, 256, 1), lax.dynamic_slice_in_dim(w, 512 + xi * 64, 64, 1)

    (ga, gb), (ua, ub), (wa, wb) = x_half(gate_weight), x_half(up_weight), x_half(wd_t)
    wgu = jnp.concatenate([ga, ua, gb, ub], axis=1)
    wdh = jnp.concatenate([wa, wb, jnp.zeros((d, 64), BF16)], axis=1)

    th = t // 2
    sent = th if split else t
    wd = -(-d // 128) * 128
    piece = S((sent, wd), F32)
    sums = [S((th // 2, wd), F32)] * 2 if split else [S((th, wd), F32)]
    n_sums = len(sums)
    saved = [S((th, d), BF16), S((groups, th, 256), BF16), S((groups, th, 128), BF16), S((groups, th, 128), BF16),
             S((groups, th, 256), BF16), S((th, 128), F32), S((th, d), F32), S((th, d), BF16), S((th, 384), BF16)]
    scratch = [pltpu.VMEM((th, d), F32)] * 2 + [pltpu.VMEM((t, 128), BF16)] * 2
    weights = [win_t, attn_out, g1, g2, cs, sn, seqr, valr]
    ffn_w = [gate_weight, up_weight, wd_t]

    def forward(second, x, adds, old):
        part = old is not None
        outs = list(saved) + ([piece] if part else [])
        outs += [S((th, d), F32), S((th, f), BF16), S((th, d), F32)] if second else [S((th, d), BF16)] + [S((th, f), F32)] * 2
        ins = [idx, x, *adds] + weights + ffn_w
        at = 2 + len(adds)
        ins += [old[2], old[3], old[7]] if part else []
        ins += [cotangent] if second else []
        res = call(functools.partial(fwd_kernel, second, split, int(part), groups), outs + sums, ins, scratch, smem=1,
                   flops=4 * 10**9, grouped=[at, at + 1],
                   late=[at + 4, at + 5, at + 8, at + 9, at + 10] + ([at + 13] if part else [])
                   + ([len(ins) - 1] if second else []))
        return list(res[:-n_sums]), list(res[-n_sums:])

    cot_rows = lax.dynamic_slice_in_dim(cotangent, core * sent, sent, 0) if split else cotangent
    cot_s = jnp.pad(cot_rows.astype(F32), ((0, 0), (0, wd - d)))

    tokens_t = tokens.T
    cot_x = links.x(cot_s)
    a1, s1a = forward(False, tokens_t, [], None)
    *a1, tok_a, gate1a, up1a = a1
    r1a = links.sum_cores(s1a)
    y1a = links.y_start(r1a)
    b1, s1b = forward(False, after(tokens_t, r1a), [], a1)
    *b1, n2as, tok_b, gate1b, up1b = b1
    s1b, n2as, y1a, cot_x = tie(s1b, n2as, y1a, cot_x)
    sum1a = links.sum_chips(r1a, y1a)
    r1b = links.sum_cores(s1b)
    y1b = links.y_start(r1b)
    n2a_x = links.x(n2as)
    cot_p = links.both_cores(cot_x)
    a2, s2a = forward(True, after(a1[6], r1b), sum1a, None)
    *a2, x1a, duh2a, part2a = a2
    s2a, y1b, n2a_x = tie(s2a, y1b, n2a_x)
    sum1b = links.sum_chips(r1b, y1b)
    n2a_p = links.both_cores(n2a_x)
    r2a = links.sum_cores(s2a)
    y2a = links.y_start(r2a)
    b2, s2b = forward(True, after(b1[6], r2a, n2a_p, cot_p), sum1b, a2)
    *b2, n2bs, x1b, duh2b, part2b = b2
    h2a, h2b = a2[6], b2[6]
    s2b, n2bs, y2a = tie(s2b, n2bs, y2a)
    sum2a = links.sum_chips(r2a, y2a)
    r2b = links.sum_cores(s2b)
    y2b = links.y_start(r2b)
    n2b_x = links.x(n2bs)
    grad_outs = [S((d, f), F32), S((d, 384), F32)]
    gscratch = [pltpu.VMEM((t, d), BF16), pltpu.VMEM((t, d), BF16), pltpu.VMEM((t, f), BF16), pltpu.VMEM((t, 384), BF16)]

    tail = [cs, sn, seqr, valr]

    def backward_a(sums, dz, r):
        outs = [S((th, d), F32), S((th, d), BF16), S((groups, th, 128), BF16), S((groups, th, 128), F32),
                S((groups, 2, th, 128), F32), S((1, d), F32)]
        return call(
            functools.partial(bwd_a_kernel, split, groups), outs,
            [idx, *sums, dz, r[6], *r[1:6], attn_out, g2] + tail, smem=1, flops=4 * 10**9,
            grouped=[n_sums + 3, n_sums + 4, n_sums + 5, n_sums + 6, n_sums + 8], late=[n_sums + 7, n_sums + 10, n_sums + 11],
        )

    def backward_b(last, sums, dz, first, ra, rb, xa, xb):
        xt = BF16 if last else F32
        outs = [S((th, d), BF16), S((groups, th, 320), BF16), S((groups, th, 320), BF16), S((th, d), xt), S((th, d), xt),
                S((1, d), F32), S((1, d), F32)] + ([] if last else [piece])
        dha, _, dqxa, dqya, dkva, _ = first
        return call(
            functools.partial(bwd_b_kernel, last, split, groups), outs,
            [idx, *sums, dz, rb[6], *rb[1:6], xa, xb, ra[2], ra[3], dha, dqxa, dqya, dkva, win_t, attn_out, g1, g2] + tail,
            [pltpu.VMEM((th, d), F32)] * 3 + [pltpu.VMEM((2, t, 128), F32), pltpu.VMEM((t, 128), BF16),
             pltpu.VMEM((t, 128), BF16), pltpu.VMEM((th, 128), F32)],
            smem=1, flops=6 * 10**9,
            grouped=[n_sums + k for k in (3, 4, 5, 6, 10, 11, 13, 14, 15, 16, 17)],
            late=[n_sums + k for k in (7, 20, 21, 8, 9, 12)],
        )

    acc = call(own_grads_kernel, grad_outs, [after(a2[7], r2b, sum2a), b2[7], duh2a, duh2b, a2[8], b2[8], cotangent],
               flops=2 * 10**9)
    first2 = backward_a(after(sum2a, acc), cotangent[:th], a2)
    first2, y2b = tie(first2, y2b)
    sum2b = links.sum_chips(r2b, y2b)
    da2b, dp2a, dp2b, dz1a, dz1b, dg1b, dg2b1, dfs = backward_b(
        False, sum2b, cotangent[th:], first2, a2, b2, x1a, x1b)
    dfs, dz1a, dz1b, n2b_x = tie(dfs, dz1a, dz1b, n2b_x)
    df_x = links.x(dfs)
    n2b_p = links.both_cores(n2b_x)
    da2a, dg2b0 = first2[1], first2[5]
    res = call(
        functools.partial(ffn_back_kernel, split), [S((th, f), BF16)] * 2 + [S((th, d), BF16)] * 2 + sums * 2,
        [idx, dz1a, dz1b, gate1a, gate1b, up1a, up1b] + ffn_w, [pltpu.VMEM((th, d), F32)], smem=1, flops=2 * 10**9,
        late=[1, 9, 3, 5, 7, 8, 2, 4, 6],
    )
    duh1, df1, s3 = res[:2], res[2:4], res[4:]
    r3a, r3b = links.sum_cores(s3[:n_sums]), links.sum_cores(s3[n_sums:])
    y3a, y3b = links.y_start(r3a), links.y_start(r3b)
    acc = call(
        functools.partial(both_grads_kernel, len(n2b_p)), grad_outs,
        [*n2b_p, *cot_p, wgu, wdh, after(a1[7], r3a, r3b), b1[7], *duh1, a1[8], b1[8], *df1, *acc], gscratch,
        flops=6 * 10**9, late=[12 + 2 * len(n2b_p) - 2 + 0, 12 + 2 * len(n2b_p) - 1, *range(2 * len(n2b_p) + 2)],
    )
    acc, df_x = tie(acc, df_x)
    df_p = links.both_cores(df_x)
    count = len(df_p)
    chunks = call(
        functools.partial(last_grads_kernel, count, len(CHUNKS)), [S((n, f), F32) for n in CHUNKS],
        [*n2a_p, *df_p, wgu, wdh, *acc], gscratch + [pltpu.VMEM((d, f), F32), pltpu.VMEM((d, 384), F32)],
        flops=4 * 10**9, late=[2 * count + 2, 2 * count + 3],
    )
    quarter = 512 // links.narrow
    group_owner = after(group_owner, acc)
    order = jnp.arange(groups, dtype=jnp.int32)
    sharing = (group_owner[:, None] == group_owner[None, :]) & (order[None, :] < order[:, None])
    rank = jnp.sum(sharing.astype(jnp.int32), axis=1)
    first = jnp.sum(jnp.where((group_owner == member) & (rank == 0), order, 0))
    extra = jnp.sum(jnp.where(rank == 1, order, 0))
    extra_owner = jnp.sum(jnp.where(rank == 1, group_owner, 0))
    idx = jnp.stack([xi, core, first, extra, member, (extra_owner == member).astype(jnp.int32)]).astype(jnp.int32)
    chunks, y3a = tie(chunks, y3a)
    sum3a = links.sum_chips(r3a, y3a)
    lead = quarter // 2 + 8
    made = {}

    def job_a(dep):
        made["a"] = backward_a(after(sum3a, dep), dz1a, a1)
        return made["a"]

    def job_b(dep):
        first, got = tie(made["a"], y3b)
        sums = links.sum_chips(r3b, got)
        made["b"] = backward_b(True, after(sums, dep), dz1b, first, a1, b1, tok_a, tok_b)
        return made["b"]

    def job_grads(dep):
        first, (da1b, dp1a, dp1b, _, _, dg1a, dg2a1) = made["a"], made["b"]
        gains = jnp.concatenate([dg1a + dg1b, first[5] + dg2a1 + dg2b0 + dg2b1], axis=0)
        return call(
            attn_grad_kernel, [S((n, wd), F32) for n in (lead, 128, 128, lead + 256)],
            [idx, after(a1[0], dep), b1[0], a2[0], b2[0], dp1a, dp1b, dp2a, dp2b, a1[4], b1[4], a2[4], b2[4], first[1],
             da1b, da2a, da2b, gains],
            [pltpu.VMEM((512, d), F32), pltpu.VMEM((quarter + 16, d), F32)], smem=1, flops=2 * 10**9,
        )

    part2 = lax.psum(after((part2a, part2b), y3b), "narrow")

    def finish_out(vals, theirs):
        total = after(part2, vals[4])
        return [jnp.concatenate([h + p for h, p in zip((h2a, h2b), total)], axis=0).astype(BF16)]

    def unpack(vals, theirs):
        return call(functools.partial(unpack_kernel, 4, False), [S((d, f), F32)] * 2,
                    [idx, *vals[:4], *theirs[:4]], smem=1, late=[1, 5, 2, 6, 3, 7, 4, 8])

    def unpack_down(vals, theirs):
        return call(functools.partial(unpack_kernel, 2, True), [S((d, f), F32)],
                    [idx, *vals[4:6], *theirs[4:6]], smem=1, late=[1, 3, 2, 4])

    def collect(vals, theirs):
        r, o = vals[6], theirs[6]
        second = jnp.where(xi == 0, jnp.concatenate([r, o], 0), jnp.concatenate([o, r], 0))
        return second, links.gather_narrow(second[:quarter])

    done, theirs, results = links.sum_lines(
        chunks, [job_a, job_b, job_grads], {4: finish_out, 3: unpack, 5: unpack_down, 6: collect})
    layer_out = results[4][0]
    dx = jnp.concatenate(made["b"][3:5], axis=0)
    ggate, gup = results[3]
    gdown, = results[5]
    second, slot1 = results[6]
    small = second[quarter : quarter + 2, :d]
    gin, gout = call(
        functools.partial(attn_finish_kernel, links.narrow), [S((SLOTS, 320, d), F32), S((SLOTS, 192, d), F32)],
        [idx, *done[7:], *theirs[7:], slot1], smem=1,
    )
    gin = jnp.swapaxes(gin, 1, 2)
    return layer_out, dx, gin, gout, ggate, gup, gdown.T, small[0], small[1]


def _pad(outs, split):
    return list(outs) if split else list(outs) + [None]


def solution(mesh):
    in_specs = (P("wide", None), P(), P(), P(None, "narrow"), P(None, "narrow"), P("narrow", None), P(), P(),
                P("wide", None), P("wide"), P("wide"), P("wide"), P())
    out_specs = (P("wide", None), P("wide", None), P("narrow", None, None), P("narrow", None, None),
                 P(None, "narrow"), P(None, "narrow"), P("narrow", None), P(), P())
    return jax.shard_map(functools.partial(per_device, Links(mesh)), mesh=mesh, in_specs=in_specs,
                         out_specs=out_specs, check_vma=False)
```

```python
import functools
import math

import jax
import jax.numpy as jnp
from jax import lax
from jax.experimental import pallas as pl
from jax.experimental.pallas import tpu as pltpu
from jax.sharding import PartitionSpec as P

HEAD = 64
Q_PER = 3
SLOTS = 2
EPS = 1e-05
THETA = 10000.0
RB = 128
TR = 32
VMEM = 56
F32 = jnp.float32
BF16 = jnp.bfloat16
NEG = -1e30


def dot(a, b):
    return jnp.dot(a, b, preferred_element_type=F32)


def dot_nt(a, b):
    return lax.dot_general(a, b, (((1,), (1,)), ((), ())), preferred_element_type=F32)


def dot_tn(a, b):
    return lax.dot_general(a, b, (((0,), (0,)), ((), ())), preferred_element_type=F32)


def lane_iota(rows):
    return lax.broadcasted_iota(jnp.int32, (rows, 128), 1)


def low_half(rows):
    return lane_iota(rows) < HEAD


def rope128(v, cs, sn):
    lane = lane_iota(v.shape[0])
    partner = jnp.where((lane & 63) < 32, pltpu.roll(v, 96, 1), pltpu.roll(v, 32, 1))
    return v * cs + partner * sn


def allowed_bias(seqr_ref, valr_ref, r0, nk):
    t = r0 + lax.broadcasted_iota(jnp.int32, (RB, nk), 0)
    u = lax.broadcasted_iota(jnp.int32, (RB, nk), 1)
    mine = jnp.broadcast_to(seqr_ref[:, r0 : r0 + RB].astype(F32), (128, RB)).T[:, :1]
    same = mine == seqr_ref[:, :nk].astype(F32)
    ok = (same & (u <= t) & (valr_ref[:, :nk] == 1)) | (u == t)
    return jnp.where(ok, 0.0, NEG).astype(F32)


def masked_heads(x, y):
    low = low_half(1).astype(F32)
    low_b, high_b = low.astype(BF16), (1.0 - low).astype(BF16)
    return jnp.concatenate([x * low_b, x * high_b, y * low_b], axis=0)


def pack_half(xi, a, b):
    low = low_half(a.shape[0])
    at, bt = a[:, 512:], b[:, 512:]
    if xi == 0:
        return a[:, :256], b[:, :256], jnp.where(low, at, pltpu.roll(bt, 64, 1))
    return a[:, 256:512], b[:, 256:512], jnp.where(low, pltpu.roll(at, 64, 1), bt)


def store_pair(idx, ref, rows, a, b):
    for xi in range(2):
        @pl.when(idx[0] == xi)
        def _():
            p, q, r = pack_half(xi, a, b)
            ref[rows, :256] = p.astype(ref.dtype)
            ref[rows, 256:512] = q.astype(ref.dtype)
            ref[rows, 512:] = r.astype(ref.dtype)


def store_one(idx, ref, rows, a):
    low = low_half(a.shape[0])
    at = a[:, 512:]
    for xi in range(2):
        @pl.when(idx[0] == xi)
        def _():
            ref[rows, :256] = a[:, xi * 256 : xi * 256 + 256].astype(ref.dtype)
            ref[rows, 256:] = jnp.where(low, at if xi == 0 else pltpu.roll(at, 64, 1), 0.0).astype(ref.dtype)


def ffn_back(dhid, gate, up, sig):
    return dhid * up * sig * (1.0 + gate * (1.0 - sig)), dhid * (gate * sig)


def put_wide(ref, v):
    d = v.shape[1]
    ref[:, :d] = v
    if ref.shape[1] > d:
        ref[:, d:] = jnp.zeros((ref.shape[0], ref.shape[1] - d), ref.dtype)


def half_rows(ref, which, n):
    return ref[pl.ds(pl.multiple_of(which * n, 8), n), :]


def split_send(idx, whole, keep, send):
    n = keep.shape[0]
    put_wide(keep, half_rows(whole, idx[1], n))
    put_wide(send, half_rows(whole, 1 - idx[1], n))


def take_sum(idx, pieces, out):
    d = out.shape[1]
    if len(pieces) == 1:
        out[...] = pieces[0][:, :d]
        return
    n = pieces[0].shape[0]
    out[pl.ds(pl.multiple_of(idx[1] * n, n), n), :] = pieces[0][:, :d]
    out[pl.ds(pl.multiple_of((1 - idx[1]) * n, n), n), :] = pieces[1][:, :d]


class Late:
    def __init__(self, source, buffer, sems, at, grouped):
        self.source, self.buffer, self.sems, self.at, self.grouped = source, buffer, sems, at, grouped
        self.waited = False

    def copy(self, g=None):
        if g is None:
            return pltpu.make_async_copy(self.source, self.buffer, self.sems.at[self.at])
        return pltpu.make_async_copy(self.source.at[g], self.buffer.at[g], self.sems.at[self.at + g])

    def start(self):
        self.copy().start()

    def wait(self):
        if not self.waited:
            self.copy().wait()
            self.waited = True
        return self.buffer


def ready(*refs):
    got = [r.wait() if isinstance(r, Late) else r for r in refs]
    return got if len(got) > 1 else got[0]


def ready_group(g, *refs):
    for r in refs:
        r.copy(g).wait()


def buffers(*refs):
    return [r.buffer for r in refs]


def fwd_kernel(second, split, part, groups, *refs):
    it = iter(refs)
    idx = next(it)
    x_ref = next(it)
    add_refs = [next(it) for _ in range(2 if split else 1)] if second else None
    win, wout, g1, g2, cs_ref, sn_ref, seqr, valr, wg, wu, wdt = (next(it) for _ in range(11))
    kt_old, vt_old, n2_old = (next(it) for _ in range(3)) if part else (None, None, None)
    part_old = next(it) if part and second else None
    cot = next(it) if second else None
    n1_ref, qk_ref, kt_ref, vt_ref, o_ref, lse_ref, h_ref, n2_ref, hidh_ref = (next(it) for _ in range(9))
    n2s_ref = next(it) if part else None
    x_out = next(it)
    if second:
        duh_ref, part_refs = next(it), [next(it) for _ in range(2 if part and split else 1)]
    else:
        gate_ref, up_ref = next(it), next(it)
    outs = [next(it) for _ in range(2 if split else 1)]
    acc, whole, ktf, vtf = (next(it) for _ in range(4))
    t = n1_ref.shape[0]
    base = part * t

    if second:
        take_sum(idx, add_refs, acc)
        x = x_ref[...] + acc[...]
        x_out[...] = x
    else:
        x = x_ref[:, base : base + t].astype(F32).T
        x_out[...] = x.astype(BF16)
    r1 = lax.rsqrt(jnp.mean(x * x, axis=1, keepdims=True) + EPS)
    n1_ref[...] = (x * r1 * g1[...]).astype(BF16)
    acc[...] = x
    flush(n1_ref)
    flush(x_out)
    lse_ref[...] = jnp.zeros_like(lse_ref)
    cs_ref, sn_ref = ready(cs_ref, sn_ref)
    win_l, wout_l = win, wout
    win, wout = buffers(win, wout)

    def group(g, carry):
        ready_group(g, win_l, wout_l)
        n1 = n1_ref[...]
        qk = dot_nt(n1, win[g, :256, :])
        v = dot_nt(n1, win[g, 256:320, :])
        cs, sn = cs_ref[base : base + t, :], sn_ref[base : base + t, :]
        xr = rope128(qk[:, :128], cs, sn)
        yr = rope128(qk[:, 128:], cs, sn)
        qk_ref[g, :, :128] = xr.astype(BF16)
        qk_ref[g, :, 128:] = yr.astype(BF16)
        kt = jnp.where(low_half(t), pltpu.roll(yr, 64, 1), yr).astype(BF16)
        vt = jnp.concatenate([v, v], axis=1).astype(BF16)
        kt_ref[g] = kt
        vt_ref[g] = vt
        if part:
            ktf[:base, :] = kt_old[g]
            vtf[:base, :] = vt_old[g]
        ktf[base : base + t, :] = kt
        vtf[base : base + t, :] = vt
        for rb in range(t // RB):
            r0 = rb * RB
            nk = base + r0 + RB
            rows = slice(r0, r0 + RB)
            q = masked_heads(qk_ref[g, rows, :128], qk_ref[g, rows, 128:])
            s = dot_nt(q, ktf[:nk, :])
            bias = allowed_bias(seqr, valr, base + r0, nk)
            es, ms, lls = [], [], []
            for r in range(0, 3 * RB, TR):
                st = s[r : r + TR] * 0.125 + bias[r % RB : r % RB + TR]
                mt = jnp.max(st, axis=1, keepdims=True)
                et = jnp.exp(st - mt)
                ms.append(mt)
                lls.append(jnp.sum(et, axis=1, keepdims=True))
                es.append(et.astype(BF16))
            m, l = jnp.concatenate(ms, axis=0), jnp.concatenate(lls, axis=0)
            o = dot(jnp.concatenate(es, axis=0), vtf[:nk, :]) / l
            low = low_half(RB)
            o_ref[g, rows, :128] = jnp.where(low, o[:RB], o[RB : 2 * RB]).astype(BF16)
            o_ref[g, rows, 128:] = jnp.where(low, o[2 * RB :], 0.0).astype(BF16)
            ls = m + jnp.log(l)
            lane = lane_iota(RB)
            cur = lse_ref[rows, :]
            for j in range(3):
                cur = jnp.where(lane == g * 3 + j, ls[j * RB : (j + 1) * RB], cur)
            lse_ref[rows, :] = cur
        acc[...] += dot(o_ref[g, :, :192], wout[g])
        return carry

    lax.fori_loop(0, groups, group, 0)
    for ref in (qk_ref, kt_ref, vt_ref, o_ref, lse_ref):
        flush(ref)
    h = acc[...]
    h_ref[...] = h
    flush(h_ref)
    r2 = lax.rsqrt(jnp.mean(h * h, axis=1, keepdims=True) + EPS)
    n2 = (h * r2 * g2[...]).astype(BF16)
    n2_ref[...] = n2
    flush(n2_ref)
    if part:
        n2_old = ready(n2_old)
        if split:
            for c in range(2):
                @pl.when(idx[1] == c)
                def _():
                    put_wide(n2s_ref, (n2_old if c == 0 else n2_ref)[...].astype(F32))
        else:
            put_wide(n2s_ref.at[:t, :], n2_old[...].astype(F32))
            put_wide(n2s_ref.at[t:, :], n2_ref[...].astype(F32))
    if part:
        flush(n2s_ref)
    wg, wu, wdt = ready(wg, wu, wdt)
    every = slice(0, t)
    gate = dot(n2, wg[...])
    up = dot(n2, wu[...])
    sig = jax.nn.sigmoid(gate)
    hid = gate * sig * up
    store_one(idx, hidh_ref, every, hid)
    flush(hidh_ref)
    if second:
        cot = ready(cot)
        if part and split:
            part_old = ready(part_old)
            half = t // 2
            whole[...] = dot_nt(hid.astype(BF16), wdt[...])
            for ref, which in zip(part_refs, (idx[1], 1 - idx[1])):
                put_wide(ref.at[:half, :], half_rows(part_old, which, half))
                put_wide(ref.at[half:, :], half_rows(whole, which, half))
                flush(ref)
        elif part:
            part_old = ready(part_old)
            put_wide(part_refs[0].at[:t, :], part_old[...])
            put_wide(part_refs[0].at[t:, :], dot_nt(hid.astype(BF16), wdt[...]))
        else:
            part_refs[0][...] = dot_nt(hid.astype(BF16), wdt[...])
            flush(part_refs[0])
        dgate, dup = ffn_back(dot(cot[base : base + t, :], wdt[...]), gate, up, sig)
        store_pair(idx, duh_ref, every, dgate, dup)
        flush(duh_ref)
        whole[...] = dot_nt(dgate.astype(BF16), wg[...]) + dot_nt(dup.astype(BF16), wu[...])
    else:
        gate_ref[...] = gate
        up_ref[...] = up
        flush(gate_ref)
        flush(up_ref)
        whole[...] = dot_nt(hid.astype(BF16), wdt[...])
    if split:
        split_send(idx, whole, *outs)
    else:
        put_wide(outs[0], whole[...])


def norm_back(dn, stream, gain):
    r = lax.rsqrt(jnp.mean(stream * stream, axis=1, keepdims=True) + EPS)
    m = stream * r
    dgain = jnp.sum(dn * m, axis=0, keepdims=True)
    dm = dn * gain
    return r * (dm - m * jnp.mean(dm * m, axis=1, keepdims=True)), dgain


def bwd_enter(idx, dn2_refs, dz_ref, h_ref, g2, dh_ref, da_ref, dg2_ref):
    take_sum(idx, dn2_refs, dh_ref)
    dh, dg2 = norm_back(dh_ref[...], h_ref[...], g2[...])
    dh = dz_ref[...].astype(F32) + dh
    dh_ref[...] = dh
    da_ref[...] = dh.astype(BF16)
    dg2_ref[...] = dg2


def bwd_block(g, r0, base, da, qk_ref, o_ref, lse_ref, ktf, vtf, wout, seqr, valr, dkv):
    low, lane = low_half(RB), lane_iota(RB)
    nk = base + r0 + RB
    rows = slice(r0, r0 + RB)
    do = dot_nt(da[rows], wout[g])
    dox = do[:, :128].astype(BF16)
    doy = jnp.concatenate([do[:, 128:192], jnp.zeros((RB, 64), F32)], axis=1).astype(BF16)
    px = dox.astype(F32) * o_ref[g, rows, :128].astype(F32)
    py = doy.astype(F32) * o_ref[g, rows, 128:].astype(F32)
    delta = jnp.concatenate(
        [
            jnp.sum(jnp.where(low, px, 0.0), axis=1, keepdims=True),
            jnp.sum(jnp.where(low, 0.0, px), axis=1, keepdims=True),
            jnp.sum(py, axis=1, keepdims=True),
        ],
        axis=0,
    )
    ls = lse_ref[rows, :]
    lse = jnp.concatenate(
        [jnp.sum(jnp.where(lane == g * 3 + j, ls, 0.0), axis=1, keepdims=True) for j in range(3)], axis=0
    )
    q = masked_heads(qk_ref[g, rows, :128], qk_ref[g, rows, 128:])
    dos = masked_heads(dox, doy)
    kt = ktf(nk)
    s = dot_nt(q, kt)
    dp = dot_nt(dos, vtf(nk))
    bias = allowed_bias(seqr, valr, base + r0, nk)
    ps, dss = [], []
    for r in range(0, 3 * RB, TR):
        part = slice(r, r + TR)
        pt = jnp.exp(s[part] * 0.125 + bias[r % RB : r % RB + TR] - lse[part])
        ps.append(pt.astype(BF16))
        dss.append((pt * (dp[part] - delta[part])).astype(BF16))
    p, ds = jnp.concatenate(ps, axis=0), jnp.concatenate(dss, axis=0)
    dq = dot(ds, kt) * 0.125
    dkv[0, :nk, :] += dot_tn(ds, q)
    dkv[1, :nk, :] += dot_tn(p, dos)
    return jnp.where(low, dq[:RB], dq[RB : 2 * RB]), dq[2 * RB :]


def bwd_a_kernel(split, groups, *refs):
    it = iter(refs)
    idx = next(it)
    dn2_refs = [next(it) for _ in range(2 if split else 1)]
    dz_ref, h_ref, qk_ref, kt_ref, vt_ref, o_ref, lse_ref, wout, g2, cs_ref, sn_ref, seqr, valr = (
        next(it) for _ in range(13))
    dh_ref, da_ref, dqx_ref, dqy_ref, dkv_ref, dg2_ref = (next(it) for _ in range(6))
    t = dh_ref.shape[0]
    bwd_enter(idx, dn2_refs, dz_ref, h_ref, g2, dh_ref, da_ref, dg2_ref)
    flush(dh_ref)
    flush(da_ref)
    dkv_ref[...] = jnp.zeros_like(dkv_ref)
    lse_ref, cs_ref, sn_ref = ready(lse_ref, cs_ref, sn_ref)
    waits = (qk_ref, kt_ref, vt_ref, o_ref, wout)
    qk_ref, kt_ref, vt_ref, o_ref, wout = buffers(*waits)

    def group(g, carry):
        ready_group(g, *waits)
        da = da_ref[...]
        for r0 in range(0, t, RB):
            rows = slice(r0, r0 + RB)
            dqx, dqy = bwd_block(g, r0, 0, da, qk_ref, o_ref, lse_ref, lambda n: kt_ref[g, :n, :],
                                 lambda n: vt_ref[g, :n, :], wout, seqr, valr, dkv_ref.at[g])
            dqx_ref[g, rows, :] = rope128(dqx, cs_ref[rows, :], -sn_ref[rows, :]).astype(BF16)
            dqy_ref[g, rows, :] = dqy
        return carry

    lax.fori_loop(0, groups, group, 0)


def bwd_b_kernel(last, split, groups, *refs):
    it = iter(refs)
    idx = next(it)
    dn2_refs = [next(it) for _ in range(2 if split else 1)]
    (dz_ref, h_ref, qk_ref, kt_ref, vt_ref, o_ref, lse_ref, xa_ref, xb_ref, kt_old, vt_old, dha_ref, dqxa_ref, dqya_ref,
     dkva_ref, win, wout, g1, g2, cs_ref, sn_ref, seqr, valr) = (next(it) for _ in range(23))
    da_ref, dpa_ref, dpb_ref, dg1_ref, dg2_ref, dxa_ref = (next(it) for _ in range(6))
    dxb_ref = None if last else next(it)
    dfs_ref = None if last else next(it)
    dh_ref, acca, accb, dkv, ktf, vtf, dqy_ref = (next(it) for _ in range(7))
    t = dh_ref.shape[0]
    bwd_enter(idx, dn2_refs, dz_ref, h_ref, g2, dh_ref, da_ref, dg2_ref)
    acca[...] = jnp.zeros_like(acca)
    flush(da_ref)
    accb[...] = jnp.zeros_like(accb)
    lse_ref, cs_ref, sn_ref = ready(lse_ref, cs_ref, sn_ref)
    waits = (qk_ref, kt_ref, vt_ref, o_ref, kt_old, vt_old, dqxa_ref, dqya_ref, dkva_ref, win, wout)
    qk_ref, kt_ref, vt_ref, o_ref, kt_old, vt_old, dqxa_ref, dqya_ref, dkva_ref, win, wout = buffers(*waits)

    def group(g, carry):
        ready_group(g, *waits)
        da = da_ref[...]
        ktf[:t, :] = kt_old[g]
        ktf[t:, :] = kt_ref[g]
        vtf[:t, :] = vt_old[g]
        vtf[t:, :] = vt_ref[g]
        dkv[:, :t, :] = dkva_ref[g]
        dkv[:, t:, :] = jnp.zeros((2, t, 128), F32)
        for r0 in range(0, t, RB):
            rows = slice(r0, r0 + RB)
            dqx, dqy = bwd_block(g, r0, t, da, qk_ref, o_ref, lse_ref, lambda n: ktf[:n, :], lambda n: vtf[:n, :],
                                 wout, seqr, valr, dkv)
            full = slice(t + r0, t + r0 + RB)
            dpb_ref[g, rows, :128] = rope128(dqx, cs_ref[full, :], -sn_ref[full, :]).astype(BF16)
            dqy_ref[rows, :] = dqy
        dpa_ref[g, :, :128] = dqxa_ref[g]
        low = low_half(t)
        for k, (ref, dqy) in enumerate(((dpa_ref, dqya_ref[g]), (dpb_ref, dqy_ref[...]))):
            rows = slice(k * t, k * t + t)
            dk, dv = dkv[0, rows, :], dkv[1, rows, :]
            dk = (dk + pltpu.roll(dk, 64, 1)) * 0.125
            dv = dv + pltpu.roll(dv, 64, 1)
            dy = jnp.where(low, dqy, dk)
            ref[g, :, 128:256] = rope128(dy, cs_ref[rows, :], -sn_ref[rows, :]).astype(BF16)
            ref[g, :, 256:320] = dv[:, :64].astype(BF16)
        acca[...] += dot(dpa_ref[g], win[g])
        accb[...] += dot(dpb_ref[g], win[g])
        return carry

    lax.fori_loop(0, groups, group, 0)
    flush(dpa_ref)
    flush(dpb_ref)
    xa_ref, xb_ref, dha_ref = ready(xa_ref, xb_ref, dha_ref)
    dxa, dg1a = norm_back(acca[...], xa_ref[...].astype(F32), g1[...])
    dxb, dg1b = norm_back(accb[...], xb_ref[...].astype(F32), g1[...])
    dg1_ref[...] = dg1a + dg1b
    if last:
        dxa_ref[:, :t] = (dxa + dha_ref[...]).T.astype(BF16)
        dxa_ref[:, t:] = (dxb + dh_ref[...]).T.astype(BF16)
    else:
        dxa_ref[...] = dxa + dha_ref[...]
        dxb_ref[...] = dxb + dh_ref[...]
        flush(dxa_ref)
        flush(dxb_ref)
    if not last:
        if split:
            for c in range(2):
                @pl.when(idx[1] == c)
                def _():
                    put_wide(dfs_ref, (dxa_ref if c == 0 else dxb_ref)[...].astype(BF16).astype(F32))
        else:
            put_wide(dfs_ref.at[:t, :], dxa_ref[...].astype(BF16).astype(F32))
            put_wide(dfs_ref.at[t:, :], dxb_ref[...].astype(BF16).astype(F32))


def ffn_back_kernel(split, *refs):
    idx, dza, dzb, gatea, gateb, upa, upb, wg, wu, wdt, duha, duhb, dfa, dfb, *rest = refs
    outs, whole = rest[:-1], rest[-1]
    per = len(outs) // 2
    for k, (dz_ref, gate_ref, up_ref, duh_ref, df_ref) in enumerate(
            ((dza, gatea, upa, duha, dfa), (dzb, gateb, upb, duhb, dfb))):
        df = ready(dz_ref)[...].astype(BF16)
        df_ref[...] = df
        flush(df_ref)
        wdt, gate_ref, up_ref = ready(wdt, gate_ref, up_ref)
        gate, up = gate_ref[...], up_ref[...]
        dgate, dup = ffn_back(dot(df, wdt[...]), gate, up, jax.nn.sigmoid(gate))
        store_pair(idx, duh_ref, slice(0, df.shape[0]), dgate, dup)
        flush(duh_ref)
        wg, wu = ready(wg, wu)
        whole[...] = dot_nt(dgate.astype(BF16), wg[...]) + dot_nt(dup.astype(BF16), wu[...])
        if split:
            split_send(idx, whole, *outs[per * k : per * k + per])
        else:
            put_wide(outs[k], whole[...])
        for ref in outs[per * k : per * k + per]:
            flush(ref)


def own_grads(n2, duh, hidh, df, base, put):
    for r in range(0, n2[0].shape[1], 320):
        put(0, r, sum((dot_tn(a[:, r : r + 320], b[...]) for a, b in zip(n2, duh)), base(0, r)))
        put(1, r, sum((dot_tn(a[:, r : r + 320], b[...]) for a, b in zip(df, hidh)), base(1, r)))


def peer_acts(n2, df, wgu, wdh, du, hd, rows):
    gu = dot(n2, wgu[...])
    dh = dot(df, wdh[...])
    ga, ua, tile = gu[:, :256], gu[:, 256:512], gu[:, 512:]
    turned = pltpu.roll(tile, 64, 1)
    sa, sb = jax.nn.sigmoid(ga), jax.nn.sigmoid(tile)
    low = low_half(n2.shape[0])
    hd[rows, :256] = (ga * sa * ua).astype(BF16)
    hd[rows, 256:] = jnp.where(low, tile * sb * turned, 0.0).astype(BF16)
    dga, dua = ffn_back(dh[:, :256], ga, ua, sa)
    dgb, dub = ffn_back(dh[:, 256:], tile, turned, sb)
    du[rows, :256] = dga.astype(BF16)
    du[rows, 256:512] = dua.astype(BF16)
    du[rows, 512:] = jnp.where(low, dgb, pltpu.roll(dub, 64, 1)).astype(BF16)


def peer_grads(n2p, dfp, wgu, wdh, scratch, base, put):
    n2, df, du, hd = scratch
    d = n2.shape[1]
    n = n2p[0].shape[0]
    for i in range(len(n2p)):
        rows = slice(i * n, i * n + n)
        n2[rows, :] = n2p[i][:, :d].astype(BF16)
        df[rows, :] = dfp[i][:, :d].astype(BF16)
        for r in range(i * n, i * n + n, 256):
            part = slice(r, r + 256)
            peer_acts(n2[part, :], df[part, :], wgu, wdh, du, hd, part)
    own_grads([n2], [du], [hd], [df], base, put)


def own_grads_kernel(*refs):
    n2, duh, hidh, cot, outs = refs[:2], refs[2:4], refs[4:6], refs[6], refs[7:]
    t = n2[0].shape[0]

    def put(k, r, v):
        outs[k][r : r + 320, :] = v
        flush(outs[k], slice(r, r + 320))

    own_grads(n2, duh, hidh, [cot.at[:t, :], cot.at[t:, :]], lambda k, r: 0.0, put)


def both_grads_kernel(count, *refs):
    n2p, dfp = refs[:count], refs[count : 2 * count]
    wgu, wdh, *rest = refs[2 * count :]
    n2, duh, hidh, df = (rest[2 * k : 2 * k + 2] for k in range(4))
    old, outs, scratch = rest[8:10], rest[10:12], rest[12:]

    def put(k, r, v):
        outs[k][r : r + 320, :] = v

    def put_last(k, r, v):
        outs[k][r : r + 320, :] = v
        flush(outs[k], slice(r, r + 320))

    old = ready(*old)
    own_grads(n2, duh, hidh, df, lambda k, r: old[k][r : r + 320, :], put)
    n2p, dfp = [ready(r) for r in n2p], [ready(r) for r in dfp]
    wgu, wdh = ready(wgu, wdh)
    peer_grads(n2p, dfp, wgu, wdh, scratch, lambda k, r: outs[k][r : r + 320, :], put_last)


def last_grads_kernel(count, n_chunks, *refs):
    n2p, dfp = refs[:count], refs[count : 2 * count]
    wgu, wdh, *rest = refs[2 * count :]
    old, chunks, scratch = rest[:2], rest[2 : 2 + n_chunks], rest[2 + n_chunks : 6 + n_chunks]
    gu, dn = rest[6 + n_chunks :]

    def put(k, r, v):
        (gu, dn)[k][r : r + 320, :] = v

    peer_grads(n2p, dfp, wgu, wdh, scratch, lambda k, r: ready(old[k])[r : r + 320, :], put)
    at = 0
    half = dn.shape[0] // 2
    for out in chunks:
        n = out.shape[0]
        if at < gu.shape[0]:
            out[...] = gu[at : at + n, :]
        else:
            r = at - gu.shape[0]
            a, b = dn[r : r + n, :], dn[half + r : half + r + n, :]
            out[:, :256] = a[:, :256]
            out[:, 256:512] = b[:, :256]
            out[:, 512:] = jnp.where(low_half(n), a[:, 256:], pltpu.roll(b[:, 256:], 64, 1))
        flush(out)
        at += n


def unpack_kernel(count, stacked, *refs):
    idx = refs[0]
    own, other, outs = refs[1 : 1 + count], refs[1 + count : 1 + 2 * count], refs[1 + 2 * count :]
    at = 0
    for o, p in zip(own, other):
        o, p = ready(o, p)
        n = o.shape[0]
        for xi in range(2):
            @pl.when(idx[0] == xi)
            def _():
                a, b = (o, p) if xi == 0 else (p, o)
                low = low_half(n)
                at4, bt4 = a[:, 512:], b[:, 512:]
                firsts = jnp.where(low, at4, pltpu.roll(bt4, 64, 1))
                seconds = jnp.where(low, pltpu.roll(at4, 64, 1), bt4)
                for k, tile in ((0, firsts), (1, seconds)):
                    ref = outs[0] if stacked else outs[k]
                    r = at + (k * (ref.shape[0] // 2) if stacked else 0)
                    ref[r : r + n, :256] = a[:, 256 * k : 256 * k + 256]
                    ref[r : r + n, 256:512] = b[:, 256 * k : 256 * k + 256]
                    ref[r : r + n, 512:] = tile
        for k in range(2):
            ref = outs[0] if stacked else outs[k]
            r = at + (k * (ref.shape[0] // 2) if stacked else 0)
            flush(ref, slice(r, r + n))
        at += n


def attn_grad_kernel(idx, *refs):
    n1, dp, o, da = (refs[4 * k : 4 * k + 4] for k in range(4))
    gains, keep2, keep0, keep1, send, whole, extra = refs[16:]

    def grads(g, out, at):
        out[at : at + 320, :] = sum(dot_tn(p[g], n[...]) for p, n in zip(dp, n1))
        out[at + 320 : at + 512, :] = sum(dot_tn(v[g, :, :192], a[...]) for v, a in zip(o, da))

    grads(idx[2], whole, 0)
    half = whole.shape[0] // 2
    lead = send.shape[0] - half
    for k, ref in enumerate((keep0, keep1)):
        put_wide(ref, whole[pl.ds(pl.multiple_of(idx[0] * half + k * (half // 2), 8), half // 2), :])
    put_wide(send.at[lead:, :], half_rows(whole, 1 - idx[0], half))
    grads(idx[3], whole, 0)
    rows_in, rows_out = 320 // idx_parts(extra), 192 // idx_parts(extra)
    extra[:rows_in, :] = whole[pl.ds(pl.multiple_of(idx[4] * rows_in, 8), rows_in), :]
    extra[rows_in : rows_in + rows_out, :] = whole[pl.ds(pl.multiple_of(320 + idx[4] * rows_out, 8), rows_out), :]
    n = rows_in + rows_out
    extra[n:, :] = jnp.zeros((extra.shape[0] - n, extra.shape[1]), F32)
    extra[n : n + 2, :] = gains[...]
    half = extra.shape[0] // 2
    put_wide(keep2, half_rows(extra, idx[0], half))
    put_wide(send.at[:lead, :], half_rows(extra, 1 - idx[0], half))


def out_kernel(idx, ha, hb, *refs):
    pieces, out, whole = refs[:-2], refs[-2], refs[-1]
    t, d = ha.shape
    half = t // len(pieces)
    for k, h in enumerate((ha, hb)):
        if len(pieces) == 1:
            whole[...] = pieces[0][k * t : k * t + t, :d]
        else:
            rows = slice(k * half, k * half + half)
            whole[pl.ds(pl.multiple_of(idx[1] * half, half), half), :] = pieces[0][rows, :d]
            whole[pl.ds(pl.multiple_of((1 - idx[1]) * half, half), half), :] = pieces[1][rows, :d]
        out[:, k * t : k * t + t] = (whole[...] + h[...]).T.astype(BF16)


def attn_finish_kernel(parts, idx, a0, a1, b0, b1, *rest):
    slot1, gin, gout = rest[:-2], *rest[-2:]
    d = gin.shape[2]
    for xi in range(2):
        @pl.when(idx[0] == xi)
        def _():
            p0, p1, q0, q1 = (a0, a1, b0, b1) if xi == 0 else (b0, b1, a0, a1)
            gin[0, :128, :] = p0[:, :d]
            gin[0, 128:256, :] = p1[:, :d]
            gin[0, 256:, :] = q0[:64, :d]
            gout[0, :64, :] = q0[64:, :d]
            gout[0, 64:, :] = q1[:, :d]
    mine = idx[5].astype(F32)
    rows_in, rows_out = 320 // parts, 192 // parts
    for k, quarter in enumerate(slot1):
        m = (idx[4] // 2 * (1 - k % 2) + (1 - idx[4] // 2) * (k % 2)) * 2 + (
            idx[4] % 2 * (1 - k // 2) + (1 - idx[4] % 2) * (k // 2))
        gin[1, pl.ds(pl.multiple_of(m * rows_in, 8), rows_in), :] = quarter[:rows_in, :d] * mine
        gout[1, pl.ds(pl.multiple_of(m * rows_out, 8), rows_out), :] = (
            quarter[rows_in : rows_in + rows_out, :d] * mine)


def idx_parts(extra):
    return 512 // (extra.shape[0] - 16)


BIG = 32 * 1024
OUT = {}


def flush(ref, rows=None):
    out, sem, whole = OUT[id(ref)]
    part = ref if rows is None else ref.at[rows, :]
    to = out if rows is None else out.at[rows, :]
    pltpu.make_async_copy(part, to, sem).start()
    OUT[id(ref)] = (out, sem, True)


def size(a):
    return math.prod(a.shape) * jnp.dtype(a.dtype).itemsize


def call(kernel, outs, ins, scratch=(), smem=0, flops=0, late=(), grouped=(), first=()):
    n_in, n_out = len(ins), len(outs)
    big_in = [i for i in range(smem, n_in) if size(ins[i]) >= BIG]
    big_out = [i for i in range(n_out) if size(outs[i]) >= BIG]
    in_specs = [
        pl.BlockSpec(memory_space=pltpu.SMEM if i < smem else pl.ANY if i in big_in else pltpu.VMEM) for i in range(n_in)
    ]
    out_specs = [pl.BlockSpec(memory_space=pl.ANY if i in big_out else pltpu.VMEM) for i in range(n_out)]
    buffers = [pltpu.VMEM(ins[i].shape, ins[i].dtype) for i in big_in]
    buffers += [pltpu.VMEM(outs[i].shape, outs[i].dtype) for i in big_out]
    at, n_sems = {}, 0
    for i in big_in:
        at[i] = n_sems
        n_sems += ins[i].shape[0] if i in grouped else 1
    out_at = n_sems
    sems = pltpu.SemaphoreType.DMA((n_sems + len(big_out),))

    def body(*refs):
        ins_, outs_, rest = list(refs[:n_in]), list(refs[n_in : n_in + n_out]), list(refs[n_in + n_out :])
        own, (bufs, sem) = rest[: len(scratch)], (rest[len(scratch) : -1], rest[-1])
        kept = []
        for k, i in enumerate(big_in):
            kept.append((i, Late(ins_[i], bufs[k], sem, at[i], i in grouped)))
        items = dict(kept)
        for i in big_in:
            if i not in late and i not in grouped:
                items[i].start()
        for i in first:
            items[i].start()
        for g in range(max((ins[i].shape[0] for i in grouped), default=0)):
            for i in grouped:
                items[i].copy(g).start()
        for i in late:
            if i in items and i not in first:
                items[i].start()
        for i, item in kept:
            early = i not in late and i not in grouped
            ins_[i] = item.wait() if early else item
        OUT.clear()
        for k, i in enumerate(big_out):
            buf = bufs[len(big_in) + k]
            OUT[id(buf)] = (outs_[i], sem.at[out_at + k], False)
            outs_[i] = buf
        kernel(*ins_, *outs_, *own)
        for i in big_out:
            if not OUT[id(outs_[i])][2]:
                flush(outs_[i])
        for i, item in kept:
            assert item.grouped or item.waited
        for i in big_out:
            out, s, _ = OUT[id(outs_[i])]
            pltpu.make_async_copy(outs_[i], out, s).wait()
        OUT.clear()

    return pl.pallas_call(
        body,
        out_shape=tuple(outs),
        in_specs=in_specs,
        out_specs=tuple(out_specs),
        scratch_shapes=list(scratch) + buffers + [sems],
        compiler_params=pltpu.CompilerParams(vmem_limit_bytes=VMEM * 1024 * 1024),
        cost_estimate=pl.CostEstimate(flops=1, bytes_accessed=1, transcendentals=0),
    )(*ins)


def S(shape, dtype):
    return jax.ShapeDtypeStruct(shape, dtype)


def add_kernel(a, b, out):
    out[...] = a[...] + b[...]


def pick_kernel(flag, a, b, out):
    @pl.when(flag[0] == 1)
    def _():
        out[...] = a[...]

    @pl.when(flag[0] != 1)
    def _():
        out[...] = b[...]


def small_call(kernel, ins, smem=0):
    a = ins[-1]
    return pl.pallas_call(
        kernel,
        out_shape=jax.ShapeDtypeStruct(a.shape, a.dtype),
        in_specs=[pl.BlockSpec(memory_space=pltpu.SMEM)] * smem + [pl.BlockSpec(memory_space=pltpu.VMEM)] * 2,
        out_specs=pl.BlockSpec(memory_space=pltpu.VMEM),
        compiler_params=pltpu.CompilerParams(vmem_limit_bytes=8 * 2**20),
        cost_estimate=pl.CostEstimate(flops=1, bytes_accessed=1, transcendentals=0),
    )(*ins)


def add(a, b):
    return small_call(add_kernel, [a, b])


def add_pieces(keeps, got):
    def kernel(*refs):
        n = len(keeps)
        at = 0
        for keep, out in zip(refs[:n], refs[n + 1 :]):
            out[...] = keep[...] + refs[n][at : at + keep.shape[0], :]
            at += keep.shape[0]

    return pl.pallas_call(
        kernel,
        out_shape=tuple(jax.ShapeDtypeStruct(k.shape, k.dtype) for k in keeps),
        compiler_params=pltpu.CompilerParams(vmem_limit_bytes=12 * 2**20),
        cost_estimate=pl.CostEstimate(flops=1, bytes_accessed=1, transcendentals=0),
    )(*keeps, got)


class Links:
    def __init__(self, mesh):
        self.wide, self.narrow = mesh.shape["wide"], mesh.shape["narrow"]
        self.known = (self.wide, self.narrow) == (8, 4)

    def permute(self, v, step):
        pairs = []
        for w in range(self.wide):
            for n in range(self.narrow):
                to = step(w // 2, w % 2, n // 2, n % 2)
                if to is not None:
                    z, x, y, c = to
                    pairs.append((w * self.narrow + n, (z * 2 + x) * self.narrow + y * 2 + c))
        return lax.ppermute(v, ("wide", "narrow"), pairs)

    def core(self, v):
        return self.permute(v, lambda z, x, y, c: (z, x, y, 1 - c))

    def y(self, v):
        return self.permute(v, lambda z, x, y, c: (z, x, 1 - y, c))

    def x(self, v):
        return self.permute(v, lambda z, x, y, c: (z, 1 - x, y, c))

    def inward(self, v):
        return self.permute(v, lambda z, x, y, c: ({0: 1, 3: 2}[z], x, y, c) if z in (0, 3) else None)

    def outward(self, v):
        return self.permute(v, lambda z, x, y, c: ({1: 0, 2: 3}[z], x, y, c) if z in (1, 2) else None)

    def middle(self, v):
        return self.permute(v, lambda z, x, y, c: (3 - z, x, y, c) if z in (1, 2) else None)

    def sum_cores(self, pieces):
        return add(pieces[0], self.core(pieces[1])) if self.known else pieces[0]

    def y_start(self, r):
        return self.y(r) if self.known else r

    def sum_chips(self, r, got):
        if not self.known:
            return [lax.psum(r, "narrow")]
        r = add(r, got)
        return [r, self.core(r)]

    def both_cores(self, got):
        return [got, self.core(got)] if self.known else [got]

    def sum_lines(self, chunks, jobs, pieces, finish, hooks):
        last = chunks[0]
        if not self.known:
            for job in jobs:
                last = job(last)
            *keeps, send = last
            n = len(chunks) + len(keeps)
            got = self.x(send)
            pairs, at = [], 0
            for keep in keeps:
                pairs.append((keep, at))
                at += keep.shape[0]
            vals, theirs, results = list(chunks) + [None] * len(pairs), [None] * n, {}
            groups = [list(range(k, self.wide, 2)) for k in range(2)]
            for i, (keep, at) in enumerate(pairs):
                vals[len(chunks) + i] = keep + got[at : at + keep.shape[0]]
            vals = [lax.psum(r, "wide", axis_index_groups=groups) for r in vals]
            theirs = [self.x(r) for r in vals]
            for c, hook in hooks.items():
                results[c] = hook(vals, theirs)
            results[None] = finish([lax.psum(pieces[0], "narrow")])
            return vals, theirs, results
        z = lax.axis_index("wide") // 2
        inner = ((z == 1) | (z == 2)).astype(jnp.int32).reshape(1)
        n_keep = 3
        n = len(chunks) + n_keep
        order = [*range(POS_A), len(chunks), *range(POS_A, len(chunks)), *range(len(chunks) + 1, n)]
        moved = [None] * n
        for c in order[:U_AHEAD]:
            moved[c] = self.inward(chunks[c])
        vals, theirs, results = list(chunks) + [None] * n_keep, [None] * n, {}
        tr = self.core(pieces[1])
        for s in range(n + LAGS[3]):
            if s == OUT_SLOTS[0]:
                tr = last = add(pieces[0], after(tr, last))
                ty = self.y(tr)
            if s == OUT_SLOTS[1]:
                tr = last = add(tr, after(ty, last))
                tc = self.core(tr)
            if s == OUT_SLOTS[2]:
                results[None] = finish([tr, after(tc, last)])
                last = results[None][0]
            if s in J_SLOTS:
                made = jobs[J_SLOTS.index(s)](last)
                last = made[0]
            if s == J_SLOTS[2]:
                *keeps, send = made
                got = self.x(send)
            if s == R_SLOT:
                got = after(got, last)
                sums = add_pieces(keeps, got)
                last = sums[0]
                for i, v in enumerate(sums):
                    vals[len(chunks) + i] = v
            for stage in range(4):
                c = s - LAGS[stage]
                if not 0 <= c < n:
                    continue
                c = order[c]
                if stage == 3:
                    theirs[c] = last = after(theirs[c], last)
                    if c in hooks:
                        results[c] = hooks[c](vals, theirs)
                        last = results[c][0]
                    continue
                new = after(moved[c], last)
                vals[c] = small_call(pick_kernel, [inner, vals[c], new], 1) if stage == 2 else add(vals[c], new)
                last = vals[c]
                if stage == 0:
                    moved[c] = self.middle(vals[c])
                    if s + U_AHEAD < n:
                        p = order[s + U_AHEAD]
                        moved[p] = self.inward(after(vals[p], last))
                elif stage == 1:
                    moved[c] = self.outward(vals[c])
                else:
                    theirs[c] = self.x(vals[c])
        return vals, theirs, results

    def gather_narrow(self, v):
        o = self.permute(v, lambda z, x, y, c: (z, x, 1 - y, c))
        p = self.permute(v, lambda z, x, y, c: (z, x, y, 1 - c))
        return [v, o, p, self.permute(o, lambda z, x, y, c: (z, x, y, 1 - c))]


def tie(*groups):
    return lax.optimization_barrier(groups)


def after(v, *deps):
    return lax.optimization_barrier((v, *deps))[0]


LAGS = (0, 1, 2, 5)
POS_A = 6
R_SLOT = 4
U_AHEAD = 2
J_SLOTS = (0, 1, 2)
OUT_SLOTS = (2, 5, 7)
CHUNKS = (240, 240, 240, 240, 240, 240)


def per_device(links, tokens, attn_in, attn_out, gate_weight, up_weight, down_weight, attn_gain, ffn_gain,
               cotangent, seq_ids, positions, valid_mask, group_owner):
    t, d = tokens.shape
    groups = attn_in.shape[0]
    f = gate_weight.shape[1]
    split = links.known
    member = lax.axis_index("narrow")
    xi = lax.axis_index("wide") % 2
    core = member % 2
    idx = jnp.stack([xi, core]).astype(jnp.int32)
    lane = jnp.arange(128, dtype=jnp.int32)
    half = HEAD // 2
    freq = THETA ** (-(lane % half).astype(F32) / half)
    angles = positions.astype(F32)[:, None] * freq[None, :]
    cs = jnp.cos(angles)
    sn = jnp.sin(angles) * jnp.where(lane % HEAD < half, -1.0, 1.0).astype(F32)[None, :]
    seqr, valr = seq_ids.reshape(1, t), valid_mask.reshape(1, t)
    g1, g2 = attn_gain.reshape(1, d), ffn_gain.reshape(1, d)
    win_t = jnp.swapaxes(attn_in, 1, 2)
    wd_t = down_weight.T

    def x_half(w):
        return lax.dynamic_slice_in_dim(w, xi * 256, 256, 1), lax.dynamic_slice_in_dim(w, 512 + xi * 64, 64, 1)

    (ga, gb), (ua, ub), (wa, wb) = x_half(gate_weight), x_half(up_weight), x_half(wd_t)
    wgu = jnp.concatenate([ga, ua, gb, ub], axis=1)
    wdh = jnp.concatenate([wa, wb, jnp.zeros((d, 64), BF16)], axis=1)

    th = t // 2
    sent = th if split else t
    wd = -(-d // 128) * 128
    piece = S((sent, wd), F32)
    sums = [S((th // 2, wd), F32)] * 2 if split else [S((th, wd), F32)]
    n_sums = len(sums)
    saved = [S((th, d), BF16), S((groups, th, 256), BF16), S((groups, th, 128), BF16), S((groups, th, 128), BF16),
             S((groups, th, 256), BF16), S((th, 128), F32), S((th, d), F32), S((th, d), BF16), S((th, 384), BF16)]
    scratch = [pltpu.VMEM((th, d), F32)] * 2 + [pltpu.VMEM((t, 128), BF16)] * 2
    weights = [win_t, attn_out, g1, g2, cs, sn, seqr, valr]
    ffn_w = [gate_weight, up_weight, wd_t]

    def forward(second, x, adds, old):
        part = old is not None
        outs = list(saved) + ([piece] if part else [])
        outs += [S((th, d), F32), S((th, f), BF16)] + ([piece] * n_sums if part else [S((th, d), F32)]) if second else [S((th, d), BF16)] + [S((th, f), F32)] * 2
        ins = [idx, x, *adds] + weights + ffn_w
        at = 2 + len(adds)
        ins += [old[2], old[3], old[7]] if part else []
        ins += [old[9]] if part and second else []
        ins += [cotangent] if second else []
        res = call(functools.partial(fwd_kernel, second, split, int(part), groups), outs + sums, ins, scratch, smem=1,
                   flops=4 * 10**9, grouped=[at, at + 1], first=[at + 4, at + 5],
                   late=[at + 4, at + 5, at + 8, at + 9, at + 10] + ([at + 13] if part else [])
                   + ([at + 14] if part and second else [])
                   + ([len(ins) - 1] if second else []))
        return list(res[:-n_sums]), list(res[-n_sums:])

    cot_rows = lax.dynamic_slice_in_dim(cotangent, core * sent, sent, 0) if split else cotangent
    cot_s = jnp.pad(cot_rows.astype(F32), ((0, 0), (0, wd - d)))

    tokens_t = tokens.T
    cot_x = links.x(cot_s)
    a1, s1a = forward(False, tokens_t, [], None)
    *a1, tok_a, gate1a, up1a = a1
    r1a = links.sum_cores(s1a)
    y1a = links.y_start(r1a)
    b1, s1b = forward(False, after(tokens_t, r1a), [], a1)
    *b1, n2as, tok_b, gate1b, up1b = b1
    s1b, n2as, y1a = tie(s1b, n2as, y1a)
    sum1a = links.sum_chips(r1a, y1a)
    r1b = links.sum_cores(s1b)
    y1b = links.y_start(r1b)
    n2a_x = links.x(n2as)
    a2, s2a = forward(True, after(a1[6], r1b), sum1a, None)
    *a2, x1a, duh2a, part2a = a2
    s2a, y1b, cot_x = tie(s2a, y1b, cot_x)
    sum1b = links.sum_chips(r1b, y1b)
    cot_p = links.both_cores(cot_x)
    r2a = links.sum_cores(s2a)
    y2a = links.y_start(r2a)
    b2, s2b = forward(True, after(b1[6], r2a, cot_p), sum1b, a2 + [part2a])
    b2, (n2bs, x1b, duh2b, *out2) = b2[:9], b2[9:]
    h2a, h2b = a2[6], b2[6]
    s2b, n2bs, y2a, n2a_x = tie(s2b, n2bs, y2a, n2a_x)
    n2a_p = links.both_cores(n2a_x)
    sum2a = links.sum_chips(r2a, y2a)
    r2b = links.sum_cores(s2b)
    y2b = links.y_start(r2b)
    n2b_x = links.x(n2bs)
    grad_outs = [S((d, f), F32), S((d, 384), F32)]
    gscratch = [pltpu.VMEM((t, d), BF16), pltpu.VMEM((t, d), BF16), pltpu.VMEM((t, f), BF16), pltpu.VMEM((t, 384), BF16)]

    tail = [cs, sn, seqr, valr]

    def backward_a(sums, dz, r):
        outs = [S((th, d), F32), S((th, d), BF16), S((groups, th, 128), BF16), S((groups, th, 128), F32),
                S((groups, 2, th, 128), F32), S((1, d), F32)]
        return call(
            functools.partial(bwd_a_kernel, split, groups), outs,
            [idx, *sums, dz, r[6], *r[1:6], attn_out, g2] + tail, smem=1, flops=4 * 10**9,
            grouped=[n_sums + 3, n_sums + 4, n_sums + 5, n_sums + 6, n_sums + 8], late=[n_sums + 7, n_sums + 10, n_sums + 11],
            first=[n_sums + 7, n_sums + 10, n_sums + 11],
        )

    def backward_b(last, sums, dz, first, ra, rb, xa, xb):
        outs = [S((th, d), BF16), S((groups, th, 320), BF16), S((groups, th, 320), BF16), S((1, d), F32), S((1, d), F32)]
        outs += [S((d, t), BF16)] if last else [S((th, d), F32), S((th, d), F32), piece]
        dha, _, dqxa, dqya, dkva, _ = first
        return call(
            functools.partial(bwd_b_kernel, last, split, groups), outs,
            [idx, *sums, dz, rb[6], *rb[1:6], xa, xb, ra[2], ra[3], dha, dqxa, dqya, dkva, win_t, attn_out, g1, g2] + tail,
            [pltpu.VMEM((th, d), F32)] * 3 + [pltpu.VMEM((2, t, 128), F32), pltpu.VMEM((t, 128), BF16),
             pltpu.VMEM((t, 128), BF16), pltpu.VMEM((th, 128), F32)],
            smem=1, flops=6 * 10**9,
            grouped=[n_sums + k for k in (3, 4, 5, 6, 10, 11, 13, 14, 15, 16, 17)],
            late=[n_sums + k for k in (7, 20, 21, 8, 9, 12)], first=[n_sums + 7, n_sums + 20, n_sums + 21],
        )

    acc = call(own_grads_kernel, grad_outs, [after(a2[7], r2b, sum2a), b2[7], duh2a, duh2b, a2[8], b2[8], cotangent],
               flops=2 * 10**9)
    first2 = backward_a(after(sum2a, acc), cotangent[:th], a2)
    first2, y2b = tie(first2, y2b)
    sum2b = links.sum_chips(r2b, y2b)
    da2b, dp2a, dp2b, dg1b, dg2b1, dz1a, dz1b, dfs = backward_b(
        False, sum2b, cotangent[th:], first2, a2, b2, x1a, x1b)
    dfs, dz1a, dz1b, n2b_x = tie(dfs, dz1a, dz1b, n2b_x)
    df_x = links.x(dfs)
    n2b_p = links.both_cores(n2b_x)
    da2a, dg2b0 = first2[1], first2[5]
    res = call(
        functools.partial(ffn_back_kernel, split), [S((th, f), BF16)] * 2 + [S((th, d), BF16)] * 2 + sums * 2,
        [idx, dz1a, dz1b, gate1a, gate1b, up1a, up1b] + ffn_w, [pltpu.VMEM((th, d), F32)], smem=1, flops=2 * 10**9,
        late=[1, 9, 3, 5, 7, 8, 2, 4, 6],
    )
    duh1, df1, s3 = res[:2], res[2:4], res[4:]
    r3a, r3b = links.sum_cores(s3[:n_sums]), links.sum_cores(s3[n_sums:])
    y3a, y3b = links.y_start(r3a), links.y_start(r3b)
    acc = call(
        functools.partial(both_grads_kernel, len(n2b_p)), grad_outs,
        [*n2b_p, *cot_p, wgu, wdh, after(a1[7], r3a, r3b), b1[7], *duh1, a1[8], b1[8], *df1, *acc], gscratch,
        flops=6 * 10**9, late=[12 + 2 * len(n2b_p) - 2 + 0, 12 + 2 * len(n2b_p) - 1, *range(2 * len(n2b_p) + 2)],
    )
    acc, df_x = tie(acc, df_x)
    df_p = links.both_cores(df_x)
    count = len(df_p)
    chunks = call(
        functools.partial(last_grads_kernel, count, len(CHUNKS)), [S((n, f), F32) for n in CHUNKS],
        [*n2a_p, *df_p, wgu, wdh, *acc], gscratch + [pltpu.VMEM((d, f), F32), pltpu.VMEM((d, 384), F32)],
        flops=4 * 10**9, late=[2 * count + 2, 2 * count + 3],
    )
    quarter = 512 // links.narrow
    group_owner = after(group_owner, acc)
    order = jnp.arange(groups, dtype=jnp.int32)
    sharing = (group_owner[:, None] == group_owner[None, :]) & (order[None, :] < order[:, None])
    rank = jnp.sum(sharing.astype(jnp.int32), axis=1)
    first = jnp.sum(jnp.where((group_owner == member) & (rank == 0), order, 0))
    extra = jnp.sum(jnp.where(rank == 1, order, 0))
    extra_owner = jnp.sum(jnp.where(rank == 1, group_owner, 0))
    idx = jnp.stack([xi, core, first, extra, member, (extra_owner == member).astype(jnp.int32)]).astype(jnp.int32)
    chunks, y3a = tie(chunks, y3a)
    sum3a = links.sum_chips(r3a, y3a)
    lead = quarter // 2 + 8
    made = {}

    def job_a(dep):
        made["a"] = backward_a(after(sum3a, dep), dz1a, a1)
        return made["a"]

    def job_b(dep):
        first, got = tie(made["a"], y3b)
        sums = links.sum_chips(r3b, got)
        made["b"] = backward_b(True, after(sums, dep), dz1b, first, a1, b1, tok_a, tok_b)
        return made["b"]

    def job_grads(dep):
        first, (da1b, dp1a, dp1b, dg1a, dg2a1, _) = made["a"], made["b"]
        gains = jnp.concatenate([dg1a + dg1b, first[5] + dg2a1 + dg2b0 + dg2b1], axis=0)
        return call(
            attn_grad_kernel, [S((n, wd), F32) for n in (lead, 128, 128, lead + 256)],
            [idx, after(a1[0], dep), b1[0], a2[0], b2[0], dp1a, dp1b, dp2a, dp2b, a1[4], b1[4], a2[4], b2[4], first[1],
             da1b, da2a, da2b, gains],
            [pltpu.VMEM((512, d), F32), pltpu.VMEM((quarter + 16, d), F32)], smem=1, flops=2 * 10**9,
        )

    def finish_out(pieces):
        return call(out_kernel, [S((d, t), BF16)], [idx, h2a, h2b, *pieces], [pltpu.VMEM((th, d), F32)], smem=1)

    def unpack(vals, theirs):
        return call(functools.partial(unpack_kernel, 4, False), [S((d, f), F32)] * 2,
                    [idx, *vals[:4], *theirs[:4]], smem=1, late=[1, 5, 2, 6, 3, 7, 4, 8])

    def unpack_down(vals, theirs):
        return call(functools.partial(unpack_kernel, 2, True), [S((d, f), F32)],
                    [idx, *vals[4:6], *theirs[4:6]], smem=1, late=[1, 3, 2, 4])

    def collect(vals, theirs):
        r, o = vals[6], theirs[6]
        second = jnp.where(xi == 0, jnp.concatenate([r, o], 0), jnp.concatenate([o, r], 0))
        return second, links.gather_narrow(second[:quarter])

    done, theirs, results = links.sum_lines(
        chunks, [job_a, job_b, job_grads], out2, finish_out, {3: unpack, 5: unpack_down, 6: collect})
    layer_out = results[None][0].T
    dx = made["b"][5].T
    ggate, gup = results[3]
    gdown, = results[5]
    second, slot1 = results[6]
    small = second[quarter : quarter + 2, :d]
    gin, gout = call(
        functools.partial(attn_finish_kernel, links.narrow), [S((SLOTS, 320, d), F32), S((SLOTS, 192, d), F32)],
        [idx, *done[7:], *theirs[7:], *slot1], smem=1,
    )
    gin = jnp.swapaxes(gin, 1, 2)
    return layer_out, dx, gin, gout, ggate, gup, gdown.T, small[0], small[1]


def _pad(outs, split):
    return list(outs) if split else list(outs) + [None]


def solution(mesh):
    in_specs = (P("wide", None), P(), P(), P(None, "narrow"), P(None, "narrow"), P("narrow", None), P(), P(),
                P("wide", None), P("wide"), P("wide"), P("wide"), P())
    out_specs = (P("wide", None), P("wide", None), P("narrow", None, None), P("narrow", None, None),
                 P(None, "narrow"), P(None, "narrow"), P("narrow", None), P(), P())
    return jax.shard_map(functools.partial(per_device, Links(mesh)), mesh=mesh, in_specs=in_specs,
                         out_specs=out_specs, check_vma=False)
```

```python
import functools
import math

import jax
import jax.numpy as jnp
from jax import lax
from jax.experimental import pallas as pl
from jax.experimental.pallas import tpu as pltpu
from jax.sharding import PartitionSpec as P

HEAD = 64
Q_PER = 3
SLOTS = 2
EPS = 1e-05
THETA = 10000.0
RB = 128
TR = 32
VMEM = 56
F32 = jnp.float32
BF16 = jnp.bfloat16
NEG = -1e30


def dot(a, b):
    return jnp.dot(a, b, preferred_element_type=F32)


def dot_nt(a, b):
    return lax.dot_general(a, b, (((1,), (1,)), ((), ())), preferred_element_type=F32)


def dot_tn(a, b):
    return lax.dot_general(a, b, (((0,), (0,)), ((), ())), preferred_element_type=F32)


def lane_iota(rows):
    return lax.broadcasted_iota(jnp.int32, (rows, 128), 1)


def low_half(rows):
    return lane_iota(rows) < HEAD


def rope128(v, cs, sn):
    lane = lane_iota(v.shape[0])
    partner = jnp.where((lane & 63) < 32, pltpu.roll(v, 96, 1), pltpu.roll(v, 32, 1))
    return v * cs + partner * sn


def allowed_bias(seqr_ref, valr_ref, r0, nk):
    t = r0 + lax.broadcasted_iota(jnp.int32, (RB, nk), 0)
    u = lax.broadcasted_iota(jnp.int32, (RB, nk), 1)
    mine = jnp.broadcast_to(seqr_ref[:, r0 : r0 + RB].astype(F32), (128, RB)).T[:, :1]
    same = mine == seqr_ref[:, :nk].astype(F32)
    ok = (same & (u <= t) & (valr_ref[:, :nk] == 1)) | (u == t)
    return jnp.where(ok, 0.0, NEG).astype(F32)


def masked_heads(x, y):
    low = low_half(1).astype(F32)
    low_b, high_b = low.astype(BF16), (1.0 - low).astype(BF16)
    return jnp.concatenate([x * low_b, x * high_b, y * low_b], axis=0)


def pack_half(xi, a, b):
    low = low_half(a.shape[0])
    at, bt = a[:, 512:], b[:, 512:]
    if xi == 0:
        return a[:, :256], b[:, :256], jnp.where(low, at, pltpu.roll(bt, 64, 1))
    return a[:, 256:512], b[:, 256:512], jnp.where(low, pltpu.roll(at, 64, 1), bt)


def store_pair(idx, ref, rows, a, b):
    for xi in range(2):
        @pl.when(idx[0] == xi)
        def _():
            p, q, r = pack_half(xi, a, b)
            ref[rows, :256] = p.astype(ref.dtype)
            ref[rows, 256:512] = q.astype(ref.dtype)
            ref[rows, 512:] = r.astype(ref.dtype)


def store_one(idx, ref, rows, a):
    low = low_half(a.shape[0])
    at = a[:, 512:]
    for xi in range(2):
        @pl.when(idx[0] == xi)
        def _():
            ref[rows, :256] = a[:, xi * 256 : xi * 256 + 256].astype(ref.dtype)
            ref[rows, 256:] = jnp.where(low, at if xi == 0 else pltpu.roll(at, 64, 1), 0.0).astype(ref.dtype)


def ffn_back(dhid, gate, up, sig):
    return dhid * up * sig * (1.0 + gate * (1.0 - sig)), dhid * (gate * sig)


def put_wide(ref, v):
    d = v.shape[1]
    ref[:, :d] = v
    if ref.shape[1] > d:
        ref[:, d:] = jnp.zeros((ref.shape[0], ref.shape[1] - d), ref.dtype)


def half_rows(ref, which, n):
    return ref[pl.ds(pl.multiple_of(which * n, 8), n), :]


def split_send(idx, whole, keep, send):
    n = keep.shape[0]
    put_wide(keep, half_rows(whole, idx[1], n))
    put_wide(send, half_rows(whole, 1 - idx[1], n))


def take_sum(idx, pieces, out):
    d = out.shape[1]
    if len(pieces) == 1:
        out[...] = pieces[0][:, :d]
        return
    n = pieces[0].shape[0]
    out[pl.ds(pl.multiple_of(idx[1] * n, n), n), :] = pieces[0][:, :d]
    out[pl.ds(pl.multiple_of((1 - idx[1]) * n, n), n), :] = pieces[1][:, :d]


class Late:
    def __init__(self, source, buffer, sems, at, grouped, pick=None):
        self.pick = pick
        self.source, self.buffer, self.sems, self.at, self.grouped = source, buffer, sems, at, grouped
        self.waited = False

    def copy(self, g=None):
        if g is None:
            return pltpu.make_async_copy(self.source, self.buffer, self.sems.at[self.at])
        source = g if self.pick is None else self.pick[2 + g]
        return pltpu.make_async_copy(self.source.at[source], self.buffer.at[g], self.sems.at[self.at + g])

    def start(self):
        self.copy().start()

    def wait(self):
        if not self.waited:
            self.copy().wait()
            self.waited = True
        return self.buffer


def ready(*refs):
    got = [r.wait() if isinstance(r, Late) else r for r in refs]
    return got if len(got) > 1 else got[0]


def ready_group(g, *refs):
    for r in refs:
        r.copy(g).wait()


def buffers(*refs):
    return [r.buffer for r in refs]


def fwd_kernel(second, split, part, groups, *refs):
    it = iter(refs)
    idx = next(it)
    x_ref = next(it)
    add_refs = [next(it) for _ in range(2 if split else 1)] if second else None
    win, wout, g1, g2, cs_ref, sn_ref, seqr, valr, wg, wu, wdt = (next(it) for _ in range(11))
    kt_old, vt_old, n2_old = (next(it) for _ in range(3)) if part else (None, None, None)
    part_old = next(it) if part and second else None
    cot = next(it) if second else None
    n1_ref, qk_ref, kt_ref, vt_ref, o_ref, lse_ref, h_ref, n2_ref, hidh_ref = (next(it) for _ in range(9))
    n2s_ref = next(it) if part else None
    x_out = next(it)
    if second:
        duh_ref, part_refs = next(it), [next(it) for _ in range(2 if part and split else 1)]
    else:
        gate_ref, up_ref = next(it), next(it)
    outs = [next(it) for _ in range(2 if split else 1)]
    acc, whole, ktf, vtf = (next(it) for _ in range(4))
    t = n1_ref.shape[0]
    base = part * t

    if second:
        take_sum(idx, add_refs, acc)
        x = x_ref[...] + acc[...]
        x_out[...] = x
    else:
        x = x_ref[:, base : base + t].astype(F32).T
        x_out[...] = x.astype(BF16)
    r1 = lax.rsqrt(jnp.mean(x * x, axis=1, keepdims=True) + EPS)
    n1_ref[...] = (x * r1 * g1[...]).astype(BF16)
    acc[...] = x
    flush(n1_ref)
    flush(x_out)
    lse_ref[...] = jnp.zeros_like(lse_ref)
    cs_ref, sn_ref = ready(cs_ref, sn_ref)
    win_l, wout_l = win, wout
    win, wout = buffers(win, wout)

    def group(g, carry):
        ready_group(g, win_l, wout_l)
        n1 = n1_ref[...]
        qk = dot_nt(n1, win[g, :256, :])
        v = dot_nt(n1, win[g, 256:320, :])
        cs, sn = cs_ref[base : base + t, :], sn_ref[base : base + t, :]
        xr = rope128(qk[:, :128], cs, sn)
        yr = rope128(qk[:, 128:], cs, sn)
        qk_ref[g, :, :128] = xr.astype(BF16)
        qk_ref[g, :, 128:] = yr.astype(BF16)
        kt = jnp.where(low_half(t), pltpu.roll(yr, 64, 1), yr).astype(BF16)
        vt = jnp.concatenate([v, v], axis=1).astype(BF16)
        kt_ref[g] = kt
        vt_ref[g] = vt
        if part:
            ktf[:base, :] = kt_old[g]
            vtf[:base, :] = vt_old[g]
        ktf[base : base + t, :] = kt
        vtf[base : base + t, :] = vt
        for rb in range(t // RB):
            r0 = rb * RB
            nk = base + r0 + RB
            rows = slice(r0, r0 + RB)
            q = masked_heads(qk_ref[g, rows, :128], qk_ref[g, rows, 128:])
            s = dot_nt(q, ktf[:nk, :])
            bias = allowed_bias(seqr, valr, base + r0, nk)
            es, ms, lls = [], [], []
            for r in range(0, 3 * RB, TR):
                st = s[r : r + TR] * 0.125 + bias[r % RB : r % RB + TR]
                mt = jnp.max(st, axis=1, keepdims=True)
                et = jnp.exp(st - mt)
                ms.append(mt)
                lls.append(jnp.sum(et, axis=1, keepdims=True))
                es.append(et.astype(BF16))
            m, l = jnp.concatenate(ms, axis=0), jnp.concatenate(lls, axis=0)
            o = dot(jnp.concatenate(es, axis=0), vtf[:nk, :]) / l
            low = low_half(RB)
            o_ref[g, rows, :128] = jnp.where(low, o[:RB], o[RB : 2 * RB]).astype(BF16)
            o_ref[g, rows, 128:] = jnp.where(low, o[2 * RB :], 0.0).astype(BF16)
            ls = m + jnp.log(l)
            lane = lane_iota(RB)
            cur = lse_ref[rows, :]
            for j in range(3):
                cur = jnp.where(lane == g * 3 + j, ls[j * RB : (j + 1) * RB], cur)
            lse_ref[rows, :] = cur
        acc[...] += dot(o_ref[g, :, :192], wout[g])
        return carry

    lax.fori_loop(0, groups, group, 0)
    for ref in (qk_ref, kt_ref, vt_ref, o_ref, lse_ref):
        flush(ref)
    h = acc[...]
    h_ref[...] = h
    flush(h_ref)
    r2 = lax.rsqrt(jnp.mean(h * h, axis=1, keepdims=True) + EPS)
    n2 = (h * r2 * g2[...]).astype(BF16)
    n2_ref[...] = n2
    flush(n2_ref)
    if part:
        n2_old = ready(n2_old)
        if split:
            for c in range(2):
                @pl.when(idx[1] == c)
                def _():
                    put_wide(n2s_ref, (n2_old if c == 0 else n2_ref)[...].astype(F32))
        else:
            put_wide(n2s_ref.at[:t, :], n2_old[...].astype(F32))
            put_wide(n2s_ref.at[t:, :], n2_ref[...].astype(F32))
    if part:
        flush(n2s_ref)
    wg, wu, wdt = ready(wg, wu, wdt)
    every = slice(0, t)
    gate = dot(n2, wg[...])
    up = dot(n2, wu[...])
    sig = jax.nn.sigmoid(gate)
    hid = gate * sig * up
    store_one(idx, hidh_ref, every, hid)
    flush(hidh_ref)
    if second:
        cot = ready(cot)
        if part and split:
            part_old = ready(part_old)
            half = t // 2
            whole[...] = dot_nt(hid.astype(BF16), wdt[...])
            for ref, which in zip(part_refs, (idx[1], 1 - idx[1])):
                put_wide(ref.at[:half, :], half_rows(part_old, which, half))
                put_wide(ref.at[half:, :], half_rows(whole, which, half))
                flush(ref)
        elif part:
            part_old = ready(part_old)
            put_wide(part_refs[0].at[:t, :], part_old[...])
            put_wide(part_refs[0].at[t:, :], dot_nt(hid.astype(BF16), wdt[...]))
        else:
            part_refs[0][...] = dot_nt(hid.astype(BF16), wdt[...])
            flush(part_refs[0])
        dgate, dup = ffn_back(dot(cot[base : base + t, :], wdt[...]), gate, up, sig)
        store_pair(idx, duh_ref, every, dgate, dup)
        flush(duh_ref)
        whole[...] = dot_nt(dgate.astype(BF16), wg[...]) + dot_nt(dup.astype(BF16), wu[...])
    else:
        gate_ref[...] = gate
        up_ref[...] = up
        flush(gate_ref)
        flush(up_ref)
        whole[...] = dot_nt(hid.astype(BF16), wdt[...])
    if split:
        split_send(idx, whole, *outs)
    else:
        put_wide(outs[0], whole[...])


def norm_back(dn, stream, gain):
    r = lax.rsqrt(jnp.mean(stream * stream, axis=1, keepdims=True) + EPS)
    m = stream * r
    dgain = jnp.sum(dn * m, axis=0, keepdims=True)
    dm = dn * gain
    return r * (dm - m * jnp.mean(dm * m, axis=1, keepdims=True)), dgain


def bwd_enter(idx, dn2_refs, dz_ref, h_ref, g2, dh_ref, da_ref, dg2_ref):
    take_sum(idx, dn2_refs, dh_ref)
    dh, dg2 = norm_back(dh_ref[...], h_ref[...], g2[...])
    dh = dz_ref[...].astype(F32) + dh
    dh_ref[...] = dh
    da_ref[...] = dh.astype(BF16)
    dg2_ref[...] = dg2


def bwd_block(g, r0, base, do, qk_ref, o_ref, lse_ref, ktf, vtf, seqr, valr, dkv):
    low, lane = low_half(RB), lane_iota(RB)
    nk = base + r0 + RB
    rows = slice(r0, r0 + RB)
    do = do[rows]
    dox = do[:, :128].astype(BF16)
    doy = jnp.concatenate([do[:, 128:192], jnp.zeros((RB, 64), F32)], axis=1).astype(BF16)
    px = dox.astype(F32) * o_ref[g, rows, :128].astype(F32)
    py = doy.astype(F32) * o_ref[g, rows, 128:].astype(F32)
    delta = jnp.concatenate(
        [
            jnp.sum(jnp.where(low, px, 0.0), axis=1, keepdims=True),
            jnp.sum(jnp.where(low, 0.0, px), axis=1, keepdims=True),
            jnp.sum(py, axis=1, keepdims=True),
        ],
        axis=0,
    )
    ls = lse_ref[rows, :]
    lse = jnp.concatenate(
        [jnp.sum(jnp.where(lane == g * 3 + j, ls, 0.0), axis=1, keepdims=True) for j in range(3)], axis=0
    )
    q = masked_heads(qk_ref[g, rows, :128], qk_ref[g, rows, 128:])
    dos = masked_heads(dox, doy)
    kt = ktf(nk)
    s = dot_nt(q, kt)
    dp = dot_nt(dos, vtf(nk))
    bias = allowed_bias(seqr, valr, base + r0, nk)
    ps, dss = [], []
    for r in range(0, 3 * RB, TR):
        part = slice(r, r + TR)
        pt = jnp.exp(s[part] * 0.125 + bias[r % RB : r % RB + TR] - lse[part])
        ps.append(pt.astype(BF16))
        dss.append((pt * (dp[part] - delta[part])).astype(BF16))
    p, ds = jnp.concatenate(ps, axis=0), jnp.concatenate(dss, axis=0)
    dq = dot(ds, kt) * 0.125
    dkv[0, :nk, :] += dot_tn(ds, q)
    dkv[1, :nk, :] += dot_tn(p, dos)
    return jnp.where(low, dq[:RB], dq[RB : 2 * RB]), dq[2 * RB :]


def bwd_a_kernel(split, groups, *refs):
    it = iter(refs)
    idx = next(it)
    dn2_refs = [next(it) for _ in range(2 if split else 1)]
    dz_ref, h_ref, qk_ref, kt_ref, vt_ref, o_ref, lse_ref, wout, g2, cs_ref, sn_ref, seqr, valr = (
        next(it) for _ in range(13))
    dh_ref, da_ref, dqx_ref, dqy_ref, dkv_ref, dg2_ref = (next(it) for _ in range(6))
    t = dh_ref.shape[0]
    bwd_enter(idx, dn2_refs, dz_ref, h_ref, g2, dh_ref, da_ref, dg2_ref)
    flush(dh_ref)
    flush(da_ref)
    dkv_ref[...] = jnp.zeros_like(dkv_ref)
    lse_ref, cs_ref, sn_ref = ready(lse_ref, cs_ref, sn_ref)
    waits = (qk_ref, kt_ref, vt_ref, o_ref, wout)
    qk_ref, kt_ref, vt_ref, o_ref, wout = buffers(*waits)

    def group(g, carry):
        ready_group(g, *waits)
        do = dot_nt(da_ref[...], wout[g])
        for r0 in range(0, t, RB):
            rows = slice(r0, r0 + RB)
            dqx, dqy = bwd_block(g, r0, 0, do, qk_ref, o_ref, lse_ref, lambda n: kt_ref[g, :n, :],
                                 lambda n: vt_ref[g, :n, :], seqr, valr, dkv_ref.at[g])
            dqx_ref[g, rows, :] = rope128(dqx, cs_ref[rows, :], -sn_ref[rows, :]).astype(BF16)
            dqy_ref[g, rows, :] = dqy
        return carry

    lax.fori_loop(0, groups, group, 0)


def bwd_b_kernel(last, split, groups, *refs):
    it = iter(refs)
    idx = next(it)
    dn2_refs = [next(it) for _ in range(2 if split else 1)]
    (dz_ref, h_ref, qk_ref, kt_ref, vt_ref, o_ref, lse_ref, xa_ref, xb_ref, kt_old, vt_old, dha_ref, dqxa_ref, dqya_ref,
     dkva_ref, win, wout, g1, g2, cs_ref, sn_ref, seqr, valr) = (next(it) for _ in range(23))
    da_ref, dpa_ref, dpb_ref, dg1_ref, dg2_ref, dxa_ref = (next(it) for _ in range(6))
    dxb_ref = None if last else next(it)
    dfs_ref = None if last else next(it)
    dh_ref, acca, accb, dkv, ktf, vtf, dqy_ref = (next(it) for _ in range(7))
    t = dh_ref.shape[0]
    bwd_enter(idx, dn2_refs, dz_ref, h_ref, g2, dh_ref, da_ref, dg2_ref)
    acca[...] = jnp.zeros_like(acca)
    flush(da_ref)
    accb[...] = jnp.zeros_like(accb)
    lse_ref, cs_ref, sn_ref = ready(lse_ref, cs_ref, sn_ref)
    waits = (qk_ref, kt_ref, vt_ref, o_ref, kt_old, vt_old, dqxa_ref, dqya_ref, dkva_ref, win, wout)
    qk_ref, kt_ref, vt_ref, o_ref, kt_old, vt_old, dqxa_ref, dqya_ref, dkva_ref, win, wout = buffers(*waits)

    def group(g, carry):
        ready_group(g, *waits)
        do = dot_nt(da_ref[...], wout[g])
        ktf[:t, :] = kt_old[g]
        ktf[t:, :] = kt_ref[g]
        vtf[:t, :] = vt_old[g]
        vtf[t:, :] = vt_ref[g]
        dkv[:, :t, :] = dkva_ref[g]
        dkv[:, t:, :] = jnp.zeros((2, t, 128), F32)
        for r0 in range(0, t, RB):
            rows = slice(r0, r0 + RB)
            dqx, dqy = bwd_block(g, r0, t, do, qk_ref, o_ref, lse_ref, lambda n: ktf[:n, :], lambda n: vtf[:n, :],
                                 seqr, valr, dkv)
            full = slice(t + r0, t + r0 + RB)
            dpb_ref[g, rows, :128] = rope128(dqx, cs_ref[full, :], -sn_ref[full, :]).astype(BF16)
            dqy_ref[rows, :] = dqy
        dpa_ref[g, :, :128] = dqxa_ref[g]
        low = low_half(t)
        for k, (ref, dqy) in enumerate(((dpa_ref, dqya_ref[g]), (dpb_ref, dqy_ref[...]))):
            rows = slice(k * t, k * t + t)
            dk, dv = dkv[0, rows, :], dkv[1, rows, :]
            dk = (dk + pltpu.roll(dk, 64, 1)) * 0.125
            dv = dv + pltpu.roll(dv, 64, 1)
            dy = jnp.where(low, dqy, dk)
            ref[g, :, 128:256] = rope128(dy, cs_ref[rows, :], -sn_ref[rows, :]).astype(BF16)
            ref[g, :, 256:320] = dv[:, :64].astype(BF16)
        both = dot(jnp.concatenate([dpa_ref[g], dpb_ref[g]], axis=0), win[g])
        acca[...] += both[:t]
        accb[...] += both[t:]
        return carry

    lax.fori_loop(0, groups, group, 0)
    flush(dpa_ref)
    flush(dpb_ref)
    xa_ref, xb_ref, dha_ref = ready(xa_ref, xb_ref, dha_ref)
    dxa, dg1a = norm_back(acca[...], xa_ref[...].astype(F32), g1[...])
    dxb, dg1b = norm_back(accb[...], xb_ref[...].astype(F32), g1[...])
    dg1_ref[...] = dg1a + dg1b
    if last:
        dxa_ref[:, :t] = (dxa + dha_ref[...]).T.astype(BF16)
        dxa_ref[:, t:] = (dxb + dh_ref[...]).T.astype(BF16)
    else:
        dxa_ref[...] = dxa + dha_ref[...]
        dxb_ref[...] = dxb + dh_ref[...]
        flush(dxa_ref)
        flush(dxb_ref)
    if not last:
        if split:
            for c in range(2):
                @pl.when(idx[1] == c)
                def _():
                    put_wide(dfs_ref, (dxa_ref if c == 0 else dxb_ref)[...].astype(BF16).astype(F32))
        else:
            put_wide(dfs_ref.at[:t, :], dxa_ref[...].astype(BF16).astype(F32))
            put_wide(dfs_ref.at[t:, :], dxb_ref[...].astype(BF16).astype(F32))


def ffn_back_kernel(split, *refs):
    idx, dza, dzb, gatea, gateb, upa, upb, wg, wu, wdt, duha, duhb, dfa, dfb, *rest = refs
    outs, whole = rest[:-1], rest[-1]
    per = len(outs) // 2
    for k, (dz_ref, gate_ref, up_ref, duh_ref, df_ref) in enumerate(
            ((dza, gatea, upa, duha, dfa), (dzb, gateb, upb, duhb, dfb))):
        df = ready(dz_ref)[...].astype(BF16)
        df_ref[...] = df
        flush(df_ref)
        wdt, gate_ref, up_ref = ready(wdt, gate_ref, up_ref)
        gate, up = gate_ref[...], up_ref[...]
        dgate, dup = ffn_back(dot(df, wdt[...]), gate, up, jax.nn.sigmoid(gate))
        store_pair(idx, duh_ref, slice(0, df.shape[0]), dgate, dup)
        flush(duh_ref)
        wg, wu = ready(wg, wu)
        whole[...] = dot_nt(dgate.astype(BF16), wg[...]) + dot_nt(dup.astype(BF16), wu[...])
        if split:
            split_send(idx, whole, *outs[per * k : per * k + per])
        else:
            put_wide(outs[k], whole[...])
        for ref in outs[per * k : per * k + per]:
            flush(ref)


def own_grads(n2, duh, hidh, df, base, put):
    for r in range(0, n2[0].shape[1], 320):
        put(0, r, sum((dot_tn(a[:, r : r + 320], b[...]) for a, b in zip(n2, duh)), base(0, r)))
        put(1, r, sum((dot_tn(a[:, r : r + 320], b[...]) for a, b in zip(df, hidh)), base(1, r)))


def peer_acts(xi, n2, df, wg, wu, wdt, du, hd, rows):
    half = pl.ds(pl.multiple_of(xi * 256, 128), 256)
    last = slice(512, 640)

    def own_half(v):
        return jnp.where(xi == 0, v, pltpu.roll(v, 64, 1))

    ga, gb = dot(n2, wg[:, half]), own_half(dot(n2, wg[:, last]))
    ua, ub = dot(n2, wu[:, half]), own_half(dot(n2, wu[:, last]))
    dha, dhb = dot(df, wdt[:, half]), own_half(dot(df, wdt[:, last]))
    sa, sb = jax.nn.sigmoid(ga), jax.nn.sigmoid(gb)
    low = low_half(n2.shape[0])
    hd[rows, :256] = (ga * sa * ua).astype(BF16)
    hd[rows, 256:] = jnp.where(low, gb * sb * ub, 0.0).astype(BF16)
    dga, dua = ffn_back(dha, ga, ua, sa)
    dgb, dub = ffn_back(dhb, gb, ub, sb)
    du[rows, :256] = dga.astype(BF16)
    du[rows, 256:512] = dua.astype(BF16)
    du[rows, 512:] = jnp.where(low, dgb, pltpu.roll(dub, 64, 1)).astype(BF16)


def peer_grads(xi, n2p, dfp, weights, scratch, base, put):
    n2, df, du, hd = scratch
    d = n2.shape[1]
    n = n2p[0].shape[0]
    for i in range(len(n2p)):
        rows = slice(i * n, i * n + n)
        n2[rows, :] = n2p[i][:, :d].astype(BF16)
        df[rows, :] = dfp[i][:, :d].astype(BF16)
        for r in range(i * n, i * n + n, 256):
            part = slice(r, r + 256)
            peer_acts(xi, n2[part, :], df[part, :], *weights, du, hd, part)
    own_grads([n2], [du], [hd], [df], base, put)


def own_grads_kernel(*refs):
    n2, duh, hidh, cot, outs = refs[:2], refs[2:4], refs[4:6], refs[6], refs[7:]
    t = n2[0].shape[0]

    def put(k, r, v):
        outs[k][r : r + 320, :] = v
        flush(outs[k], slice(r, r + 320))

    own_grads(n2, duh, hidh, [cot.at[:t, :], cot.at[t:, :]], lambda k, r: 0.0, put)


def both_grads_kernel(count, *refs):
    idx, refs = refs[0], refs[1:]
    n2p, dfp = refs[:count], refs[count : 2 * count]
    wg, wu, wdt, *rest = refs[2 * count :]
    n2, duh, hidh, df = (rest[2 * k : 2 * k + 2] for k in range(4))
    old, outs, scratch = rest[8:10], rest[10:12], rest[12:]

    def put(k, r, v):
        outs[k][r : r + 320, :] = v

    def put_last(k, r, v):
        outs[k][r : r + 320, :] = v
        flush(outs[k], slice(r, r + 320))

    old = ready(*old)
    own_grads(n2, duh, hidh, df, lambda k, r: old[k][r : r + 320, :], put)
    n2p, dfp = [ready(r) for r in n2p], [ready(r) for r in dfp]
    weights = ready(wg, wu, wdt)
    peer_grads(idx[0], n2p, dfp, weights, scratch, lambda k, r: outs[k][r : r + 320, :], put_last)


def last_grads_kernel(count, n_chunks, *refs):
    idx, refs = refs[0], refs[1:]
    n2p, dfp = refs[:count], refs[count : 2 * count]
    wg, wu, wdt, *rest = refs[2 * count :]
    old, chunks, scratch = rest[:2], rest[2 : 2 + n_chunks], rest[2 + n_chunks : 6 + n_chunks]
    gu, dn = rest[6 + n_chunks :]

    def put(k, r, v):
        (gu, dn)[k][r : r + 320, :] = v

    peer_grads(idx[0], n2p, dfp, (wg, wu, wdt), scratch, lambda k, r: ready(old[k])[r : r + 320, :], put)
    at = 0
    half = dn.shape[0] // 2
    for out in chunks:
        n = out.shape[0]
        if at < gu.shape[0]:
            out[...] = gu[at : at + n, :]
        else:
            r = at - gu.shape[0]
            a, b = dn[r : r + n, :], dn[half + r : half + r + n, :]
            out[:, :256] = a[:, :256]
            out[:, 256:512] = b[:, :256]
            out[:, 512:] = jnp.where(low_half(n), a[:, 256:], pltpu.roll(b[:, 256:], 64, 1))
        flush(out)
        at += n


def unpack_kernel(count, stacked, *refs):
    idx = refs[0]
    own, other, outs = refs[1 : 1 + count], refs[1 + count : 1 + 2 * count], refs[1 + 2 * count :]
    at = 0
    for o, p in zip(own, other):
        o, p = ready(o, p)
        n = o.shape[0]
        for xi in range(2):
            @pl.when(idx[0] == xi)
            def _():
                a, b = (o, p) if xi == 0 else (p, o)
                low = low_half(n)
                at4, bt4 = a[:, 512:], b[:, 512:]
                firsts = jnp.where(low, at4, pltpu.roll(bt4, 64, 1))
                seconds = jnp.where(low, pltpu.roll(at4, 64, 1), bt4)
                for k, tile in ((0, firsts), (1, seconds)):
                    ref = outs[0] if stacked else outs[k]
                    r = at + (k * (ref.shape[0] // 2) if stacked else 0)
                    ref[r : r + n, :256] = a[:, 256 * k : 256 * k + 256]
                    ref[r : r + n, 256:512] = b[:, 256 * k : 256 * k + 256]
                    ref[r : r + n, 512:] = tile
        for k in range(2):
            ref = outs[0] if stacked else outs[k]
            r = at + (k * (ref.shape[0] // 2) if stacked else 0)
            flush(ref, slice(r, r + n))
        at += n


def attn_grad_kernel(idx, *refs):
    n1, dp, o, da = (refs[4 * k : 4 * k + 4] for k in range(4))
    da = [ready(v) for v in da]
    gains, keep2, keep0, keep1, send, whole, extra = refs[16:]

    def grads(g, out, at):
        ready_group(g, *dp)
        out[at : at + 320, :] = sum(dot_tn(p[g], n[...]) for p, n in zip(buffers(*dp), n1))
        ready_group(g, *o)
        out[at + 320 : at + 512, :] = sum(dot_tn(v[g, :, :192], a[...]) for v, a in zip(buffers(*o), da))

    grads(0, whole, 0)
    half = whole.shape[0] // 2
    lead = send.shape[0] - half
    for at, ref in ((0, keep0), (keep0.shape[0], keep1)):
        put_wide(ref, whole[pl.ds(pl.multiple_of(idx[0] * half + at, 8), ref.shape[0]), :])
    put_wide(send.at[lead:, :], half_rows(whole, 1 - idx[0], half))
    grads(1, whole, 0)
    rows_in, rows_out = 320 // idx_parts(extra), 192 // idx_parts(extra)
    extra[:rows_in, :] = whole[pl.ds(pl.multiple_of(idx[4] * rows_in, 8), rows_in), :]
    extra[rows_in : rows_in + rows_out, :] = whole[pl.ds(pl.multiple_of(320 + idx[4] * rows_out, 8), rows_out), :]
    n = rows_in + rows_out
    extra[n:, :] = jnp.zeros((extra.shape[0] - n, extra.shape[1]), F32)
    extra[n : n + 2, :] = gains[...]
    half = extra.shape[0] // 2
    put_wide(keep2, half_rows(extra, idx[0], half))
    put_wide(send.at[:lead, :], half_rows(extra, 1 - idx[0], half))


def out_kernel(idx, ha, hb, *refs):
    pieces, out, whole = refs[:-2], refs[-2], refs[-1]
    t, d = ha.shape
    half = t // len(pieces)
    for k, h in enumerate((ha, hb)):
        if len(pieces) == 1:
            whole[...] = pieces[0][k * t : k * t + t, :d]
        else:
            rows = slice(k * half, k * half + half)
            whole[pl.ds(pl.multiple_of(idx[1] * half, half), half), :] = pieces[0][rows, :d]
            whole[pl.ds(pl.multiple_of((1 - idx[1]) * half, half), half), :] = pieces[1][rows, :d]
        out[:, k * t : k * t + t] = (whole[...] + h[...]).T.astype(BF16)


def attn_finish_kernel(parts, idx, a0, a1, b0, b1, *rest):
    slot1, gin, gout = rest[:-2], *rest[-2:]
    d = gin.shape[2]
    mine = idx[5].astype(F32)
    rows_in, rows_out = 320 // parts, 192 // parts
    for k, quarter in enumerate(slot1):
        quarter = ready(quarter)
        m = (idx[4] // 2 * (1 - k % 2) + (1 - idx[4] // 2) * (k % 2)) * 2 + (
            idx[4] % 2 * (1 - k // 2) + (1 - idx[4] % 2) * (k // 2))
        gin[1, pl.ds(pl.multiple_of(m * rows_in, 8), rows_in), :] = quarter[:rows_in, :d] * mine
        gout[1, pl.ds(pl.multiple_of(m * rows_out, 8), rows_out), :] = (
            quarter[rows_in : rows_in + rows_out, :d] * mine)
    flush(gin, slice(1, 2))
    flush(gout, slice(1, 2))
    a0, a1, b0, b1 = ready(a0, a1, b0, b1)
    for xi in range(2):
        @pl.when(idx[0] == xi)
        def _():
            p0, p1, q0, q1 = (a0, a1, b0, b1) if xi == 0 else (b0, b1, a0, a1)
            n = p0.shape[0]
            gin[0, :n, :] = p0[:, :d]
            gin[0, n:256, :] = p1[:, :d]
            gin[0, 256:, :] = q0[:64, :d]
            gout[0, : n - 64, :] = q0[64:, :d]
            gout[0, n - 64 :, :] = q1[:, :d]
    flush(gin, slice(0, 1))
    flush(gout, slice(0, 1))


def idx_parts(extra):
    return 512 // (extra.shape[0] - 16)


BIG = 32 * 1024
OUT = {}


def flush(ref, rows=None):
    out, sem, whole = OUT[id(ref)]
    part = ref if rows is None else ref.at[rows, :]
    to = out if rows is None else out.at[rows, :]
    pltpu.make_async_copy(part, to, sem).start()
    OUT[id(ref)] = (out, sem, True)


def size(a):
    return math.prod(a.shape) * jnp.dtype(a.dtype).itemsize


def call(kernel, outs, ins, scratch=(), smem=0, flops=0, late=(), grouped=(), first=(), picked=()):
    n_in, n_out = len(ins), len(outs)
    big_in = [i for i in range(smem, n_in) if size(ins[i]) >= BIG]
    big_out = [i for i in range(n_out) if size(outs[i]) >= BIG]
    in_specs = [
        pl.BlockSpec(memory_space=pltpu.SMEM if i < smem else pl.ANY if i in big_in else pltpu.VMEM) for i in range(n_in)
    ]
    out_specs = [pl.BlockSpec(memory_space=pl.ANY if i in big_out else pltpu.VMEM) for i in range(n_out)]
    buffers = [pltpu.VMEM((2, *ins[i].shape[1:]) if i in picked else ins[i].shape, ins[i].dtype) for i in big_in]
    buffers += [pltpu.VMEM(outs[i].shape, outs[i].dtype) for i in big_out]
    at, n_sems = {}, 0
    for i in big_in:
        at[i] = n_sems
        n_sems += ins[i].shape[0] if i in grouped else 2 if i in picked else 1
    out_at = n_sems
    sems = pltpu.SemaphoreType.DMA((n_sems + len(big_out),))

    def body(*refs):
        ins_, outs_, rest = list(refs[:n_in]), list(refs[n_in : n_in + n_out]), list(refs[n_in + n_out :])
        own, (bufs, sem) = rest[: len(scratch)], (rest[len(scratch) : -1], rest[-1])
        kept = []
        for k, i in enumerate(big_in):
            pick = ins_[0] if i in picked else None
            kept.append((i, Late(ins_[i], bufs[k], sem, at[i], i in grouped or i in picked, pick)))
        items = dict(kept)
        for i in big_in:
            if i not in late and i not in grouped and i not in picked:
                items[i].start()
        for i in first:
            items[i].start()
        for g in range(2):
            for i in picked:
                items[i].copy(g).start()
        for g in range(max((ins[i].shape[0] for i in grouped), default=0)):
            for i in grouped:
                items[i].copy(g).start()
        for i in late:
            if i in items and i not in first:
                items[i].start()
        for i, item in kept:
            early = i not in late and i not in grouped and i not in picked
            ins_[i] = item.wait() if early else item
        OUT.clear()
        for k, i in enumerate(big_out):
            buf = bufs[len(big_in) + k]
            OUT[id(buf)] = (outs_[i], sem.at[out_at + k], False)
            outs_[i] = buf
        kernel(*ins_, *outs_, *own)
        for i in big_out:
            if not OUT[id(outs_[i])][2]:
                flush(outs_[i])
        for i, item in kept:
            assert item.grouped or item.waited
        for i in big_out:
            out, s, _ = OUT[id(outs_[i])]
            pltpu.make_async_copy(outs_[i], out, s).wait()
        OUT.clear()

    return pl.pallas_call(
        body,
        out_shape=tuple(outs),
        in_specs=in_specs,
        out_specs=tuple(out_specs),
        scratch_shapes=list(scratch) + buffers + [sems],
        compiler_params=pltpu.CompilerParams(vmem_limit_bytes=VMEM * 1024 * 1024),
        cost_estimate=pl.CostEstimate(flops=1, bytes_accessed=1, transcendentals=0),
    )(*ins)


def S(shape, dtype):
    return jax.ShapeDtypeStruct(shape, dtype)


def add_kernel(a, b, out):
    out[...] = a[...] + b[...]


def pick_kernel(flag, a, b, out):
    @pl.when(flag[0] == 1)
    def _():
        out[...] = a[...]

    @pl.when(flag[0] != 1)
    def _():
        out[...] = b[...]


def small_call(kernel, ins, smem=0):
    a = ins[-1]
    return pl.pallas_call(
        kernel,
        out_shape=jax.ShapeDtypeStruct(a.shape, a.dtype),
        in_specs=[pl.BlockSpec(memory_space=pltpu.SMEM)] * smem + [pl.BlockSpec(memory_space=pltpu.VMEM)] * 2,
        out_specs=pl.BlockSpec(memory_space=pltpu.VMEM),
        compiler_params=pltpu.CompilerParams(vmem_limit_bytes=8 * 2**20),
        cost_estimate=pl.CostEstimate(flops=1, bytes_accessed=1, transcendentals=0),
    )(*ins)


def add(a, b):
    return small_call(add_kernel, [a, b])


def add_pieces(keeps, got):
    def kernel(*refs):
        n = len(keeps)
        at = 0
        for keep, out in zip(refs[:n], refs[n + 1 :]):
            out[...] = keep[...] + refs[n][at : at + keep.shape[0], :]
            at += keep.shape[0]

    return pl.pallas_call(
        kernel,
        out_shape=tuple(jax.ShapeDtypeStruct(k.shape, k.dtype) for k in keeps),
        compiler_params=pltpu.CompilerParams(vmem_limit_bytes=12 * 2**20),
        cost_estimate=pl.CostEstimate(flops=1, bytes_accessed=1, transcendentals=0),
    )(*keeps, got)


class Links:
    def __init__(self, mesh):
        self.wide, self.narrow = mesh.shape["wide"], mesh.shape["narrow"]
        self.known = (self.wide, self.narrow) == (8, 4)

    def permute(self, v, step):
        pairs = []
        for w in range(self.wide):
            for n in range(self.narrow):
                to = step(w // 2, w % 2, n // 2, n % 2)
                if to is not None:
                    z, x, y, c = to
                    pairs.append((w * self.narrow + n, (z * 2 + x) * self.narrow + y * 2 + c))
        return lax.ppermute(v, ("wide", "narrow"), pairs)

    def core(self, v):
        return self.permute(v, lambda z, x, y, c: (z, x, y, 1 - c))

    def y(self, v):
        return self.permute(v, lambda z, x, y, c: (z, x, 1 - y, c))

    def x(self, v):
        return self.permute(v, lambda z, x, y, c: (z, 1 - x, y, c))

    def inward(self, v):
        return self.permute(v, lambda z, x, y, c: ({0: 1, 3: 2}[z], x, y, c) if z in (0, 3) else None)

    def outward(self, v):
        return self.permute(v, lambda z, x, y, c: ({1: 0, 2: 3}[z], x, y, c) if z in (1, 2) else None)

    def middle(self, v):
        return self.permute(v, lambda z, x, y, c: (3 - z, x, y, c) if z in (1, 2) else None)

    def sum_cores(self, pieces):
        return add(pieces[0], self.core(pieces[1])) if self.known else pieces[0]

    def y_start(self, r):
        return self.y(r) if self.known else r

    def sum_chips(self, r, got):
        if not self.known:
            return [lax.psum(r, "narrow")]
        r = add(r, got)
        return [r, self.core(r)]

    def both_cores(self, got):
        return [got, self.core(got)] if self.known else [got]

    def sum_lines(self, chunks, jobs, pieces, finish, hooks):
        last = chunks[0]
        if not self.known:
            for job in jobs:
                last = job(last)
            *keeps, send = last
            n = len(chunks) + len(keeps)
            got = self.x(send)
            pairs, at = [], 0
            for keep in keeps:
                pairs.append((keep, at))
                at += keep.shape[0]
            vals, theirs, results = list(chunks) + [None] * len(pairs), [None] * n, {}
            groups = [list(range(k, self.wide, 2)) for k in range(2)]
            for i, (keep, at) in enumerate(pairs):
                vals[len(chunks) + i] = keep + got[at : at + keep.shape[0]]
            vals = [lax.psum(r, "wide", axis_index_groups=groups) for r in vals]
            theirs = [self.x(r) for r in vals]
            for c, hook in hooks.items():
                results[c] = hook(vals, theirs)
            results[None] = finish([lax.psum(pieces[0], "narrow")])
            return vals, theirs, results
        z = lax.axis_index("wide") // 2
        inner = ((z == 1) | (z == 2)).astype(jnp.int32).reshape(1)
        n_keep = 3
        n = len(chunks) + n_keep
        order = [*range(POS_A), len(chunks), *range(POS_A, len(chunks)), *range(len(chunks) + 1, n)]
        moved = [None] * n
        for c in order[:U_AHEAD]:
            moved[c] = self.inward(chunks[c])
        vals, theirs, results = list(chunks) + [None] * n_keep, [None] * n, {}
        tr = self.core(pieces[1])
        for s in range(n + LAGS[3]):
            if s == OUT_SLOTS[0]:
                tr = last = add(pieces[0], after(tr, last))
                ty = self.y(tr)
            if s == OUT_SLOTS[1]:
                tr = last = add(tr, after(ty, last))
                tc = self.core(tr)
            if s == OUT_SLOTS[2]:
                results[None] = finish([tr, after(tc, last)])
                last = results[None][0]
            if s in J_SLOTS:
                made = jobs[J_SLOTS.index(s)](last)
                last = made[0]
            if s == J_SLOTS[2]:
                *keeps, send = made
                got = self.x(send)
            if s == R_SLOT:
                got = after(got, last)
                sums = add_pieces(keeps, got)
                last = sums[0]
                for i, v in enumerate(sums):
                    vals[len(chunks) + i] = v
            for stage in range(4):
                c = s - LAGS[stage]
                if not 0 <= c < n:
                    continue
                c = order[c]
                if stage == 3:
                    theirs[c] = last = after(theirs[c], last)
                    if c in hooks:
                        results[c] = hooks[c](vals, theirs)
                        last = results[c][0]
                    continue
                new = after(moved[c], last)
                vals[c] = small_call(pick_kernel, [inner, vals[c], new], 1) if stage == 2 else add(vals[c], new)
                last = vals[c]
                if stage == 0:
                    moved[c] = self.middle(vals[c])
                    if s + U_AHEAD < n:
                        p = order[s + U_AHEAD]
                        moved[p] = self.inward(after(vals[p], last))
                elif stage == 1:
                    moved[c] = self.outward(vals[c])
                else:
                    theirs[c] = self.x(vals[c])
        return vals, theirs, results

    def gather_narrow(self, v):
        o = self.permute(v, lambda z, x, y, c: (z, x, 1 - y, c))
        p = self.permute(v, lambda z, x, y, c: (z, x, y, 1 - c))
        return [v, o, p, self.permute(o, lambda z, x, y, c: (z, x, y, 1 - c))]


def tie(*groups):
    return lax.optimization_barrier(groups)


def after(v, *deps):
    return lax.optimization_barrier((v, *deps))[0]


LAGS = (0, 1, 3, 4)
POS_A = 6
B_ROWS = 128
R_SLOT = 4
U_AHEAD = 2
J_SLOTS = (0, 1, 2)
OUT_SLOTS = (3, 6, 8)
CHUNKS = (240, 240, 240, 240, 240, 240)


def per_device(links, tokens, attn_in, attn_out, gate_weight, up_weight, down_weight, attn_gain, ffn_gain,
               cotangent, seq_ids, positions, valid_mask, group_owner):
    t, d = tokens.shape
    groups = attn_in.shape[0]
    f = gate_weight.shape[1]
    split = links.known
    member = lax.axis_index("narrow")
    xi = lax.axis_index("wide") % 2
    core = member % 2
    idx = jnp.stack([xi, core]).astype(jnp.int32)
    lane = jnp.arange(128, dtype=jnp.int32)
    half = HEAD // 2
    freq = THETA ** (-(lane % half).astype(F32) / half)
    angles = positions.astype(F32)[:, None] * freq[None, :]
    cs = jnp.cos(angles)
    sn = jnp.sin(angles) * jnp.where(lane % HEAD < half, -1.0, 1.0).astype(F32)[None, :]
    seqr, valr = seq_ids.reshape(1, t), valid_mask.reshape(1, t)
    g1, g2 = attn_gain.reshape(1, d), ffn_gain.reshape(1, d)
    win_t = jnp.swapaxes(attn_in, 1, 2)
    wd_t = down_weight.T

    th = t // 2
    sent = th if split else t
    wd = -(-d // 128) * 128
    piece = S((sent, wd), F32)
    sums = [S((th // 2, wd), F32)] * 2 if split else [S((th, wd), F32)]
    n_sums = len(sums)
    saved = [S((th, d), BF16), S((groups, th, 256), BF16), S((groups, th, 128), BF16), S((groups, th, 128), BF16),
             S((groups, th, 256), BF16), S((th, 128), F32), S((th, d), F32), S((th, d), BF16), S((th, 384), BF16)]
    scratch = [pltpu.VMEM((th, d), F32)] * 2 + [pltpu.VMEM((t, 128), BF16)] * 2
    weights = [win_t, attn_out, g1, g2, cs, sn, seqr, valr]
    ffn_w = [gate_weight, up_weight, wd_t]

    def forward(second, x, adds, old):
        part = old is not None
        outs = list(saved) + ([piece] if part else [])
        outs += [S((th, d), F32), S((th, f), BF16)] + ([piece] * n_sums if part else [S((th, d), F32)]) if second else [S((th, d), BF16)] + [S((th, f), F32)] * 2
        ins = [idx, x, *adds] + weights + ffn_w
        at = 2 + len(adds)
        ins += [old[2], old[3], old[7]] if part else []
        ins += [old[9]] if part and second else []
        ins += [cotangent] if second else []
        res = call(functools.partial(fwd_kernel, second, split, int(part), groups), outs + sums, ins, scratch, smem=1,
                   flops=4 * 10**9, grouped=[at, at + 1], first=[at + 4, at + 5],
                   late=[at + 4, at + 5, at + 8, at + 9, at + 10] + ([at + 13] if part else [])
                   + ([at + 14] if part and second else [])
                   + ([len(ins) - 1] if second else []))
        return list(res[:-n_sums]), list(res[-n_sums:])

    cot_rows = lax.dynamic_slice_in_dim(cotangent, core * sent, sent, 0) if split else cotangent
    cot_s = jnp.pad(cot_rows.astype(F32), ((0, 0), (0, wd - d)))

    tokens_t = tokens.T
    cot_x = links.x(cot_s)
    a1, s1a = forward(False, tokens_t, [], None)
    *a1, tok_a, gate1a, up1a = a1
    r1a = links.sum_cores(s1a)
    y1a = links.y_start(r1a)
    b1, s1b = forward(False, after(tokens_t, r1a), [], a1)
    *b1, n2as, tok_b, gate1b, up1b = b1
    s1b, n2as, y1a = tie(s1b, n2as, y1a)
    sum1a = links.sum_chips(r1a, y1a)
    r1b = links.sum_cores(s1b)
    y1b = links.y_start(r1b)
    n2a_x = links.x(n2as)
    a2, s2a = forward(True, after(a1[6], r1b), sum1a, None)
    *a2, x1a, duh2a, part2a = a2
    s2a, y1b, cot_x = tie(s2a, y1b, cot_x)
    sum1b = links.sum_chips(r1b, y1b)
    cot_p = links.both_cores(cot_x)
    r2a = links.sum_cores(s2a)
    y2a = links.y_start(r2a)
    b2, s2b = forward(True, after(b1[6], r2a, cot_p), sum1b, a2 + [part2a])
    b2, (n2bs, x1b, duh2b, *out2) = b2[:9], b2[9:]
    h2a, h2b = a2[6], b2[6]
    s2b, n2bs, y2a, n2a_x = tie(s2b, n2bs, y2a, n2a_x)
    n2a_p = links.both_cores(n2a_x)
    sum2a = links.sum_chips(r2a, y2a)
    r2b = links.sum_cores(s2b)
    y2b = links.y_start(r2b)
    n2b_x = links.x(n2bs)
    grad_outs = [S((d, f), F32), S((d, 384), F32)]
    gscratch = [pltpu.VMEM((t, d), BF16), pltpu.VMEM((t, d), BF16), pltpu.VMEM((t, f), BF16), pltpu.VMEM((t, 384), BF16)]

    tail = [cs, sn, seqr, valr]

    def backward_a(sums, dz, r):
        outs = [S((th, d), F32), S((th, d), BF16), S((groups, th, 128), BF16), S((groups, th, 128), F32),
                S((groups, 2, th, 128), F32), S((1, d), F32)]
        return call(
            functools.partial(bwd_a_kernel, split, groups), outs,
            [idx, *sums, dz, r[6], *r[1:6], attn_out, g2] + tail, smem=1, flops=4 * 10**9,
            grouped=[n_sums + 3, n_sums + 4, n_sums + 5, n_sums + 6, n_sums + 8], late=[n_sums + 7, n_sums + 10, n_sums + 11],
            first=[n_sums + 7, n_sums + 10, n_sums + 11],
        )

    def backward_b(last, sums, dz, first, ra, rb, xa, xb):
        outs = [S((th, d), BF16), S((groups, th, 320), BF16), S((groups, th, 320), BF16), S((1, d), F32), S((1, d), F32)]
        outs += [S((d, t), BF16)] if last else [S((th, d), F32), S((th, d), F32), piece]
        dha, _, dqxa, dqya, dkva, _ = first
        return call(
            functools.partial(bwd_b_kernel, last, split, groups), outs,
            [idx, *sums, dz, rb[6], *rb[1:6], xa, xb, ra[2], ra[3], dha, dqxa, dqya, dkva, win_t, attn_out, g1, g2] + tail,
            [pltpu.VMEM((th, d), F32)] * 3 + [pltpu.VMEM((2, t, 128), F32), pltpu.VMEM((t, 128), BF16),
             pltpu.VMEM((t, 128), BF16), pltpu.VMEM((th, 128), F32)],
            smem=1, flops=6 * 10**9,
            grouped=[n_sums + k for k in (3, 4, 5, 6, 10, 11, 13, 14, 15, 16, 17)],
            late=[n_sums + k for k in (7, 20, 21, 8, 9, 12)], first=[n_sums + 7, n_sums + 20, n_sums + 21],
        )

    acc = call(own_grads_kernel, grad_outs, [after(a2[7], r2b, sum2a), b2[7], duh2a, duh2b, a2[8], b2[8], cotangent],
               flops=2 * 10**9)
    first2 = backward_a(after(sum2a, acc), cotangent[:th], a2)
    first2, y2b = tie(first2, y2b)
    sum2b = links.sum_chips(r2b, y2b)
    da2b, dp2a, dp2b, dg1b, dg2b1, dz1a, dz1b, dfs = backward_b(
        False, sum2b, cotangent[th:], first2, a2, b2, x1a, x1b)
    dfs, dz1a, dz1b, n2b_x = tie(dfs, dz1a, dz1b, n2b_x)
    df_x = links.x(dfs)
    n2b_p = links.both_cores(n2b_x)
    da2a, dg2b0 = first2[1], first2[5]
    res = call(
        functools.partial(ffn_back_kernel, split), [S((th, f), BF16)] * 2 + [S((th, d), BF16)] * 2 + sums * 2,
        [idx, dz1a, dz1b, gate1a, gate1b, up1a, up1b] + ffn_w, [pltpu.VMEM((th, d), F32)], smem=1, flops=2 * 10**9,
        late=[1, 9, 3, 5, 7, 8, 2, 4, 6],
    )
    duh1, df1, s3 = res[:2], res[2:4], res[4:]
    r3a, r3b = links.sum_cores(s3[:n_sums]), links.sum_cores(s3[n_sums:])
    y3a, y3b = links.y_start(r3a), links.y_start(r3b)
    acc = call(
        functools.partial(both_grads_kernel, len(n2b_p)), grad_outs,
        [idx, *n2b_p, *cot_p, *ffn_w, after(a1[7], r3a, r3b), b1[7], *duh1, a1[8], b1[8], *df1, *acc], gscratch,
        flops=6 * 10**9, smem=1,
        late=[12 + 2 * len(n2b_p), 13 + 2 * len(n2b_p), *range(1, 2 * len(n2b_p) + 4)],
    )
    acc, df_x = tie(acc, df_x)
    df_p = links.both_cores(df_x)
    count = len(df_p)
    chunks = call(
        functools.partial(last_grads_kernel, count, len(CHUNKS)), [S((n, f), F32) for n in CHUNKS],
        [idx, *n2a_p, *df_p, *ffn_w, *acc], gscratch + [pltpu.VMEM((d, f), F32), pltpu.VMEM((d, 384), F32)],
        flops=4 * 10**9, smem=1, late=[2 * count + 4, 2 * count + 5],
    )
    quarter = 512 // links.narrow
    group_owner = after(group_owner, acc)
    order = jnp.arange(groups, dtype=jnp.int32)
    sharing = (group_owner[:, None] == group_owner[None, :]) & (order[None, :] < order[:, None])
    rank = jnp.sum(sharing.astype(jnp.int32), axis=1)
    first = jnp.sum(jnp.where((group_owner == member) & (rank == 0), order, 0))
    extra = jnp.sum(jnp.where(rank == 1, order, 0))
    extra_owner = jnp.sum(jnp.where(rank == 1, group_owner, 0))
    idx = jnp.stack([xi, core, first, extra, member, (extra_owner == member).astype(jnp.int32)]).astype(jnp.int32)
    chunks, y3a = tie(chunks, y3a)
    sum3a = links.sum_chips(r3a, y3a)
    lead = quarter // 2 + 8
    made = {}

    def job_a(dep):
        made["a"] = backward_a(after(sum3a, dep), dz1a, a1)
        return made["a"]

    def job_b(dep):
        first, got = tie(made["a"], y3b)
        sums = links.sum_chips(r3b, got)
        made["b"] = backward_b(True, after(sums, dep), dz1b, first, a1, b1, tok_a, tok_b)
        return made["b"]

    def job_grads(dep):
        first, (da1b, dp1a, dp1b, dg1a, dg2a1, _) = made["a"], made["b"]
        gains = jnp.concatenate([dg1a + dg1b, first[5] + dg2a1 + dg2b0 + dg2b1], axis=0)
        return call(
            attn_grad_kernel, [S((n, wd), F32) for n in (lead, B_ROWS, 256 - B_ROWS, lead + 256)],
            [idx, after(a1[0], dep), b1[0], a2[0], b2[0], dp1a, dp1b, dp2a, dp2b, a1[4], b1[4], a2[4], b2[4], first[1],
             da1b, da2a, da2b, gains],
            [pltpu.VMEM((512, d), F32), pltpu.VMEM((quarter + 16, d), F32)], smem=1, flops=2 * 10**9,
            picked=range(5, 13), late=range(13, 17),
        )

    def finish_out(pieces):
        return call(out_kernel, [S((d, t), BF16)], [idx, h2a, h2b, *pieces], [pltpu.VMEM((th, d), F32)], smem=1)

    nc = len(CHUNKS)
    ng = next(k for k in range(1, nc) if sum(CHUNKS[:k]) == d)

    def unpack(vals, theirs):
        return call(functools.partial(unpack_kernel, ng, False), [S((d, f), F32)] * 2,
                    [idx, *vals[:ng], *theirs[:ng]], smem=1,
                    late=[k for c in range(ng) for k in (1 + c, 1 + ng + c)])

    def unpack_down(vals, theirs):
        return call(functools.partial(unpack_kernel, nc - ng, True), [S((d, f), F32)],
                    [idx, *vals[ng:nc], *theirs[ng:nc]], smem=1,
                    late=[k for c in range(nc - ng) for k in (1 + c, 1 + nc - ng + c)])

    def collect(vals, theirs):
        r, o = vals[nc], theirs[nc]
        second = jnp.where(xi == 0, jnp.concatenate([r, o], 0), jnp.concatenate([o, r], 0))
        return second, links.gather_narrow(second[:quarter])

    done, theirs, results = links.sum_lines(
        chunks, [job_a, job_b, job_grads], out2, finish_out, {ng - 1: unpack, nc - 1: unpack_down, nc: collect})
    layer_out = results[None][0].T
    dx = made["b"][5].T
    ggate, gup = results[ng - 1]
    gdown, = results[nc - 1]
    second, slot1 = results[nc]
    small = second[quarter : quarter + 2, :d]
    gin, gout = call(
        functools.partial(attn_finish_kernel, links.narrow), [S((SLOTS, 320, d), F32), S((SLOTS, 192, d), F32)],
        [idx, *done[nc + 1 :], *theirs[nc + 1 :], *slot1], smem=1, late=[*range(5, 5 + len(slot1)), 1, 2, 3, 4],
    )
    gin = jnp.swapaxes(gin, 1, 2)
    return layer_out, dx, gin, gout, ggate, gup, gdown.T, small[0], small[1]


def _pad(outs, split):
    return list(outs) if split else list(outs) + [None]


def solution(mesh):
    in_specs = (P("wide", None), P(), P(), P(None, "narrow"), P(None, "narrow"), P("narrow", None), P(), P(),
                P("wide", None), P("wide"), P("wide"), P("wide"), P())
    out_specs = (P("wide", None), P("wide", None), P("narrow", None, None), P("narrow", None, None),
                 P(None, "narrow"), P(None, "narrow"), P("narrow", None), P(), P())
    return jax.shard_map(functools.partial(per_device, Links(mesh)), mesh=mesh, in_specs=in_specs,
                         out_specs=out_specs, check_vma=False)
```

```python
import functools
import math

import jax
import jax.numpy as jnp
from jax import lax
from jax.experimental import pallas as pl
from jax.experimental.pallas import tpu as pltpu
from jax.sharding import PartitionSpec as P

HEAD = 64
Q_PER = 3
SLOTS = 2
EPS = 1e-05
THETA = 10000.0
RB = 128
TR = 32
VMEM = 56
F32 = jnp.float32
BF16 = jnp.bfloat16
NEG = -1e30


def dot(a, b):
    return jnp.dot(a, b, preferred_element_type=F32)


def dot_nt(a, b):
    return lax.dot_general(a, b, (((1,), (1,)), ((), ())), preferred_element_type=F32)


def dot_tn(a, b):
    return lax.dot_general(a, b, (((0,), (0,)), ((), ())), preferred_element_type=F32)


def lane_iota(rows):
    return lax.broadcasted_iota(jnp.int32, (rows, 128), 1)


def low_half(rows):
    return lane_iota(rows) < HEAD


def rope128(v, cs, sn):
    lane = lane_iota(v.shape[0])
    partner = jnp.where((lane & 63) < 32, pltpu.roll(v, 96, 1), pltpu.roll(v, 32, 1))
    return v * cs + partner * sn


def allowed_bias(seqr_ref, valr_ref, r0, nk):
    t = r0 + lax.broadcasted_iota(jnp.int32, (RB, nk), 0)
    u = lax.broadcasted_iota(jnp.int32, (RB, nk), 1)
    mine = jnp.broadcast_to(seqr_ref[:, r0 : r0 + RB].astype(F32), (128, RB)).T[:, :1]
    same = mine == seqr_ref[:, :nk].astype(F32)
    ok = (same & (u <= t) & (valr_ref[:, :nk] == 1)) | (u == t)
    return jnp.where(ok, 0.0, NEG).astype(F32)


def masked_heads(x, y):
    low = low_half(1).astype(F32)
    low_b, high_b = low.astype(BF16), (1.0 - low).astype(BF16)
    return jnp.concatenate([x * low_b, x * high_b, y * low_b], axis=0)


def pack_half(xi, a, b):
    low = low_half(a.shape[0])
    at, bt = a[:, 512:], b[:, 512:]
    if xi == 0:
        return a[:, :256], b[:, :256], jnp.where(low, at, pltpu.roll(bt, 64, 1))
    return a[:, 256:512], b[:, 256:512], jnp.where(low, pltpu.roll(at, 64, 1), bt)


def store_pair(idx, ref, rows, a, b):
    for xi in range(2):
        @pl.when(idx[0] == xi)
        def _():
            p, q, r = pack_half(xi, a, b)
            ref[rows, :256] = p.astype(ref.dtype)
            ref[rows, 256:512] = q.astype(ref.dtype)
            ref[rows, 512:] = r.astype(ref.dtype)


def store_one(idx, ref, rows, a):
    low = low_half(a.shape[0])
    at = a[:, 512:]
    for xi in range(2):
        @pl.when(idx[0] == xi)
        def _():
            ref[rows, :256] = a[:, xi * 256 : xi * 256 + 256].astype(ref.dtype)
            ref[rows, 256:] = jnp.where(low, at if xi == 0 else pltpu.roll(at, 64, 1), 0.0).astype(ref.dtype)


def ffn_back(dhid, gate, up, sig):
    return dhid * up * sig * (1.0 + gate * (1.0 - sig)), dhid * (gate * sig)


def put_wide(ref, v):
    d = v.shape[1]
    ref[:, :d] = v
    if ref.shape[1] > d:
        ref[:, d:] = jnp.zeros((ref.shape[0], ref.shape[1] - d), ref.dtype)


def half_rows(ref, which, n):
    return ref[pl.ds(pl.multiple_of(which * n, 8), n), :]


def split_send(idx, whole, keep, send):
    n = keep.shape[0]
    put_wide(keep, half_rows(whole, idx[1], n))
    put_wide(send, half_rows(whole, 1 - idx[1], n))


def take_sum(idx, pieces, out):
    d = out.shape[1]
    if len(pieces) == 1:
        out[...] = pieces[0][:, :d]
        return
    n = pieces[0].shape[0]
    out[pl.ds(pl.multiple_of(idx[1] * n, n), n), :] = pieces[0][:, :d]
    out[pl.ds(pl.multiple_of((1 - idx[1]) * n, n), n), :] = pieces[1][:, :d]


class Late:
    def __init__(self, source, buffer, sems, at, grouped, pick=None):
        self.pick = pick
        self.source, self.buffer, self.sems, self.at, self.grouped = source, buffer, sems, at, grouped
        self.waited = False

    def copy(self, g=None):
        if g is None:
            return pltpu.make_async_copy(self.source, self.buffer, self.sems.at[self.at])
        source = g if self.pick is None else self.pick[2 + g]
        return pltpu.make_async_copy(self.source.at[source], self.buffer.at[g], self.sems.at[self.at + g])

    def start(self):
        self.copy().start()

    def wait(self):
        if not self.waited:
            self.copy().wait()
            self.waited = True
        return self.buffer


def ready(*refs):
    got = [r.wait() if isinstance(r, Late) else r for r in refs]
    return got if len(got) > 1 else got[0]


def ready_group(g, *refs):
    for r in refs:
        r.copy(g).wait()


def buffers(*refs):
    return [r.buffer for r in refs]


def fwd_kernel(second, split, part, groups, *refs):
    it = iter(refs)
    idx = next(it)
    x_ref = next(it)
    add_refs = [next(it) for _ in range(2 if split else 1)] if second else None
    win, wout, g1, g2, cs_ref, sn_ref, seqr, valr, wg, wu, wdt = (next(it) for _ in range(11))
    kt_old, vt_old, n2_old = (next(it) for _ in range(3)) if part else (None, None, None)
    part_old = next(it) if part and second else None
    cot = next(it) if second else None
    n1_ref, qk_ref, kt_ref, vt_ref, o_ref, lse_ref, h_ref, n2_ref, hidh_ref = (next(it) for _ in range(9))
    n2s_ref = next(it) if part else None
    x_out = next(it)
    if second:
        duh_ref, part_refs = next(it), [next(it) for _ in range(2 if part and split else 1)]
    outs = [next(it) for _ in range(2 if split else 1)]
    acc, whole, ktf, vtf = (next(it) for _ in range(4))
    t = n1_ref.shape[0]
    base = part * t

    if second:
        take_sum(idx, add_refs, acc)
        x = x_ref[...] + acc[...]
        x_out[...] = x
    else:
        x = x_ref[:, base : base + t].astype(F32).T
        x_out[...] = x.astype(BF16)
    r1 = lax.rsqrt(jnp.mean(x * x, axis=1, keepdims=True) + EPS)
    n1_ref[...] = (x * r1 * g1[...]).astype(BF16)
    acc[...] = x
    flush(n1_ref)
    flush(x_out)
    lse_ref[...] = jnp.zeros_like(lse_ref)
    cs_ref, sn_ref = ready(cs_ref, sn_ref)
    win_l, wout_l = win, wout
    win, wout = buffers(win, wout)

    def group(g, carry):
        ready_group(g, win_l, wout_l)
        n1 = n1_ref[...]
        qk = dot_nt(n1, win[g, :256, :])
        v = dot_nt(n1, win[g, 256:320, :])
        cs, sn = cs_ref[base : base + t, :], sn_ref[base : base + t, :]
        xr = rope128(qk[:, :128], cs, sn)
        yr = rope128(qk[:, 128:], cs, sn)
        qk_ref[g, :, :128] = xr.astype(BF16)
        qk_ref[g, :, 128:] = yr.astype(BF16)
        kt = jnp.where(low_half(t), pltpu.roll(yr, 64, 1), yr).astype(BF16)
        vt = jnp.concatenate([v, v], axis=1).astype(BF16)
        kt_ref[g] = kt
        vt_ref[g] = vt
        if part:
            ktf[:base, :] = kt_old[g]
            vtf[:base, :] = vt_old[g]
        ktf[base : base + t, :] = kt
        vtf[base : base + t, :] = vt
        for rb in range(t // RB):
            r0 = rb * RB
            nk = base + r0 + RB
            rows = slice(r0, r0 + RB)
            q = masked_heads(qk_ref[g, rows, :128], qk_ref[g, rows, 128:])
            s = dot_nt(q, ktf[:nk, :])
            bias = allowed_bias(seqr, valr, base + r0, nk)
            es, ms, lls = [], [], []
            for r in range(0, 3 * RB, TR):
                st = s[r : r + TR] * 0.125 + bias[r % RB : r % RB + TR]
                mt = jnp.max(st, axis=1, keepdims=True)
                et = jnp.exp(st - mt)
                ms.append(mt)
                lls.append(jnp.sum(et, axis=1, keepdims=True))
                es.append(et.astype(BF16))
            m, l = jnp.concatenate(ms, axis=0), jnp.concatenate(lls, axis=0)
            o = dot(jnp.concatenate(es, axis=0), vtf[:nk, :]) / l
            low = low_half(RB)
            o_ref[g, rows, :128] = jnp.where(low, o[:RB], o[RB : 2 * RB]).astype(BF16)
            o_ref[g, rows, 128:] = jnp.where(low, o[2 * RB :], 0.0).astype(BF16)
            ls = m + jnp.log(l)
            lane = lane_iota(RB)
            cur = lse_ref[rows, :]
            for j in range(3):
                cur = jnp.where(lane == g * 3 + j, ls[j * RB : (j + 1) * RB], cur)
            lse_ref[rows, :] = cur
        acc[...] += dot(o_ref[g, :, :192], wout[g])
        return carry

    lax.fori_loop(0, groups, group, 0)
    for ref in (qk_ref, kt_ref, vt_ref, o_ref, lse_ref):
        flush(ref)
    h = acc[...]
    h_ref[...] = h
    flush(h_ref)
    r2 = lax.rsqrt(jnp.mean(h * h, axis=1, keepdims=True) + EPS)
    n2 = (h * r2 * g2[...]).astype(BF16)
    n2_ref[...] = n2
    flush(n2_ref)
    if part:
        n2_old = ready(n2_old)
        if split:
            for c in range(2):
                @pl.when(idx[1] == c)
                def _():
                    put_wide(n2s_ref, (n2_old if c == 0 else n2_ref)[...].astype(F32))
        else:
            put_wide(n2s_ref.at[:t, :], n2_old[...].astype(F32))
            put_wide(n2s_ref.at[t:, :], n2_ref[...].astype(F32))
    if part:
        flush(n2s_ref)
    wg, wu, wdt = ready(wg, wu, wdt)
    every = slice(0, t)
    gate = dot(n2, wg[...])
    up = dot(n2, wu[...])
    sig = jax.nn.sigmoid(gate)
    hid = gate * sig * up
    store_one(idx, hidh_ref, every, hid)
    flush(hidh_ref)
    if second:
        cot = ready(cot)
        if part and split:
            part_old = ready(part_old)
            half = t // 2
            whole[...] = dot_nt(hid.astype(BF16), wdt[...])
            for ref, which in zip(part_refs, (idx[1], 1 - idx[1])):
                put_wide(ref.at[:half, :], half_rows(part_old, which, half))
                put_wide(ref.at[half:, :], half_rows(whole, which, half))
                flush(ref)
        elif part:
            part_old = ready(part_old)
            put_wide(part_refs[0].at[:t, :], part_old[...])
            put_wide(part_refs[0].at[t:, :], dot_nt(hid.astype(BF16), wdt[...]))
        else:
            part_refs[0][...] = dot_nt(hid.astype(BF16), wdt[...])
            flush(part_refs[0])
        dgate, dup = ffn_back(dot(cot[base : base + t, :], wdt[...]), gate, up, sig)
        store_pair(idx, duh_ref, every, dgate, dup)
        flush(duh_ref)
        whole[...] = dot_nt(dgate.astype(BF16), wg[...]) + dot_nt(dup.astype(BF16), wu[...])
    else:
        whole[...] = dot_nt(hid.astype(BF16), wdt[...])
    if split:
        split_send(idx, whole, *outs)
    else:
        put_wide(outs[0], whole[...])


def norm_back(dn, stream, gain):
    r = lax.rsqrt(jnp.mean(stream * stream, axis=1, keepdims=True) + EPS)
    m = stream * r
    dgain = jnp.sum(dn * m, axis=0, keepdims=True)
    dm = dn * gain
    return r * (dm - m * jnp.mean(dm * m, axis=1, keepdims=True)), dgain


def bwd_enter(idx, dn2_refs, dz_ref, h_ref, g2, dh_ref, da_ref, dg2_ref):
    take_sum(idx, dn2_refs, dh_ref)
    dh, dg2 = norm_back(dh_ref[...], h_ref[...], g2[...])
    dh = dz_ref[...].astype(F32) + dh
    dh_ref[...] = dh
    da_ref[...] = dh.astype(BF16)
    dg2_ref[...] = dg2


def bwd_block(g, r0, base, do, qk_ref, o_ref, lse_ref, ktf, vtf, seqr, valr, dkv):
    low, lane = low_half(RB), lane_iota(RB)
    nk = base + r0 + RB
    rows = slice(r0, r0 + RB)
    do = do[rows]
    dox = do[:, :128].astype(BF16)
    doy = jnp.concatenate([do[:, 128:192], jnp.zeros((RB, 64), F32)], axis=1).astype(BF16)
    px = dox.astype(F32) * o_ref[g, rows, :128].astype(F32)
    py = doy.astype(F32) * o_ref[g, rows, 128:].astype(F32)
    delta = jnp.concatenate(
        [
            jnp.sum(jnp.where(low, px, 0.0), axis=1, keepdims=True),
            jnp.sum(jnp.where(low, 0.0, px), axis=1, keepdims=True),
            jnp.sum(py, axis=1, keepdims=True),
        ],
        axis=0,
    )
    ls = lse_ref[rows, :]
    lse = jnp.concatenate(
        [jnp.sum(jnp.where(lane == g * 3 + j, ls, 0.0), axis=1, keepdims=True) for j in range(3)], axis=0
    )
    q = masked_heads(qk_ref[g, rows, :128], qk_ref[g, rows, 128:])
    dos = masked_heads(dox, doy)
    kt = ktf(nk)
    s = dot_nt(q, kt)
    dp = dot_nt(dos, vtf(nk))
    bias = allowed_bias(seqr, valr, base + r0, nk)
    ps, dss = [], []
    for r in range(0, 3 * RB, TR):
        part = slice(r, r + TR)
        pt = jnp.exp(s[part] * 0.125 + bias[r % RB : r % RB + TR] - lse[part])
        ps.append(pt.astype(BF16))
        dss.append((pt * (dp[part] - delta[part])).astype(BF16))
    p, ds = jnp.concatenate(ps, axis=0), jnp.concatenate(dss, axis=0)
    dq = dot(ds, kt) * 0.125
    dkv[0, :nk, :] += dot_tn(ds, q)
    dkv[1, :nk, :] += dot_tn(p, dos)
    return jnp.where(low, dq[:RB], dq[RB : 2 * RB]), dq[2 * RB :]


def bwd_a_kernel(split, groups, *refs):
    it = iter(refs)
    idx = next(it)
    dn2_refs = [next(it) for _ in range(2 if split else 1)]
    dz_ref, h_ref, qk_ref, kt_ref, vt_ref, o_ref, lse_ref, wout, g2, cs_ref, sn_ref, seqr, valr = (
        next(it) for _ in range(13))
    dh_ref, da_ref, dqx_ref, dqy_ref, dkv_ref, dg2_ref = (next(it) for _ in range(6))
    t = dh_ref.shape[0]
    bwd_enter(idx, dn2_refs, dz_ref, h_ref, g2, dh_ref, da_ref, dg2_ref)
    flush(dh_ref)
    flush(da_ref)
    dkv_ref[...] = jnp.zeros_like(dkv_ref)
    lse_ref, cs_ref, sn_ref = ready(lse_ref, cs_ref, sn_ref)
    waits = (qk_ref, kt_ref, vt_ref, o_ref, wout)
    qk_ref, kt_ref, vt_ref, o_ref, wout = buffers(*waits)

    def group(g, carry):
        ready_group(g, *waits)
        do = dot_nt(da_ref[...], wout[g])
        for r0 in range(0, t, RB):
            rows = slice(r0, r0 + RB)
            dqx, dqy = bwd_block(g, r0, 0, do, qk_ref, o_ref, lse_ref, lambda n: kt_ref[g, :n, :],
                                 lambda n: vt_ref[g, :n, :], seqr, valr, dkv_ref.at[g])
            dqx_ref[g, rows, :] = rope128(dqx, cs_ref[rows, :], -sn_ref[rows, :]).astype(BF16)
            dqy_ref[g, rows, :] = dqy
        return carry

    lax.fori_loop(0, groups, group, 0)


def bwd_b_kernel(last, split, groups, *refs):
    it = iter(refs)
    idx = next(it)
    dn2_refs = [next(it) for _ in range(2 if split else 1)]
    (dz_ref, h_ref, qk_ref, kt_ref, vt_ref, o_ref, lse_ref, xa_ref, xb_ref, kt_old, vt_old, dha_ref, dqxa_ref, dqya_ref,
     dkva_ref, win, wout, g1, g2, cs_ref, sn_ref, seqr, valr) = (next(it) for _ in range(23))
    da_ref, dpa_ref, dpb_ref, dg1_ref, dg2_ref, dxa_ref = (next(it) for _ in range(6))
    dxb_ref = None if last else next(it)
    dfs_ref = None if last else next(it)
    dh_ref, acca, accb, dkv, ktf, vtf, dqy_ref = (next(it) for _ in range(7))
    t = dh_ref.shape[0]
    bwd_enter(idx, dn2_refs, dz_ref, h_ref, g2, dh_ref, da_ref, dg2_ref)
    acca[...] = jnp.zeros_like(acca)
    flush(da_ref)
    accb[...] = jnp.zeros_like(accb)
    lse_ref, cs_ref, sn_ref = ready(lse_ref, cs_ref, sn_ref)
    waits = (qk_ref, kt_ref, vt_ref, o_ref, kt_old, vt_old, dqxa_ref, dqya_ref, dkva_ref, win, wout)
    qk_ref, kt_ref, vt_ref, o_ref, kt_old, vt_old, dqxa_ref, dqya_ref, dkva_ref, win, wout = buffers(*waits)

    def group(g, carry):
        ready_group(g, *waits)
        do = dot_nt(da_ref[...], wout[g])
        ktf[:t, :] = kt_old[g]
        ktf[t:, :] = kt_ref[g]
        vtf[:t, :] = vt_old[g]
        vtf[t:, :] = vt_ref[g]
        dkv[:, :t, :] = dkva_ref[g]
        dkv[:, t:, :] = jnp.zeros((2, t, 128), F32)
        for r0 in range(0, t, RB):
            rows = slice(r0, r0 + RB)
            dqx, dqy = bwd_block(g, r0, t, do, qk_ref, o_ref, lse_ref, lambda n: ktf[:n, :], lambda n: vtf[:n, :],
                                 seqr, valr, dkv)
            full = slice(t + r0, t + r0 + RB)
            dpb_ref[g, rows, :128] = rope128(dqx, cs_ref[full, :], -sn_ref[full, :]).astype(BF16)
            dqy_ref[rows, :] = dqy
        dpa_ref[g, :, :128] = dqxa_ref[g]
        low = low_half(t)
        for k, (ref, dqy) in enumerate(((dpa_ref, dqya_ref[g]), (dpb_ref, dqy_ref[...]))):
            rows = slice(k * t, k * t + t)
            dk, dv = dkv[0, rows, :], dkv[1, rows, :]
            dk = (dk + pltpu.roll(dk, 64, 1)) * 0.125
            dv = dv + pltpu.roll(dv, 64, 1)
            dy = jnp.where(low, dqy, dk)
            ref[g, :, 128:256] = rope128(dy, cs_ref[rows, :], -sn_ref[rows, :]).astype(BF16)
            ref[g, :, 256:320] = dv[:, :64].astype(BF16)
        both = dot(jnp.concatenate([dpa_ref[g], dpb_ref[g]], axis=0), win[g])
        acca[...] += both[:t]
        accb[...] += both[t:]
        return carry

    lax.fori_loop(0, groups, group, 0)
    flush(dpa_ref)
    flush(dpb_ref)
    xa_ref, xb_ref, dha_ref = ready(xa_ref, xb_ref, dha_ref)
    dxa, dg1a = norm_back(acca[...], xa_ref[...].astype(F32), g1[...])
    dxb, dg1b = norm_back(accb[...], xb_ref[...].astype(F32), g1[...])
    dg1_ref[...] = dg1a + dg1b
    if last:
        dxa_ref[:, :t] = (dxa + dha_ref[...]).T.astype(BF16)
        dxa_ref[:, t:] = (dxb + dh_ref[...]).T.astype(BF16)
    else:
        dxa_ref[...] = dxa + dha_ref[...]
        dxb_ref[...] = dxb + dh_ref[...]
        flush(dxa_ref)
        flush(dxb_ref)
    if not last:
        if split:
            for c in range(2):
                @pl.when(idx[1] == c)
                def _():
                    put_wide(dfs_ref, (dxa_ref if c == 0 else dxb_ref)[...].astype(BF16).astype(F32))
        else:
            put_wide(dfs_ref.at[:t, :], dxa_ref[...].astype(BF16).astype(F32))
            put_wide(dfs_ref.at[t:, :], dxb_ref[...].astype(BF16).astype(F32))


def ffn_back_kernel(split, *refs):
    idx, dza, dzb, n2a, n2b, wg, wu, wdt, duha, duhb, dfa, dfb, *rest = refs
    outs, whole = rest[:-1], rest[-1]
    per = len(outs) // 2
    for k, (dz_ref, n2_ref, duh_ref, df_ref) in enumerate(
            ((dza, n2a, duha, dfa), (dzb, n2b, duhb, dfb))):
        df = ready(dz_ref)[...].astype(BF16)
        df_ref[...] = df
        flush(df_ref)
        n2_ref, wg, wu = ready(n2_ref, wg, wu)
        gate, up = dot(n2_ref[...], wg[...]), dot(n2_ref[...], wu[...])
        wdt = ready(wdt)
        dgate, dup = ffn_back(dot(df, wdt[...]), gate, up, jax.nn.sigmoid(gate))
        store_pair(idx, duh_ref, slice(0, df.shape[0]), dgate, dup)
        flush(duh_ref)
        whole[...] = dot_nt(dgate.astype(BF16), wg[...]) + dot_nt(dup.astype(BF16), wu[...])
        if split:
            split_send(idx, whole, *outs[per * k : per * k + per])
        else:
            put_wide(outs[k], whole[...])
        for ref in outs[per * k : per * k + per]:
            flush(ref)


def own_grads(n2, duh, hidh, df, base, put):
    for r in range(0, n2[0].shape[1], 320):
        put(0, r, sum((dot_tn(a[:, r : r + 320], b[...]) for a, b in zip(n2, duh)), base(0, r)))
        put(1, r, sum((dot_tn(a[:, r : r + 320], b[...]) for a, b in zip(df, hidh)), base(1, r)))


def peer_acts(xi, n2, df, wg, wu, wdt, du, hd, rows):
    half = pl.ds(pl.multiple_of(xi * 256, 128), 256)
    last = slice(512, 640)

    def own_half(v):
        return jnp.where(xi == 0, v, pltpu.roll(v, 64, 1))

    ga, gb = dot(n2, wg[:, half]), own_half(dot(n2, wg[:, last]))
    ua, ub = dot(n2, wu[:, half]), own_half(dot(n2, wu[:, last]))
    dha, dhb = dot(df, wdt[:, half]), own_half(dot(df, wdt[:, last]))
    sa, sb = jax.nn.sigmoid(ga), jax.nn.sigmoid(gb)
    low = low_half(n2.shape[0])
    hd[rows, :256] = (ga * sa * ua).astype(BF16)
    hd[rows, 256:] = jnp.where(low, gb * sb * ub, 0.0).astype(BF16)
    dga, dua = ffn_back(dha, ga, ua, sa)
    dgb, dub = ffn_back(dhb, gb, ub, sb)
    du[rows, :256] = dga.astype(BF16)
    du[rows, 256:512] = dua.astype(BF16)
    du[rows, 512:] = jnp.where(low, dgb, pltpu.roll(dub, 64, 1)).astype(BF16)


def peer_grads(xi, n2p, dfp, weights, scratch, base, put):
    n2, df, du, hd = scratch
    d = n2.shape[1]
    n = n2p[0].shape[0]
    for i in range(len(n2p)):
        rows = slice(i * n, i * n + n)
        n2[rows, :] = n2p[i][:, :d].astype(BF16)
        df[rows, :] = dfp[i][:, :d].astype(BF16)
        for r in range(i * n, i * n + n, 256):
            part = slice(r, r + 256)
            peer_acts(xi, n2[part, :], df[part, :], *weights, du, hd, part)
    own_grads([n2], [du], [hd], [df], base, put)


def own_grads_kernel(*refs):
    n2, duh, hidh, cot, outs = refs[:2], refs[2:4], refs[4:6], refs[6], refs[7:]
    t = n2[0].shape[0]

    def put(k, r, v):
        outs[k][r : r + 320, :] = v
        flush(outs[k], slice(r, r + 320))

    own_grads(n2, duh, hidh, [cot.at[:t, :], cot.at[t:, :]], lambda k, r: 0.0, put)


def both_grads_kernel(count, *refs):
    idx, refs = refs[0], refs[1:]
    n2p, dfp = refs[:count], refs[count : 2 * count]
    wg, wu, wdt, *rest = refs[2 * count :]
    n2, duh, hidh, df = (rest[2 * k : 2 * k + 2] for k in range(4))
    old, outs, scratch = rest[8:10], rest[10:12], rest[12:]

    def put(k, r, v):
        outs[k][r : r + 320, :] = v

    def put_last(k, r, v):
        outs[k][r : r + 320, :] = v
        flush(outs[k], slice(r, r + 320))

    old = ready(*old)
    own_grads(n2, duh, hidh, df, lambda k, r: old[k][r : r + 320, :], put)
    n2p, dfp = [ready(r) for r in n2p], [ready(r) for r in dfp]
    weights = ready(wg, wu, wdt)
    peer_grads(idx[0], n2p, dfp, weights, scratch, lambda k, r: outs[k][r : r + 320, :], put_last)


def last_grads_kernel(count, n_chunks, *refs):
    idx, refs = refs[0], refs[1:]
    n2p, dfp = refs[:count], refs[count : 2 * count]
    wg, wu, wdt, *rest = refs[2 * count :]
    old, chunks, scratch = rest[:2], rest[2 : 2 + n_chunks], rest[2 + n_chunks : 6 + n_chunks]
    gu, dn = rest[6 + n_chunks :]

    def put(k, r, v):
        (gu, dn)[k][r : r + 320, :] = v

    peer_grads(idx[0], n2p, dfp, (wg, wu, wdt), scratch, lambda k, r: ready(old[k])[r : r + 320, :], put)
    at = 0
    half = dn.shape[0] // 2
    for out in chunks:
        n = out.shape[0]
        if at < gu.shape[0]:
            out[...] = gu[at : at + n, :]
        else:
            r = at - gu.shape[0]
            a, b = dn[r : r + n, :], dn[half + r : half + r + n, :]
            out[:, :256] = a[:, :256]
            out[:, 256:512] = b[:, :256]
            out[:, 512:] = jnp.where(low_half(n), a[:, 256:], pltpu.roll(b[:, 256:], 64, 1))
        flush(out)
        at += n


def unpack_kernel(count, stacked, *refs):
    idx = refs[0]
    own, other, outs = refs[1 : 1 + count], refs[1 + count : 1 + 2 * count], refs[1 + 2 * count :]
    at = 0
    for o, p in zip(own, other):
        o, p = ready(o, p)
        n = o.shape[0]
        for xi in range(2):
            @pl.when(idx[0] == xi)
            def _():
                a, b = (o, p) if xi == 0 else (p, o)
                low = low_half(n)
                at4, bt4 = a[:, 512:], b[:, 512:]
                firsts = jnp.where(low, at4, pltpu.roll(bt4, 64, 1))
                seconds = jnp.where(low, pltpu.roll(at4, 64, 1), bt4)
                for k, tile in ((0, firsts), (1, seconds)):
                    ref = outs[0] if stacked else outs[k]
                    r = at + (k * (ref.shape[0] // 2) if stacked else 0)
                    ref[r : r + n, :256] = a[:, 256 * k : 256 * k + 256]
                    ref[r : r + n, 256:512] = b[:, 256 * k : 256 * k + 256]
                    ref[r : r + n, 512:] = tile
        for k in range(2):
            ref = outs[0] if stacked else outs[k]
            r = at + (k * (ref.shape[0] // 2) if stacked else 0)
            flush(ref, slice(r, r + n))
        at += n


def attn_grad_kernel(idx, *refs):
    n1, dp, o, da = (refs[4 * k : 4 * k + 4] for k in range(4))
    da = [ready(v) for v in da]
    gains, keep2, keep0, keep1, send, whole, extra = refs[16:]

    def grads(g, out, at):
        ready_group(g, *dp)
        out[at : at + 320, :] = sum(dot_tn(p[g], n[...]) for p, n in zip(buffers(*dp), n1))
        ready_group(g, *o)
        out[at + 320 : at + 512, :] = sum(dot_tn(v[g, :, :192], a[...]) for v, a in zip(buffers(*o), da))

    grads(0, whole, 0)
    half = whole.shape[0] // 2
    lead = send.shape[0] - half
    for at, ref in ((0, keep0), (keep0.shape[0], keep1)):
        put_wide(ref, whole[pl.ds(pl.multiple_of(idx[0] * half + at, 8), ref.shape[0]), :])
    put_wide(send.at[lead:, :], half_rows(whole, 1 - idx[0], half))
    grads(1, whole, 0)
    rows_in, rows_out = 320 // idx_parts(extra), 192 // idx_parts(extra)
    extra[:rows_in, :] = whole[pl.ds(pl.multiple_of(idx[4] * rows_in, 8), rows_in), :]
    extra[rows_in : rows_in + rows_out, :] = whole[pl.ds(pl.multiple_of(320 + idx[4] * rows_out, 8), rows_out), :]
    n = rows_in + rows_out
    extra[n:, :] = jnp.zeros((extra.shape[0] - n, extra.shape[1]), F32)
    extra[n : n + 2, :] = gains[...]
    half = extra.shape[0] // 2
    put_wide(keep2, half_rows(extra, idx[0], half))
    put_wide(send.at[:lead, :], half_rows(extra, 1 - idx[0], half))


def out_kernel(idx, ha, hb, *refs):
    pieces, out, whole = refs[:-2], refs[-2], refs[-1]
    t, d = ha.shape
    half = t // len(pieces)
    for k, h in enumerate((ha, hb)):
        if len(pieces) == 1:
            whole[...] = pieces[0][k * t : k * t + t, :d]
        else:
            rows = slice(k * half, k * half + half)
            whole[pl.ds(pl.multiple_of(idx[1] * half, half), half), :] = pieces[0][rows, :d]
            whole[pl.ds(pl.multiple_of((1 - idx[1]) * half, half), half), :] = pieces[1][rows, :d]
        out[:, k * t : k * t + t] = (whole[...] + h[...]).T.astype(BF16)


def attn_finish_kernel(parts, idx, a0, a1, b0, b1, *rest):
    slot1, gin, gout = rest[:-2], *rest[-2:]
    d = gin.shape[2]
    mine = idx[5].astype(F32)
    rows_in, rows_out = 320 // parts, 192 // parts
    for k, quarter in enumerate(slot1):
        quarter = ready(quarter)
        m = (idx[4] // 2 * (1 - k % 2) + (1 - idx[4] // 2) * (k % 2)) * 2 + (
            idx[4] % 2 * (1 - k // 2) + (1 - idx[4] % 2) * (k // 2))
        gin[1, pl.ds(pl.multiple_of(m * rows_in, 8), rows_in), :] = quarter[:rows_in, :d] * mine
        gout[1, pl.ds(pl.multiple_of(m * rows_out, 8), rows_out), :] = (
            quarter[rows_in : rows_in + rows_out, :d] * mine)
    flush(gin, slice(1, 2))
    flush(gout, slice(1, 2))
    a0, a1, b0, b1 = ready(a0, a1, b0, b1)
    for xi in range(2):
        @pl.when(idx[0] == xi)
        def _():
            p0, p1, q0, q1 = (a0, a1, b0, b1) if xi == 0 else (b0, b1, a0, a1)
            n = p0.shape[0]
            gin[0, :n, :] = p0[:, :d]
            gin[0, n:256, :] = p1[:, :d]
            gin[0, 256:, :] = q0[:64, :d]
            gout[0, : n - 64, :] = q0[64:, :d]
            gout[0, n - 64 :, :] = q1[:, :d]
    flush(gin, slice(0, 1))
    flush(gout, slice(0, 1))


def idx_parts(extra):
    return 512 // (extra.shape[0] - 16)


BIG = 32 * 1024
OUT = {}


def flush(ref, rows=None):
    out, sem, whole = OUT[id(ref)]
    part = ref if rows is None else ref.at[rows, :]
    to = out if rows is None else out.at[rows, :]
    pltpu.make_async_copy(part, to, sem).start()
    OUT[id(ref)] = (out, sem, True)


def size(a):
    return math.prod(a.shape) * jnp.dtype(a.dtype).itemsize


def call(kernel, outs, ins, scratch=(), smem=0, flops=0, late=(), grouped=(), first=(), picked=()):
    n_in, n_out = len(ins), len(outs)
    big_in = [i for i in range(smem, n_in) if size(ins[i]) >= BIG]
    big_out = [i for i in range(n_out) if size(outs[i]) >= BIG]
    in_specs = [
        pl.BlockSpec(memory_space=pltpu.SMEM if i < smem else pl.ANY if i in big_in else pltpu.VMEM) for i in range(n_in)
    ]
    out_specs = [pl.BlockSpec(memory_space=pl.ANY if i in big_out else pltpu.VMEM) for i in range(n_out)]
    buffers = [pltpu.VMEM((2, *ins[i].shape[1:]) if i in picked else ins[i].shape, ins[i].dtype) for i in big_in]
    buffers += [pltpu.VMEM(outs[i].shape, outs[i].dtype) for i in big_out]
    at, n_sems = {}, 0
    for i in big_in:
        at[i] = n_sems
        n_sems += ins[i].shape[0] if i in grouped else 2 if i in picked else 1
    out_at = n_sems
    sems = pltpu.SemaphoreType.DMA((n_sems + len(big_out),))

    def body(*refs):
        ins_, outs_, rest = list(refs[:n_in]), list(refs[n_in : n_in + n_out]), list(refs[n_in + n_out :])
        own, (bufs, sem) = rest[: len(scratch)], (rest[len(scratch) : -1], rest[-1])
        kept = []
        for k, i in enumerate(big_in):
            pick = ins_[0] if i in picked else None
            kept.append((i, Late(ins_[i], bufs[k], sem, at[i], i in grouped or i in picked, pick)))
        items = dict(kept)
        for i in big_in:
            if i not in late and i not in grouped and i not in picked:
                items[i].start()
        for i in first:
            items[i].start()
        for g in range(2):
            for i in picked:
                items[i].copy(g).start()
        for g in range(max((ins[i].shape[0] for i in grouped), default=0)):
            for i in grouped:
                items[i].copy(g).start()
        for i in late:
            if i in items and i not in first:
                items[i].start()
        for i, item in kept:
            early = i not in late and i not in grouped and i not in picked
            ins_[i] = item.wait() if early else item
        OUT.clear()
        for k, i in enumerate(big_out):
            buf = bufs[len(big_in) + k]
            OUT[id(buf)] = (outs_[i], sem.at[out_at + k], False)
            outs_[i] = buf
        kernel(*ins_, *outs_, *own)
        for i in big_out:
            if not OUT[id(outs_[i])][2]:
                flush(outs_[i])
        for i, item in kept:
            assert item.grouped or item.waited
        for i in big_out:
            out, s, _ = OUT[id(outs_[i])]
            pltpu.make_async_copy(outs_[i], out, s).wait()
        OUT.clear()

    return pl.pallas_call(
        body,
        out_shape=tuple(outs),
        in_specs=in_specs,
        out_specs=tuple(out_specs),
        scratch_shapes=list(scratch) + buffers + [sems],
        compiler_params=pltpu.CompilerParams(vmem_limit_bytes=VMEM * 1024 * 1024),
        cost_estimate=pl.CostEstimate(flops=1, bytes_accessed=1, transcendentals=0),
    )(*ins)


def S(shape, dtype):
    return jax.ShapeDtypeStruct(shape, dtype)


def add_kernel(a, b, out):
    out[...] = a[...] + b[...]


def pick_kernel(flag, a, b, out):
    @pl.when(flag[0] == 1)
    def _():
        out[...] = a[...]

    @pl.when(flag[0] != 1)
    def _():
        out[...] = b[...]


def small_call(kernel, ins, smem=0):
    a = ins[-1]
    return pl.pallas_call(
        kernel,
        out_shape=jax.ShapeDtypeStruct(a.shape, a.dtype),
        in_specs=[pl.BlockSpec(memory_space=pltpu.SMEM)] * smem + [pl.BlockSpec(memory_space=pltpu.VMEM)] * 2,
        out_specs=pl.BlockSpec(memory_space=pltpu.VMEM),
        compiler_params=pltpu.CompilerParams(vmem_limit_bytes=8 * 2**20),
        cost_estimate=pl.CostEstimate(flops=1, bytes_accessed=1, transcendentals=0),
    )(*ins)


def add(a, b):
    return small_call(add_kernel, [a, b])


def add_pieces(keeps, got):
    def kernel(*refs):
        n = len(keeps)
        at = 0
        for keep, out in zip(refs[:n], refs[n + 1 :]):
            out[...] = keep[...] + refs[n][at : at + keep.shape[0], :]
            at += keep.shape[0]

    return pl.pallas_call(
        kernel,
        out_shape=tuple(jax.ShapeDtypeStruct(k.shape, k.dtype) for k in keeps),
        compiler_params=pltpu.CompilerParams(vmem_limit_bytes=12 * 2**20),
        cost_estimate=pl.CostEstimate(flops=1, bytes_accessed=1, transcendentals=0),
    )(*keeps, got)


class Links:
    def __init__(self, mesh):
        self.wide, self.narrow = mesh.shape["wide"], mesh.shape["narrow"]
        self.known = (self.wide, self.narrow) == (8, 4)

    def permute(self, v, step):
        pairs = []
        for w in range(self.wide):
            for n in range(self.narrow):
                to = step(w // 2, w % 2, n // 2, n % 2)
                if to is not None:
                    z, x, y, c = to
                    pairs.append((w * self.narrow + n, (z * 2 + x) * self.narrow + y * 2 + c))
        return lax.ppermute(v, ("wide", "narrow"), pairs)

    def core(self, v):
        return self.permute(v, lambda z, x, y, c: (z, x, y, 1 - c))

    def y(self, v):
        return self.permute(v, lambda z, x, y, c: (z, x, 1 - y, c))

    def x(self, v):
        return self.permute(v, lambda z, x, y, c: (z, 1 - x, y, c))

    def inward(self, v):
        return self.permute(v, lambda z, x, y, c: ({0: 1, 3: 2}[z], x, y, c) if z in (0, 3) else None)

    def outward(self, v):
        return self.permute(v, lambda z, x, y, c: ({1: 0, 2: 3}[z], x, y, c) if z in (1, 2) else None)

    def middle(self, v):
        return self.permute(v, lambda z, x, y, c: (3 - z, x, y, c) if z in (1, 2) else None)

    def sum_cores(self, pieces):
        return add(pieces[0], self.core(pieces[1])) if self.known else pieces[0]

    def y_start(self, r):
        return self.y(r) if self.known else r

    def sum_chips(self, r, got):
        if not self.known:
            return [lax.psum(r, "narrow")]
        r = add(r, got)
        return [r, self.core(r)]

    def both_cores(self, got):
        return [got, self.core(got)] if self.known else [got]

    def sum_lines(self, chunks, jobs, pieces, finish, hooks):
        last = chunks[0]
        if not self.known:
            for job in jobs:
                last = job(last)
            *keeps, send = last
            n = len(chunks) + len(keeps)
            got = self.x(send)
            pairs, at = [], 0
            for keep in keeps:
                pairs.append((keep, at))
                at += keep.shape[0]
            vals, theirs, results = list(chunks) + [None] * len(pairs), [None] * n, {}
            groups = [list(range(k, self.wide, 2)) for k in range(2)]
            for i, (keep, at) in enumerate(pairs):
                vals[len(chunks) + i] = keep + got[at : at + keep.shape[0]]
            vals = [lax.psum(r, "wide", axis_index_groups=groups) for r in vals]
            theirs = [self.x(r) for r in vals]
            for c, hook in hooks.items():
                results[c] = hook(vals, theirs)
            results[None] = finish([lax.psum(pieces[0], "narrow")])
            return vals, theirs, results
        z = lax.axis_index("wide") // 2
        inner = ((z == 1) | (z == 2)).astype(jnp.int32).reshape(1)
        n_keep = 3
        n = len(chunks) + n_keep
        order = [*range(POS_A), len(chunks), *range(POS_A, len(chunks)), *range(len(chunks) + 1, n)]
        moved = [None] * n
        for c in order[:U_AHEAD]:
            moved[c] = self.inward(chunks[c])
        vals, theirs, results = list(chunks) + [None] * n_keep, [None] * n, {}
        tr = self.core(pieces[1])
        for s in range(n + LAGS[3]):
            if s == OUT_SLOTS[0]:
                tr = last = add(pieces[0], after(tr, last))
                ty = self.y(tr)
            if s == OUT_SLOTS[1]:
                tr = last = add(tr, after(ty, last))
                tc = self.core(tr)
            if s == OUT_SLOTS[2]:
                results[None] = finish([tr, after(tc, last)])
                last = results[None][0]
            if s in J_SLOTS:
                made = jobs[J_SLOTS.index(s)](last)
                last = made[0]
            if s == J_SLOTS[2]:
                *keeps, send = made
                got = self.x(send)
            if s == R_SLOT:
                got = after(got, last)
                sums = add_pieces(keeps, got)
                last = sums[0]
                for i, v in enumerate(sums):
                    vals[len(chunks) + i] = v
            for stage in range(4):
                c = s - LAGS[stage]
                if not 0 <= c < n:
                    continue
                c = order[c]
                if stage == 3:
                    theirs[c] = last = after(theirs[c], last)
                    if c in hooks:
                        results[c] = hooks[c](vals, theirs)
                        last = results[c][0]
                    continue
                new = after(moved[c], last)
                vals[c] = small_call(pick_kernel, [inner, vals[c], new], 1) if stage == 2 else add(vals[c], new)
                last = vals[c]
                if stage == 0:
                    moved[c] = self.middle(vals[c])
                    if s + U_AHEAD < n:
                        p = order[s + U_AHEAD]
                        moved[p] = self.inward(after(vals[p], last))
                elif stage == 1:
                    moved[c] = self.outward(vals[c])
                else:
                    theirs[c] = self.x(vals[c])
        return vals, theirs, results

    def gather_narrow(self, v):
        o = self.permute(v, lambda z, x, y, c: (z, x, 1 - y, c))
        p = self.permute(v, lambda z, x, y, c: (z, x, y, 1 - c))
        return [v, o, p, self.permute(o, lambda z, x, y, c: (z, x, y, 1 - c))]


def tie(*groups):
    return lax.optimization_barrier(groups)


def after(v, *deps):
    return lax.optimization_barrier((v, *deps))[0]


LAGS = (0, 1, 3, 4)
POS_A = 6
B_ROWS = 128
R_SLOT = 4
U_AHEAD = 2
J_SLOTS = (0, 1, 2)
OUT_SLOTS = (3, 6, 8)
CHUNKS = (240, 240, 240, 240, 240, 240)


def per_device(links, tokens, attn_in, attn_out, gate_weight, up_weight, down_weight, attn_gain, ffn_gain,
               cotangent, seq_ids, positions, valid_mask, group_owner):
    t, d = tokens.shape
    groups = attn_in.shape[0]
    f = gate_weight.shape[1]
    split = links.known
    member = lax.axis_index("narrow")
    xi = lax.axis_index("wide") % 2
    core = member % 2
    idx = jnp.stack([xi, core]).astype(jnp.int32)
    lane = jnp.arange(128, dtype=jnp.int32)
    half = HEAD // 2
    freq = THETA ** (-(lane % half).astype(F32) / half)
    angles = positions.astype(F32)[:, None] * freq[None, :]
    cs = jnp.cos(angles)
    sn = jnp.sin(angles) * jnp.where(lane % HEAD < half, -1.0, 1.0).astype(F32)[None, :]
    seqr, valr = seq_ids.reshape(1, t), valid_mask.reshape(1, t)
    g1, g2 = attn_gain.reshape(1, d), ffn_gain.reshape(1, d)
    win_t = jnp.swapaxes(attn_in, 1, 2)
    wd_t = down_weight.T

    th = t // 2
    sent = th if split else t
    wd = -(-d // 128) * 128
    piece = S((sent, wd), F32)
    sums = [S((th // 2, wd), F32)] * 2 if split else [S((th, wd), F32)]
    n_sums = len(sums)
    saved = [S((th, d), BF16), S((groups, th, 256), BF16), S((groups, th, 128), BF16), S((groups, th, 128), BF16),
             S((groups, th, 256), BF16), S((th, 128), F32), S((th, d), F32), S((th, d), BF16), S((th, 384), BF16)]
    scratch = [pltpu.VMEM((th, d), F32)] * 2 + [pltpu.VMEM((t, 128), BF16)] * 2
    weights = [win_t, attn_out, g1, g2, cs, sn, seqr, valr]
    ffn_w = [gate_weight, up_weight, wd_t]

    def forward(second, x, adds, old):
        part = old is not None
        outs = list(saved) + ([piece] if part else [])
        outs += [S((th, d), F32), S((th, f), BF16)] + ([piece] * n_sums if part else [S((th, d), F32)]) if second else [S((th, d), BF16)]
        ins = [idx, x, *adds] + weights + ffn_w
        at = 2 + len(adds)
        ins += [old[2], old[3], old[7]] if part else []
        ins += [old[9]] if part and second else []
        ins += [cotangent] if second else []
        res = call(functools.partial(fwd_kernel, second, split, int(part), groups), outs + sums, ins, scratch, smem=1,
                   flops=4 * 10**9, grouped=[at, at + 1], first=[at + 4, at + 5],
                   late=[at + 4, at + 5, at + 8, at + 9, at + 10] + ([at + 13] if part else [])
                   + ([at + 14] if part and second else [])
                   + ([len(ins) - 1] if second else []))
        return list(res[:-n_sums]), list(res[-n_sums:])

    cot_rows = lax.dynamic_slice_in_dim(cotangent, core * sent, sent, 0) if split else cotangent
    cot_s = jnp.pad(cot_rows.astype(F32), ((0, 0), (0, wd - d)))

    tokens_t = tokens.T
    cot_x = links.x(cot_s)
    a1, s1a = forward(False, tokens_t, [], None)
    *a1, tok_a = a1
    r1a = links.sum_cores(s1a)
    y1a = links.y_start(r1a)
    b1, s1b = forward(False, after(tokens_t, r1a), [], a1)
    *b1, n2as, tok_b = b1
    s1b, n2as, y1a = tie(s1b, n2as, y1a)
    sum1a = links.sum_chips(r1a, y1a)
    r1b = links.sum_cores(s1b)
    y1b = links.y_start(r1b)
    n2a_x = links.x(n2as)
    a2, s2a = forward(True, after(a1[6], r1b), sum1a, None)
    *a2, x1a, duh2a, part2a = a2
    s2a, y1b, cot_x = tie(s2a, y1b, cot_x)
    sum1b = links.sum_chips(r1b, y1b)
    cot_p = links.both_cores(cot_x)
    r2a = links.sum_cores(s2a)
    y2a = links.y_start(r2a)
    b2, s2b = forward(True, after(b1[6], r2a, cot_p), sum1b, a2 + [part2a])
    b2, (n2bs, x1b, duh2b, *out2) = b2[:9], b2[9:]
    h2a, h2b = a2[6], b2[6]
    s2b, n2bs, y2a, n2a_x = tie(s2b, n2bs, y2a, n2a_x)
    n2a_p = links.both_cores(n2a_x)
    sum2a = links.sum_chips(r2a, y2a)
    r2b = links.sum_cores(s2b)
    y2b = links.y_start(r2b)
    n2b_x = links.x(n2bs)
    grad_outs = [S((d, f), F32), S((d, 384), F32)]
    gscratch = [pltpu.VMEM((t, d), BF16), pltpu.VMEM((t, d), BF16), pltpu.VMEM((t, f), BF16), pltpu.VMEM((t, 384), BF16)]

    tail = [cs, sn, seqr, valr]

    def backward_a(sums, dz, r):
        outs = [S((th, d), F32), S((th, d), BF16), S((groups, th, 128), BF16), S((groups, th, 128), F32),
                S((groups, 2, th, 128), F32), S((1, d), F32)]
        return call(
            functools.partial(bwd_a_kernel, split, groups), outs,
            [idx, *sums, dz, r[6], *r[1:6], attn_out, g2] + tail, smem=1, flops=4 * 10**9,
            grouped=[n_sums + 3, n_sums + 4, n_sums + 5, n_sums + 6, n_sums + 8], late=[n_sums + 7, n_sums + 10, n_sums + 11],
            first=[n_sums + 7, n_sums + 10, n_sums + 11],
        )

    def backward_b(last, sums, dz, first, ra, rb, xa, xb):
        outs = [S((th, d), BF16), S((groups, th, 320), BF16), S((groups, th, 320), BF16), S((1, d), F32), S((1, d), F32)]
        outs += [S((d, t), BF16)] if last else [S((th, d), F32), S((th, d), F32), piece]
        dha, _, dqxa, dqya, dkva, _ = first
        return call(
            functools.partial(bwd_b_kernel, last, split, groups), outs,
            [idx, *sums, dz, rb[6], *rb[1:6], xa, xb, ra[2], ra[3], dha, dqxa, dqya, dkva, win_t, attn_out, g1, g2] + tail,
            [pltpu.VMEM((th, d), F32)] * 3 + [pltpu.VMEM((2, t, 128), F32), pltpu.VMEM((t, 128), BF16),
             pltpu.VMEM((t, 128), BF16), pltpu.VMEM((th, 128), F32)],
            smem=1, flops=6 * 10**9,
            grouped=[n_sums + k for k in (3, 4, 5, 6, 10, 11, 13, 14, 15, 16, 17)],
            late=[n_sums + k for k in (7, 20, 21, 8, 9, 12)], first=[n_sums + 7, n_sums + 20, n_sums + 21],
        )

    acc = call(own_grads_kernel, grad_outs, [after(a2[7], r2b, sum2a), b2[7], duh2a, duh2b, a2[8], b2[8], cotangent],
               flops=2 * 10**9)
    first2 = backward_a(after(sum2a, acc), cotangent[:th], a2)
    first2, y2b = tie(first2, y2b)
    sum2b = links.sum_chips(r2b, y2b)
    da2b, dp2a, dp2b, dg1b, dg2b1, dz1a, dz1b, dfs = backward_b(
        False, sum2b, cotangent[th:], first2, a2, b2, x1a, x1b)
    dfs, dz1a, dz1b, n2b_x = tie(dfs, dz1a, dz1b, n2b_x)
    df_x = links.x(dfs)
    n2b_p = links.both_cores(n2b_x)
    da2a, dg2b0 = first2[1], first2[5]
    res = call(
        functools.partial(ffn_back_kernel, split), [S((th, f), BF16)] * 2 + [S((th, d), BF16)] * 2 + sums * 2,
        [idx, dz1a, dz1b, a1[7], b1[7]] + ffn_w, [pltpu.VMEM((th, d), F32)], smem=1, flops=2 * 10**9,
        late=[1, 3, 5, 6, 7, 2, 4],
    )
    duh1, df1, s3 = res[:2], res[2:4], res[4:]
    r3a, r3b = links.sum_cores(s3[:n_sums]), links.sum_cores(s3[n_sums:])
    y3a, y3b = links.y_start(r3a), links.y_start(r3b)
    acc = call(
        functools.partial(both_grads_kernel, len(n2b_p)), grad_outs,
        [idx, *n2b_p, *cot_p, *ffn_w, after(a1[7], r3a, r3b), b1[7], *duh1, a1[8], b1[8], *df1, *acc], gscratch,
        flops=6 * 10**9, smem=1,
        late=[12 + 2 * len(n2b_p), 13 + 2 * len(n2b_p), *range(1, 2 * len(n2b_p) + 4)],
    )
    acc, df_x = tie(acc, df_x)
    df_p = links.both_cores(df_x)
    count = len(df_p)
    chunks = call(
        functools.partial(last_grads_kernel, count, len(CHUNKS)), [S((n, f), F32) for n in CHUNKS],
        [idx, *n2a_p, *df_p, *ffn_w, *acc], gscratch + [pltpu.VMEM((d, f), F32), pltpu.VMEM((d, 384), F32)],
        flops=4 * 10**9, smem=1, late=[2 * count + 4, 2 * count + 5],
    )
    quarter = 512 // links.narrow
    group_owner = after(group_owner, acc)
    order = jnp.arange(groups, dtype=jnp.int32)
    sharing = (group_owner[:, None] == group_owner[None, :]) & (order[None, :] < order[:, None])
    rank = jnp.sum(sharing.astype(jnp.int32), axis=1)
    first = jnp.sum(jnp.where((group_owner == member) & (rank == 0), order, 0))
    extra = jnp.sum(jnp.where(rank == 1, order, 0))
    extra_owner = jnp.sum(jnp.where(rank == 1, group_owner, 0))
    idx = jnp.stack([xi, core, first, extra, member, (extra_owner == member).astype(jnp.int32)]).astype(jnp.int32)
    chunks, y3a = tie(chunks, y3a)
    sum3a = links.sum_chips(r3a, y3a)
    lead = quarter // 2 + 8
    made = {}

    def job_a(dep):
        made["a"] = backward_a(after(sum3a, dep), dz1a, a1)
        return made["a"]

    def job_b(dep):
        first, got = tie(made["a"], y3b)
        sums = links.sum_chips(r3b, got)
        made["b"] = backward_b(True, after(sums, dep), dz1b, first, a1, b1, tok_a, tok_b)
        return made["b"]

    def job_grads(dep):
        first, (da1b, dp1a, dp1b, dg1a, dg2a1, _) = made["a"], made["b"]
        gains = jnp.concatenate([dg1a + dg1b, first[5] + dg2a1 + dg2b0 + dg2b1], axis=0)
        return call(
            attn_grad_kernel, [S((n, wd), F32) for n in (lead, B_ROWS, 256 - B_ROWS, lead + 256)],
            [idx, after(a1[0], dep), b1[0], a2[0], b2[0], dp1a, dp1b, dp2a, dp2b, a1[4], b1[4], a2[4], b2[4], first[1],
             da1b, da2a, da2b, gains],
            [pltpu.VMEM((512, d), F32), pltpu.VMEM((quarter + 16, d), F32)], smem=1, flops=2 * 10**9,
            picked=range(5, 13), late=range(13, 17),
        )

    def finish_out(pieces):
        return call(out_kernel, [S((d, t), BF16)], [idx, h2a, h2b, *pieces], [pltpu.VMEM((th, d), F32)], smem=1)

    nc = len(CHUNKS)
    ng = next(k for k in range(1, nc) if sum(CHUNKS[:k]) == d)

    def unpack(vals, theirs):
        return call(functools.partial(unpack_kernel, ng, False), [S((d, f), F32)] * 2,
                    [idx, *vals[:ng], *theirs[:ng]], smem=1,
                    late=[k for c in range(ng) for k in (1 + c, 1 + ng + c)])

    def unpack_down(vals, theirs):
        return call(functools.partial(unpack_kernel, nc - ng, True), [S((d, f), F32)],
                    [idx, *vals[ng:nc], *theirs[ng:nc]], smem=1,
                    late=[k for c in range(nc - ng) for k in (1 + c, 1 + nc - ng + c)])

    def collect(vals, theirs):
        r, o = vals[nc], theirs[nc]
        second = jnp.where(xi == 0, jnp.concatenate([r, o], 0), jnp.concatenate([o, r], 0))
        return second, links.gather_narrow(second[:quarter])

    done, theirs, results = links.sum_lines(
        chunks, [job_a, job_b, job_grads], out2, finish_out, {ng - 1: unpack, nc - 1: unpack_down, nc: collect})
    layer_out = results[None][0].T
    dx = made["b"][5].T
    ggate, gup = results[ng - 1]
    gdown, = results[nc - 1]
    second, slot1 = results[nc]
    small = second[quarter : quarter + 2, :d]
    gin, gout = call(
        functools.partial(attn_finish_kernel, links.narrow), [S((SLOTS, 320, d), F32), S((SLOTS, 192, d), F32)],
        [idx, *done[nc + 1 :], *theirs[nc + 1 :], *slot1], smem=1, late=[*range(5, 5 + len(slot1)), 1, 2, 3, 4],
    )
    gin = jnp.swapaxes(gin, 1, 2)
    return layer_out, dx, gin, gout, ggate, gup, gdown.T, small[0], small[1]


def _pad(outs, split):
    return list(outs) if split else list(outs) + [None]


def solution(mesh):
    in_specs = (P("wide", None), P(), P(), P(None, "narrow"), P(None, "narrow"), P("narrow", None), P(), P(),
                P("wide", None), P("wide"), P("wide"), P("wide"), P())
    out_specs = (P("wide", None), P("wide", None), P("narrow", None, None), P("narrow", None, None),
                 P(None, "narrow"), P(None, "narrow"), P("narrow", None), P(), P())
    return jax.shard_map(functools.partial(per_device, Links(mesh)), mesh=mesh, in_specs=in_specs,
                         out_specs=out_specs, check_vma=False)
```
